32 devices in a mesh: batch: 8 (over y, x, core), head: 4 (over z).
Axes of the slice: x: 2, y: 2, z: 4, core: 2. Of those that a mesh axis runs over, the one named last changes fastest.
Arguments:
- hidden_in: bfloat16 [16384, 2048], P(('batch', 'head')), may hold values from -6 to 6
- out_grad: bfloat16 [16384, 2048], P(('batch', 'head')), may hold values from -6 to 6
- norm_gain: float32 [2048], replicated, may hold values from 0.1 to 1.9
- w_z: bfloat16 [2048, 4096], P(None, 'head'), may hold values from -0.125 to 0.125
- w_x: bfloat16 [2048, 4096], P(None, 'head'), may hold values from -0.125 to 0.125
- w_dt: bfloat16 [2048, 64], P(None, 'head'), may hold values from -0.125 to 0.125
- w_bc: bfloat16 [2048, 256], replicated, may hold values from -0.046875 to 0.046875
- conv_x: float32 [4, 4096], P(None, 'head'), may hold values from -3 to 3
- conv_x_bias: float32 [4096], P('head'), may hold values from -3 to 3
- conv_bc: float32 [4, 256], replicated, may hold values from -3 to 3
- conv_bc_bias: float32 [256], replicated, may hold values from -0.6 to 0.6
- dt_bias: float32 [64], P('head'), may hold values from -4 to -1
- a_log: float32 [64], P('head'), may hold values from -6.2 to -1.2
- d_skip: float32 [64], P('head'), may hold values from 0.5 to 1.5
- gate_gain: float32 [4096], P('head'), may hold values from 0.1 to 1.9
- w_out: bfloat16 [4096, 2048], P('head'), may hold values from -0.1875 to 0.1875
- doc_lengths: int32 [16, 4], P('batch'), may hold values from 1 to 512, 1024 in all within a row
- widths: int32 [16], P('batch'), may hold values from 8 to 64, as said below
Outputs:
- mixed: bfloat16 [16384, 2048], P(('batch', 'head'))
- in_grad: bfloat16 [16384, 2048], P(('batch', 'head'))
- g_norm_gain: float32 [2048], replicated
- g_w_z: float32 [2048, 4096], P(None, 'head')
- g_w_x: float32 [2048, 4096], P(None, 'head')
- g_w_dt: float32 [2048, 64], P(None, 'head')
- g_w_bc: float32 [2048, 256], replicated
- g_conv_x: float32 [4, 4096], P(None, 'head')
- g_conv_x_bias: float32 [4096], P('head')
- g_conv_bc: float32 [4, 256], replicated
- g_conv_bc_bias: float32 [256], replicated
- g_dt_bias: float32 [64], P('head')
- g_a_log: float32 [64], P('head')
- g_d_skip: float32 [64], P('head')
- g_gate_gain: float32 [4096], P('head')
- g_w_out: float32 [4096, 2048], P('head')
The draws below stay inside these ranges and needn't reach their ends.
Inputs may be any that keep to these rules, and one draw needn't show every extreme that they name: `doc_lengths`: each row sums to 1024. `widths`: each entry is 64, 32, 16 or 8; every draw has a sequence of 64 and one of 8.
All inputs are finite; a program needn't handle non-finite values.
Results may differ from the reference program's by a relative error of at most 0.018.
Values may be sent and summed in bfloat16 or wider, within the bound.
No kernel may reach another device: no remote copies, remote signals or barrier semaphores. Data moves between devices by JAX's collectives and lax.ppermute only.
A program may use at most 256 MiB of HBM per device.

```python
import math
import jax
import jax.numpy as jnp
import numpy as np
from jax import lax

D = 2048
HEADS = 64
HEAD_DIM = 64
STATE = 128
CONV = 4
SPAN = 256
SEQ_LEN = 1024
DOCS = 4
INNER = 4096
HLOC = 16
SEQS = 16
TOKENS = 16384


def draw_widths(key, part):
    key = jax.random.fold_in(key, 11)
    first_key, second_key = jax.random.split(key)
    levels = jax.random.randint(first_key, (SEQS,), 0, 4)
    ranking = jax.random.permutation(second_key, SEQS)
    levels = jnp.where(ranking == 0, 0, jnp.where(ranking == 1, 3, levels))
    return jnp.right_shift(jnp.full((SEQS,), HEADS, jnp.int32), levels.astype(jnp.int32)).astype(jnp.int32)


def block_levels(key, extent, pieces, smallest, top_value):
    level, own = 1.0, jax.random.fold_in(key, 6)
    for axis_at, shards_of in pieces:
        heights = jnp.exp(jax.random.uniform(jax.random.fold_in(own, axis_at), (shards_of,), jnp.float32, smallest / len(pieces), top_value / len(pieces)))
        level = level * jnp.repeat(heights, extent[axis_at] // shards_of).reshape([-1 if axis == axis_at else 1 for axis in range(len(extent))])
    return level


def profile(count, total, limit, slope):
    portions = [(1 << 20) // math.isqrt(standing ** slope) + 1 for standing in range(2, count + 1)]
    rest, counts = total - limit - (count - 1), [1] * (count - 1)
    while rest > 0:
        free = [i for i in range(count - 1) if counts[i] < limit]
        pool, budget = sum([portions[i] for i in free]), rest
        for i in free:
            addition = min(limit - counts[i], max(1, budget * portions[i] // pool), rest)
            counts[i] = counts[i] + addition
            rest = rest - addition
    return np.array([limit] + counts)


def ragged(stream_key, amount, total, reach, skew):
    if amount == 2:
        one = jax.random.randint(stream_key, (), max(1, total - reach), min(reach, total - 1) + 1)
        return jnp.stack([one, total - one])
    sizes = jnp.asarray(profile(amount, total, reach, skew), jnp.int32)
    pairs = (amount - 1) // 2
    giver, receiver = sizes[1:1 + 2 * pairs:2], sizes[2:2 + 2 * pairs:2]
    slack = jnp.minimum(giver - 1, reach - receiver)
    passed = jax.random.randint(jax.random.fold_in(stream_key, 1), (pairs,), 0, 1 << 20) % (slack + 1)
    sizes = sizes.at[1:1 + 2 * pairs:2].set(giver - passed).at[2:2 + 2 * pairs:2].set(receiver + passed)
    return sizes[jax.random.permutation(jax.random.fold_in(stream_key, 2), amount)]


def scatter_about(stream_key, shape, spread, reach, cuts=(), kind=jnp.bfloat16):
    level = block_levels(stream_key, shape, cuts, -0.22, 0.18) if cuts else 1.0
    drawn = jax.random.normal(stream_key, shape, jnp.float32) * spread * level
    return jnp.minimum(jnp.maximum(drawn, -reach), reach).astype(kind)


def setup_inputs(seed: int = 0) -> dict:
    arg_keys = jax.random.split(jax.random.key(seed), 19)
    hidden_in = scatter_about(arg_keys[0], (TOKENS, D), 1.0, 6.0, ((0, 32),))
    out_grad = scatter_about(arg_keys[1], (TOKENS, D), 1.0, 6.0, ((0, 32),))
    norm_gain = jnp.clip(1.0 + 0.18 * jax.random.normal(arg_keys[2], (D,), jnp.float32), 0.1, 1.9)
    w_z = scatter_about(arg_keys[3], (D, INNER), D ** -0.5, 0.125, ((1, 4),))
    w_x = scatter_about(arg_keys[4], (D, INNER), D ** -0.5, 0.125, ((1, 4),))
    w_dt = scatter_about(arg_keys[5], (D, HEADS), D ** -0.5, 0.125, ((1, 4),))
    w_bc = scatter_about(arg_keys[6], (D, 2 * STATE), (8 * D) ** -0.5, 0.046875)
    conv_x = scatter_about(arg_keys[7], (CONV, INNER), CONV ** -0.5, 3.0, ((1, 4),), jnp.float32)
    conv_x_bias = scatter_about(arg_keys[8], (INNER,), 0.5, 3.0, ((0, 4),), jnp.float32)
    conv_bc = scatter_about(arg_keys[9], (CONV, 2 * STATE), CONV ** -0.5, 3.0, (), jnp.float32)
    conv_bc_bias = scatter_about(arg_keys[10], (2 * STATE,), 0.1, 0.6, (), jnp.float32)
    dt_bias = jnp.clip(-4.0 + 3.0 * jax.random.uniform(arg_keys[11], (HEADS,), jnp.float32) ** block_levels(arg_keys[11], (HEADS,), ((0, 4),), -0.2, 0.2), -4.0, -1.0)
    a_log = jnp.clip(-6.2 + 5 * jax.random.uniform(arg_keys[12], (HEADS,), jnp.float32) ** block_levels(arg_keys[12], (HEADS,), ((0, 4),), -0.2, 0.2), -6.2, -1.2)
    d_skip = jnp.clip(0.5 + 1.0 * jax.random.uniform(arg_keys[13], (HEADS,), jnp.float32) ** block_levels(arg_keys[13], (HEADS,), ((0, 4),), -0.2, 0.2), 0.5, 1.5)
    gate_gain = jnp.clip(1.0 + 0.18 * jax.random.normal(arg_keys[14], (INNER,), jnp.float32), 0.1, 1.9)
    w_out = scatter_about(arg_keys[15], (INNER, D), (INNER // 4) ** -0.5, 0.1875, ((0, 4),))
    doc_lengths = jax.vmap(lambda own: ragged(own, DOCS, SEQ_LEN, SEQ_LEN // 2, 1))(jax.random.split(arg_keys[16], SEQS)).reshape((SEQS, DOCS)).astype(jnp.int32)
    widths = draw_widths(jax.random.fold_in(arg_keys[18], 71), 0)
    return dict(hidden_in=hidden_in, out_grad=out_grad, norm_gain=norm_gain, w_z=w_z, w_x=w_x, w_dt=w_dt, w_bc=w_bc, conv_x=conv_x, conv_x_bias=conv_x_bias, conv_bc=conv_bc, conv_bc_bias=conv_bc_bias, dt_bias=dt_bias, a_log=a_log, d_skip=d_skip, gate_gain=gate_gain, w_out=w_out, doc_lengths=doc_lengths, widths=widths)


EPSILON = 1e-05
HIGHEST = lax.Precision.HIGHEST

@jax.custom_vjp
def low(v):
    return lax.optimization_barrier(v.astype(jnp.bfloat16)).astype(jnp.float32)

@jax.custom_vjp
def low_back(v):
    return v

def low_keep(v):
    return (low(v), None)

def low_pass(kept, grad):
    return (grad,)

def back_keep(v):
    return (v, None)

def back_low(kept, grad):
    return (low(grad),)
low.defvjp(low_keep, low_pass)
low_back.defvjp(back_keep, back_low)

def shifted(values, lag_rows, fill):
    padding = jnp.full((lag_rows,) + values.shape[1:], fill, values.dtype)
    return jnp.concatenate([padding, values[:values.shape[0] - lag_rows]], axis=0)

def convolve(values, taps, offset_bias, doc_ids):
    result = offset_bias + taps[0] * values
    for lag_rows in range(1, CONV):
        same = (shifted(doc_ids, lag_rows, -1) == doc_ids).astype(jnp.float32)[:, None]
        result = result + taps[lag_rows] * shifted(values, lag_rows, 0.0) * same
    return result

def block_step(carry_pair, inputs):
    state_now, last_doc = carry_pair
    x_block, b_block, c_block, d_block, s_block, doc_block = inputs
    cum_decay = jnp.cumsum(d_block, axis=0)
    offsets = jnp.arange(SPAN)
    inside = (doc_block[:, None] == doc_block[None, :]) & (offsets[:, None] >= offsets[None, :])
    gap_decay = cum_decay[:, None, :] - cum_decay[None, :, :]
    decays = jnp.exp(jnp.where(inside[:, :, None], gap_decay, -1e+30))
    scores = jnp.dot(c_block, b_block.T, precision=HIGHEST)
    mixing = decays * scores[:, :, None] * s_block[None, :, :]
    local_out = jnp.einsum('ijh,jhp->ihp', mixing, x_block, precision=HIGHEST)
    entry_decay = jnp.exp(cum_decay) * (doc_block == last_doc).astype(jnp.float32)[:, None]
    carried = jnp.einsum('in,hpn->ihp', c_block, state_now, precision=HIGHEST) * entry_decay[:, :, None]
    tail_weight = jnp.exp(cum_decay[-1][None, :] - cum_decay) * (doc_block == doc_block[-1]).astype(jnp.float32)[:, None] * s_block
    weighted = x_block * tail_weight[:, :, None]
    fresh_state = jnp.einsum('jhp,jn->hpn', weighted, b_block, precision=HIGHEST)
    keep_decay = jnp.exp(cum_decay[-1]) * (doc_block[-1] == last_doc).astype(jnp.float32)
    state_now = state_now * keep_decay[:, None, None] + fresh_state
    return ((state_now, doc_block[-1]), local_out + carried)

def ssd_scan(values, b_rows, c_rows, decay, step_sizes, doc_ids):
    row_total, head_count, channels = values.shape
    blocks = row_total // SPAN
    inputs = (values.reshape(blocks, SPAN, head_count, channels), b_rows.reshape(blocks, SPAN, STATE), c_rows.reshape(blocks, SPAN, STATE), decay.reshape(blocks, SPAN, head_count), step_sizes.reshape(blocks, SPAN, head_count), doc_ids.reshape(blocks, SPAN))
    start = (jnp.zeros((head_count, channels, STATE), jnp.float32), jnp.int32(-1))
    ending, outputs = lax.scan(jax.checkpoint(block_step), start, inputs)
    return outputs.reshape(row_total, head_count, channels)

def layer_forward(hidden, norm_gain, w_z, w_x, w_dt, w_bc, conv_x, conv_x_bias, conv_bc, conv_bc_bias, dt_bias, a_log, d_skip, gate_gain, w_out, doc_ids, seq_width):
    inverse = lax.rsqrt(lax.optimization_barrier(jnp.mean(hidden * hidden, axis=-1, keepdims=True)) + EPSILON)
    normed = low(hidden * inverse * norm_gain)
    gate_cols = low_back(jnp.dot(normed, w_z, precision=HIGHEST))
    inner_cols = low_back(jnp.dot(normed, w_x, precision=HIGHEST))
    pair_cols = low_back(jnp.dot(normed, w_bc, precision=HIGHEST))
    rate_cols = low_back(jnp.dot(normed, w_dt, precision=HIGHEST))
    mixed_x = low(jax.nn.silu(convolve(inner_cols, conv_x, conv_x_bias, doc_ids)))
    mixed_bc = low(jax.nn.silu(convolve(pair_cols, conv_bc, conv_bc_bias, doc_ids)))
    step_sizes = jax.nn.softplus(rate_cols + dt_bias)
    decay = -step_sizes * jnp.exp(a_log)
    values = mixed_x.reshape(SEQ_LEN, HEADS, HEAD_DIM)
    scanned = ssd_scan(values, mixed_bc[:, :STATE], mixed_bc[:, STATE:], decay, step_sizes, doc_ids)
    scanned = scanned + d_skip[None, :, None] * values
    active = (jnp.arange(HEADS) % HLOC < seq_width * HLOC // HEADS).astype(jnp.float32)
    masked = (scanned * active[None, :, None]).reshape(SEQ_LEN, INNER)
    gated = masked * jax.nn.silu(gate_cols)
    channel_count = (seq_width * HEAD_DIM).astype(jnp.float32)
    scale_rows = lax.rsqrt(lax.optimization_barrier(jnp.sum(gated * gated, axis=-1, keepdims=True)) / channel_count + EPSILON)
    normed_y = low(gated * scale_rows * gate_gain)
    return hidden + jnp.dot(normed_y, w_out, precision=HIGHEST)

def reference(hidden_in, out_grad, norm_gain, w_z, w_x, w_dt, w_bc, conv_x, conv_x_bias, conv_bc, conv_bc_bias, dt_bias, a_log, d_skip, gate_gain, w_out, doc_lengths, widths):
    weights_f32 = tuple((item.astype(jnp.float32) for item in (norm_gain, w_z, w_x, w_dt, w_bc, conv_x, conv_x_bias, conv_bc, conv_bc_bias, dt_bias, a_log, d_skip, gate_gain, w_out)))
    positions = jnp.arange(SEQ_LEN)

    def one_sequence(totals, inputs):
        seq_rows, seq_cot, lengths, seq_width = inputs
        doc_ends = jnp.cumsum(lengths)
        doc_ids = lax.optimization_barrier(jnp.sum((positions[:, None] >= doc_ends[None, :]).astype(jnp.int32), axis=1)).astype(jnp.int32)

        def bound_layer(hidden, *weights):
            return layer_forward(hidden, *weights, doc_ids, seq_width)
        seq_out, pull_back = jax.vjp(bound_layer, seq_rows.astype(jnp.float32), *weights_f32)
        gradients = pull_back(seq_cot.astype(jnp.float32))
        totals = tuple((a + b for a, b in zip(totals, gradients[1:])))
        return (totals, (seq_out.astype(jnp.bfloat16), gradients[0].astype(jnp.bfloat16)))
    zero_grads = tuple((jnp.zeros_like(item) for item in weights_f32))
    totals, outputs = lax.scan(one_sequence, zero_grads, (hidden_in.reshape(SEQS, SEQ_LEN, D), out_grad.reshape(SEQS, SEQ_LEN, D), doc_lengths, widths))
    mixed = outputs[0].reshape(TOKENS, D)
    in_grad = outputs[1].reshape(TOKENS, D)
    return (mixed, in_grad, totals[0], totals[1], totals[2], totals[3], totals[4], totals[5], totals[6], totals[7], totals[8], totals[9], totals[10], totals[11], totals[12], totals[13])
```

```python
import functools

import jax
import jax.numpy as jnp
from jax import lax
from jax.experimental import pallas as pl
from jax.experimental.pallas import tpu as pltpu
from jax.sharding import PartitionSpec as P

HEAD_DIM = 64
STATE = 128
CONV = 4
SPAN = 256
SEQ_LEN = 1024
DOCS = 4
CHUNKS = SEQ_LEN // SPAN
WIDE = 256
GROUP = WIDE // HEAD_DIM
EPSILON = 1e-05
F32 = jnp.float32
BF16 = jnp.bfloat16
VMEM_LIMIT = 48 * 1024 * 1024


def dot_nn(a, b):
    return lax.dot_general(a, b, (((1,), (0,)), ((), ())), preferred_element_type=F32)


def dot_nt(a, b):
    return lax.dot_general(a, b, (((1,), (1,)), ((), ())), preferred_element_type=F32)


def dot_tn(a, b):
    return lax.dot_general(a, b, (((0,), (0,)), ((), ())), preferred_element_type=F32)


def sigmoid(v):
    return 0.5 * (1.0 + jnp.tanh(0.5 * v))


def chunk_start(info, c, per_block):
    block = (c // per_block) ^ info[DOCS]
    return pl.multiple_of((block * per_block + c % per_block) * SPAN, SPAN)


def doc_place(info, pos):
    first = jnp.zeros_like(pos)
    last = jnp.full_like(pos, SEQ_LEN)
    for k in range(DOCS):
        first = jnp.where(pos >= info[k], info[k], first)
    for k in reversed(range(DOCS)):
        last = jnp.where(pos < info[k], info[k], last)
    return pos - first, last - 1 - pos


def chunk_masks(info, c):
    local = lax.broadcasted_iota(jnp.int32, (SPAN, 128), 0)
    since, until = doc_place(info, local + c * SPAN)
    return local, since, until


def wide2(v):
    return jnp.concatenate([v, v], axis=1)


def expand(cols):
    rows = cols.shape[0]
    low = lax.broadcasted_iota(jnp.int32, (rows, 128), 1) < HEAD_DIM
    tiles = [
        jnp.where(low, cols[:, 2 * p : 2 * p + 1], cols[:, 2 * p + 1 : 2 * p + 2]) for p in range(WIDE // 128)
    ]
    return jnp.concatenate(tiles, axis=1)


def conv_inputs(src, info, c, per_block, r0):
    now = src[pl.ds(r0, SPAN), :].astype(F32)
    if c == 0:
        before = jnp.zeros((8, now.shape[1]), F32)
    else:
        p0 = chunk_start(info, c - 1, per_block)
        before = src[pl.ds(pl.multiple_of(p0 + SPAN - 16, 16), 16), :].astype(F32)[8:]
    ext = jnp.concatenate([before, now], axis=0)
    return now, [now] + [pltpu.roll(ext, k, 0)[8:] for k in range(1, CONV)]


def conv_apply(lags, taps, bias, masks):
    u = bias + taps[0] * lags[0]
    for k in range(1, CONV):
        u = u + taps[k] * (lags[k] * masks[k])
    return u


def conv_back(du, after, taps, masks_after):
    ext = jnp.concatenate([du, after], axis=0)
    total = taps[0] * du
    for k in range(1, CONV):
        total = total + taps[k] * (pltpu.roll(ext, SPAN + 8 - k, 0)[:SPAN] * masks_after[k])
    return total


def prep_kernel(per_block, info, pairs, par, bc_out, bct_out):
    taps = [par[k : k + 1, :] for k in range(CONV)]
    for c in range(CHUNKS):
        r0 = chunk_start(info, c, per_block)
        _, since, _ = chunk_masks(info, c)
        masks = [wide2((since >= k).astype(F32)) for k in range(CONV)]
        _, lags = conv_inputs(pairs, info, c, per_block, r0)
        u = conv_apply(lags, taps, par[4:5, :], masks)
        low = (u * sigmoid(u)).astype(BF16)
        bc_out[pl.ds(r0, SPAN), :] = low
        bct_out[:, pl.ds(r0, SPAN)] = low.T


def fwd_kernel(
    per_block, info, inner, gate, bc, bct, hs, par, y_out, yg_out, st_out, ss_out, score_scr, state_scr
):
    taps = [par[k : k + 1, :] for k in range(CONV)]
    bias, skip, gain, act = par[4:5, :], par[5:6, :], par[6:7, :], par[7:8, :]
    lane = lax.broadcasted_iota(jnp.int32, (1, 128), 1)
    sides = [(lane < HEAD_DIM).astype(BF16), (lane >= HEAD_DIM).astype(BF16)]

    @pl.when(pl.program_id(0) == 0)
    def _():
        ss_out[...] = jnp.zeros_like(ss_out)
        for c in range(CHUNKS):
            r0 = chunk_start(info, c, per_block)
            _, since, _ = chunk_masks(info, c)
            bcv = bc[pl.ds(r0, SPAN), :]
            score = dot_nt(bcv[:, STATE:], bcv[:, :STATE])
            gap = lax.broadcasted_iota(jnp.int32, (SPAN, SPAN), 0) - lax.broadcasted_iota(
                jnp.int32, (SPAN, SPAN), 1
            )
            score_scr[c] = jnp.where((gap >= 0) & (gap <= wide2(since)), score, 0.0)

    state_scr[...] = jnp.zeros_like(state_scr)
    for c in range(CHUNKS):
        r0 = chunk_start(info, c, per_block)
        local, since, until = chunk_masks(info, c)
        masks = [wide2((since >= k).astype(F32)) for k in range(CONV)]
        _, lags = conv_inputs(inner, info, c, per_block, r0)
        u = conv_apply(lags, taps, bias, masks)
        xf = (u * sigmoid(u)).astype(BF16).astype(F32)
        head_rows = hs[:, pl.ds(r0, SPAN)]
        cum_rows = head_rows[:8]
        cum = cum_rows.T
        step = head_rows[8:].T
        local8, since8, until8 = local[:, :8], since[:, :8], until[:, :8]
        cum_end = cum[SPAN - 1 : SPAN, :]
        entry = jnp.where(since8 > local8, jnp.exp(cum), 0.0)
        tail = jnp.where(until8 >= SPAN - 1 - local8, jnp.exp(cum_end - cum), 0.0)
        keep = entry[SPAN - 1 : SPAN, :]
        xs = (xf * expand(step)).astype(BF16)
        xw = (xf * expand(tail * step)).astype(BF16)
        state = state_scr[...]
        state_low = state.astype(BF16)
        st_out[pl.ds(c * STATE, STATE), :] = state_low
        carried = dot_nn(bc[pl.ds(r0, SPAN), STATE:], state_low) * expand(entry)
        state_scr[...] = state * expand(keep) + dot_nn(bct[:STATE, pl.ds(r0, SPAN)], xw)
        tiles = []
        for p in range(WIDE // 128):
            tile = carried[:, p * 128 : (p + 1) * 128]
            for s in range(2):
                h = 2 * p + s
                decays = jnp.exp(jnp.minimum(cum[:, h : h + 1] - cum_rows[h : h + 1, :], 0.0))
                mixing = (decays * score_scr[c]).astype(BF16)
                tile = tile + dot_nn(mixing, xs[:, p * 128 : (p + 1) * 128] * sides[s])
            tiles.append(tile)
        y = jnp.concatenate(tiles, axis=1)
        y_out[pl.ds(r0, SPAN), :] = y.astype(BF16)
        g = gate[pl.ds(r0, SPAN), :].astype(F32)
        gated = (y + skip * xf) * act * (g * sigmoid(g))
        yg_out[pl.ds(r0, SPAN), :] = (gated * gain).astype(BF16)
        square = gated * gated
        ss_out[pl.ds(r0, SPAN), :] += square[:, :128] + square[:, 128:]


def split_low(v):
    high = v.astype(BF16)
    return high, (v - high.astype(F32)).astype(BF16)


def bwd_kernel(
    per_block,
    blocks,
    info,
    inner,
    gate,
    y_in,
    dn_in,
    bc,
    bct,
    hs,
    sk,
    st,
    par,
    dgate_out,
    dinner_out,
    dbc_out,
    gp_out,
    hr_out,
    score_scr,
    pair_scr,
    mask_scr,
    adj_scr,
):
    taps = [par[k : k + 1, :] for k in range(CONV)]
    bias, skip, gain, act = par[4:5, :], par[5:6, :], par[6:7, :], par[7:8, :]
    lane = lax.broadcasted_iota(jnp.int32, (1, 128), 1)
    sides = [(lane < HEAD_DIM).astype(BF16), (lane >= HEAD_DIM).astype(BF16)]
    head_of = lax.broadcasted_iota(jnp.int32, (8, WIDE), 1) // HEAD_DIM
    row8 = lax.broadcasted_iota(jnp.int32, (8, WIDE), 0)
    pick = (head_of == row8).astype(BF16)
    pick_up = (head_of + 4 == row8).astype(BF16)

    @pl.when(pl.program_id(0) == 0)
    def _():
        dbc_out[...] = jnp.zeros_like(dbc_out)
        pair_scr[...] = jnp.zeros_like(pair_scr)
        for c in range(CHUNKS):
            r0 = chunk_start(info, c, per_block)
            _, since, until = chunk_masks(info, c)
            bcv = bc[pl.ds(r0, SPAN), :]
            score = dot_nt(bcv[:, :STATE], bcv[:, STATE:])
            gap = lax.broadcasted_iota(jnp.int32, (SPAN, SPAN), 1) - lax.broadcasted_iota(
                jnp.int32, (SPAN, SPAN), 0
            )
            score_scr[c] = jnp.where((gap >= 0) & (gap <= wide2(until)), score, 0.0)
            mask_scr[c] = jnp.where((gap <= 0) & (-gap <= wide2(since)), 1.0, 0.0).astype(BF16)

    adj_scr[...] = jnp.zeros_like(adj_scr)
    after = jnp.zeros((8, WIDE), F32)
    gp = jnp.zeros((8, WIDE), F32)
    for c in reversed(range(CHUNKS)):
        r0 = chunk_start(info, c, per_block)
        local, since, until = chunk_masks(info, c)
        masks = [wide2((since >= k).astype(F32)) for k in range(CONV)]
        masks_after = [wide2((until >= k).astype(F32)) for k in range(CONV)]
        _, lags = conv_inputs(inner, info, c, per_block, r0)
        u = conv_apply(lags, taps, bias, masks)
        su = sigmoid(u)
        xf = (u * su).astype(BF16).astype(F32)
        head_rows = hs[:, pl.ds(r0, SPAN)]
        cum_rows, step_rows = head_rows[:8], head_rows[8:]
        cum = cum_rows.T
        step = step_rows.T
        local8, since8, until8 = local[:, :8], since[:, :8], until[:, :8]
        cum_end = cum[SPAN - 1 : SPAN, :]
        entry = jnp.where(since8 > local8, jnp.exp(cum), 0.0)
        tail = jnp.where(until8 >= SPAN - 1 - local8, jnp.exp(cum_end - cum), 0.0)
        keep = entry[SPAN - 1 : SPAN, :]
        step_wide = expand(step)
        xs = (xf * step_wide).astype(BF16)
        xw = (xf * expand(tail * step)).astype(BF16)
        row_cols = sk[:, pl.ds(r0, SPAN)].T
        scale, fix = row_cols[:, 0:1], row_cols[:, 1:2]

        g = gate[pl.ds(r0, SPAN), :].astype(F32)
        sg = sigmoid(g)
        sw = g * sg
        y = y_in[pl.ds(r0, SPAN), :].astype(F32)
        dn = dn_in[pl.ds(r0, SPAN), :].astype(F32)
        masked = (y + skip * xf) * act
        gated = masked * sw
        d_scale = dn * scale
        d_gated = d_scale * gain - gated * fix
        dgate_out[pl.ds(r0, SPAN), :] = (d_gated * masked * sg * (1.0 + g * (1.0 - sg))).astype(BF16)
        dy_low = (d_gated * sw * act).astype(BF16)
        dy = dy_low.astype(F32)
        dy_entry = (dy * expand(entry)).astype(BF16)
        g_gain = jnp.sum(d_scale * gated, axis=0, keepdims=True)

        adj = adj_scr[...]
        adj_low = adj.astype(BF16)
        bcv = bc[pl.ds(r0, SPAN), :]
        d_c = dot_nt(dy_entry, st[pl.ds(c * STATE, STATE), :])
        d_b = dot_nt(xw, adj_low)
        dbc_out[pl.ds(r0, SPAN), :] += jnp.concatenate([d_b, d_c], axis=1)
        carried = dot_nn(bcv[:, :STATE], adj_low) * expand(tail)
        adj_scr[...] = adj * expand(keep) + dot_nn(bct[STATE:, pl.ds(r0, SPAN)], dy_entry)

        pair_sum = pair_scr[c]
        tiles = []
        for p in range(WIDE // 128):
            tile = carried[:, p * 128 : (p + 1) * 128]
            dy_tile = dy_low[:, p * 128 : (p + 1) * 128]
            xs_tile = xs[:, p * 128 : (p + 1) * 128]
            for s in range(2):
                h = 2 * p + s
                decays = jnp.exp(jnp.minimum(cum_rows[h : h + 1, :] - cum[:, h : h + 1], 0.0))
                mixing = (decays * score_scr[c]).astype(BF16)
                tile = tile + dot_nn(mixing, dy_tile * sides[s])
                pair_sum = pair_sum + decays * dot_nt(xs_tile * sides[s], dy_tile)
            tiles.append(tile)
        pair_scr[c] = pair_sum
        dxu = jnp.concatenate(tiles, axis=1)

        du = (step_wide * dxu + skip * dy) * (su * (1.0 + u * (1.0 - su)))
        dinner_out[pl.ds(r0, SPAN), :] = conv_back(du, after, taps, masks_after).astype(BF16)
        after = du[:8]
        sums = [jnp.sum(du * lags[k] * masks[k], axis=0, keepdims=True) for k in range(CONV)]
        sums += [jnp.sum(du, axis=0, keepdims=True), jnp.zeros((1, WIDE), F32), g_gain, jnp.zeros((1, WIDE), F32)]
        gp = gp + jnp.concatenate(sums, axis=0)

        q1h, q1l = split_low(dy * y)
        q2h, q2l = split_low(xf * dxu)
        q3h, q3l = split_low(xf * dy)
        row_term = dot_nt(pick, q1h) + dot_nt(pick, q1l)
        steps = dot_nt(pick, q2h) + dot_nt(pick, q2l) + dot_nt(pick_up, q3h) + dot_nt(pick_up, q3l)
        vh, vl = split_low(row_term - step_rows * jnp.where(row8 < GROUP, steps, 0.0))
        d_decay = dot_nn(vh, mask_scr[c]) + dot_nn(vl, mask_scr[c])
        row_local = lax.broadcasted_iota(jnp.int32, (8, SPAN), 1)
        row_since, row_until = doc_place(info, row_local + c * SPAN)
        if c < CHUNKS - 1:
            ph, plow = split_low(st[pl.ds((c + 1) * STATE, STATE), :].astype(F32) * adj)
            cross = jnp.sum(dot_nt(pick, ph) + dot_nt(pick, plow), axis=1, keepdims=True)
            d_decay = d_decay + jnp.where(row_until >= SPAN - 1 - row_local, cross, 0.0)
        d_decay = jnp.where(row_since > 0, d_decay, 0.0)
        hr_out[:, pl.ds(r0, SPAN)] = jnp.concatenate([steps, d_decay], axis=0)
    gp_out[...] = gp

    @pl.when(pl.program_id(0) == blocks - 1)
    def _():
        for c in range(CHUNKS):
            r0 = chunk_start(info, c, per_block)
            _, _, until = chunk_masks(info, c)
            gap = lax.broadcasted_iota(jnp.int32, (SPAN, SPAN), 1) - lax.broadcasted_iota(
                jnp.int32, (SPAN, SPAN), 0
            )
            pair_low = jnp.where((gap >= 0) & (gap <= wide2(until)), pair_scr[c], 0.0).astype(BF16)
            bcv = bc[pl.ds(r0, SPAN), :]
            dbc_out[pl.ds(r0, SPAN), :] += jnp.concatenate(
                [dot_nn(pair_low, bcv[:, STATE:]), dot_tn(pair_low, bcv[:, :STATE])], axis=1
            )


def pair_kernel(per_block, info, pairs, dbc_a, dbc_b, par, dp_out, gp_out):
    taps = [par[k : k + 1, :] for k in range(CONV)]
    after = jnp.zeros((8, WIDE), F32)
    gp = jnp.zeros((8, WIDE), F32)
    for c in reversed(range(CHUNKS)):
        r0 = chunk_start(info, c, per_block)
        _, since, until = chunk_masks(info, c)
        masks = [wide2((since >= k).astype(F32)) for k in range(CONV)]
        masks_after = [wide2((until >= k).astype(F32)) for k in range(CONV)]
        _, lags = conv_inputs(pairs, info, c, per_block, r0)
        u = conv_apply(lags, taps, par[4:5, :], masks)
        su = sigmoid(u)
        rows = pl.ds(r0, SPAN)
        du = (dbc_a[rows, :] + dbc_b[rows, :]) * (su * (1.0 + u * (1.0 - su)))
        dp_out[rows, :] = conv_back(du, after, taps, masks_after).astype(BF16)
        after = du[:8]
        sums = [jnp.sum(du * lags[k] * masks[k], axis=0, keepdims=True) for k in range(CONV)]
        sums += [jnp.sum(du, axis=0, keepdims=True), jnp.zeros((3, WIDE), F32)]
        gp = gp + jnp.concatenate(sums, axis=0)
    gp_out[...] = gp


def whole(shape):
    return pl.BlockSpec(shape, lambda i, info: (0,) * len(shape))


def cols(rows):
    return pl.BlockSpec((rows, WIDE), lambda i, info: (0, i))


def call(kernel, grid, in_specs, out_specs, out_shape, scratch, flops, moved, info, *operands):
    return pl.pallas_call(
        kernel,
        grid_spec=pltpu.PrefetchScalarGridSpec(
            num_scalar_prefetch=1,
            grid=(grid,),
            in_specs=in_specs,
            out_specs=out_specs,
            scratch_shapes=scratch,
        ),
        out_shape=out_shape,
        compiler_params=pltpu.CompilerParams(vmem_limit_bytes=VMEM_LIMIT),
        cost_estimate=pl.CostEstimate(flops=flops, bytes_accessed=moved, transcendentals=0),
    )(info, *operands)


def shape(dims, kind):
    return jax.ShapeDtypeStruct(dims, kind)


def prep(per_block, info, pairs, par):
    t = SEQ_LEN
    return call(
        functools.partial(prep_kernel, per_block),
        1,
        [whole((t, WIDE)), whole((8, WIDE))],
        [whole((t, WIDE)), whole((WIDE, t))],
        [shape((t, WIDE), BF16), shape((WIDE, t), BF16)],
        [],
        10**9,
        3 * 10**6,
        info,
        pairs,
        par,
    )


def scan_forward(per_block, info, inner, gate, bc, bct, hs, par):
    t, channels = inner.shape
    blocks = channels // WIDE
    return call(
        functools.partial(fwd_kernel, per_block),
        blocks,
        [
            cols(t),
            cols(t),
            whole((t, WIDE)),
            whole((WIDE, t)),
            pl.BlockSpec((16, t), lambda i, info: (i, 0)),
            cols(8),
        ],
        [cols(t), cols(t), cols(CHUNKS * STATE), whole((t, 128))],
        [
            shape((t, channels), BF16),
            shape((t, channels), BF16),
            shape((CHUNKS * STATE, channels), BF16),
            shape((t, 128), F32),
        ],
        [pltpu.VMEM((CHUNKS, SPAN, SPAN), F32), pltpu.VMEM((STATE, WIDE), F32)],
        blocks * 2 * 10**9,
        10 * t * channels,
        info,
        inner,
        gate,
        bc,
        bct,
        hs,
        par,
    )


def scan_backward(per_block, info, inner, gate, y, dn, bc, bct, hs, sk, st, par):
    t, channels = inner.shape
    blocks = channels // WIDE
    return call(
        functools.partial(bwd_kernel, per_block, blocks),
        blocks,
        [
            cols(t),
            cols(t),
            cols(t),
            cols(t),
            whole((t, WIDE)),
            whole((WIDE, t)),
            pl.BlockSpec((16, t), lambda i, info: (i, 0)),
            whole((8, t)),
            cols(CHUNKS * STATE),
            cols(8),
        ],
        [
            cols(t),
            cols(t),
            whole((t, WIDE)),
            cols(8),
            pl.BlockSpec((16, t), lambda i, info: (i, 0)),
        ],
        [
            shape((t, channels), BF16),
            shape((t, channels), BF16),
            shape((t, WIDE), F32),
            shape((8, channels), F32),
            shape((blocks * 16, t), F32),
        ],
        [
            pltpu.VMEM((CHUNKS, SPAN, SPAN), F32),
            pltpu.VMEM((CHUNKS, SPAN, SPAN), F32),
            pltpu.VMEM((CHUNKS, SPAN, SPAN), BF16),
            pltpu.VMEM((STATE, WIDE), F32),
        ],
        blocks * 5 * 10**9,
        16 * t * channels,
        info,
        inner,
        gate,
        y,
        dn,
        bc,
        bct,
        hs,
        sk,
        st,
        par,
    )


def pair_backward(per_block, info, pairs, dbc_a, dbc_b, par):
    t = SEQ_LEN
    return call(
        functools.partial(pair_kernel, per_block),
        1,
        [whole((t, WIDE)), whole((t, WIDE)), whole((t, WIDE)), whole((8, WIDE))],
        [whole((t, WIDE)), whole((8, WIDE))],
        [shape((t, WIDE), BF16), shape((8, WIDE), F32)],
        [],
        10**9,
        4 * 10**6,
        info,
        pairs,
        dbc_a,
        dbc_b,
        par,
    )


def body(
    axis_sizes,
    hidden_in,
    out_grad,
    norm_gain,
    w_z,
    w_x,
    w_dt,
    w_bc,
    conv_x,
    conv_x_bias,
    conv_bc,
    conv_bc_bias,
    dt_bias,
    a_log,
    d_skip,
    gate_gain,
    w_out,
    doc_lengths,
    widths,
):
    batches, stacks = axis_sizes
    rows, width_in = hidden_in.shape
    heads_here = dt_bias.shape[0]
    channels = w_x.shape[1]
    members = stacks // widths.shape[0]
    far_bit = members
    per_block = rows // SPAN
    place = lax.axis_index("head")
    lot = lax.axis_index("batch")
    own_seq = place // members
    ends = jnp.cumsum(lax.dynamic_index_in_dim(doc_lengths, own_seq, 0, keepdims=False))
    width = lax.dynamic_index_in_dim(widths, own_seq, 0, keepdims=False)
    info = jnp.concatenate([ends.astype(jnp.int32), (place % members).astype(jnp.int32)[None]])

    def across(v, bit):
        return lax.ppermute(v, "head", [(i, i ^ bit) for i in range(stacks)])

    def gather_rows(v):
        bit = 1
        while bit < members:
            v = jnp.concatenate([v, across(v, bit)], axis=0)
            bit *= 2
        return v

    def scatter_rows(v):
        bit = members // 2
        while bit >= 1:
            half = v.shape[0] // 2
            v = v[:half] + across(v[half:], bit)
            bit //= 2
        return v

    def sum_rows(v):
        bit = 1
        while bit < members:
            got = across(v, bit)
            flipped = got.reshape(v.shape[0], -1, 2, bit * rows)[:, :, ::-1, :].reshape(v.shape)
            v = v + flipped
            bit *= 2
        return v

    def fetch_far(w):
        piece = w.shape[0] // batches
        mine = lax.dynamic_slice_in_dim(w, lot * piece, piece, 0)
        return lax.all_gather(across(mine, far_bit), "batch", axis=0, tiled=True)

    hidden_all = gather_rows(hidden_in)
    upstream = gather_rows(out_grad)
    w_x2 = (w_x, fetch_far(w_x))
    w_z2 = (w_z, fetch_far(w_z))
    w_out2 = (w_out, fetch_far(w_out))
    w_dt_own = w_dt.T
    w_dt_far = across(w_dt_own, far_bit)
    head_row = jnp.concatenate([dt_bias, a_log])
    par_own = jnp.concatenate(
        [
            conv_x,
            conv_x_bias[None],
            jnp.repeat(d_skip, HEAD_DIM)[None],
            gate_gain[None],
            jnp.pad(head_row, (0, channels - head_row.shape[0]))[None],
        ],
        axis=0,
    )
    par_far = across(par_own, far_bit)
    active = (jnp.arange(channels) // HEAD_DIM < width * heads_here // (heads_here * stacks)).astype(F32)
    rate_par = [(v[7, :heads_here], v[7, heads_here : 2 * heads_here]) for v in (par_own, par_far)]
    par2 = [jnp.concatenate([v[:7], active[None]], axis=0) for v in (par_own, par_far)]
    step_bias = jnp.concatenate([rate_par[0][0], rate_par[1][0]])[:, None]
    speed = jnp.exp(jnp.concatenate([rate_par[0][1], rate_par[1][1]]))[:, None]
    par_bc = jnp.concatenate([conv_bc, conv_bc_bias[None], jnp.zeros((3, 2 * STATE), F32)], axis=0)

    residual_all = hidden_all.astype(F32)
    inverse_all = lax.rsqrt(jnp.mean(residual_all * residual_all, axis=-1, keepdims=True) + EPSILON)
    normed = (residual_all * inverse_all * norm_gain).astype(BF16)
    w_small = jnp.concatenate([w_bc, w_dt_own.T, w_dt_far.T], axis=1)
    small_cols = dot_nn(normed, w_small)
    pairs = small_cols[:, : 2 * STATE]
    rates = small_cols[:, 2 * STATE :].T
    step = jax.nn.softplus(rates + step_bias)
    decay = -step * speed
    upper = (jnp.arange(SPAN)[:, None] <= jnp.arange(SPAN)[None, :]).astype(F32)
    cum = lax.dot_general(
        decay.reshape(-1, SPAN), upper, (((1,), (0,)), ((), ())), precision=lax.Precision.HIGHEST
    ).reshape(decay.shape)

    def grouped(v):
        v = v.reshape(-1, GROUP, SEQ_LEN)
        return jnp.pad(v, ((0, 0), (0, 8 - GROUP), (0, 0)))

    hs = jnp.concatenate([grouped(cum), grouped(step)], axis=1).reshape(-1, SEQ_LEN)
    half = hs.shape[0] // 2
    hs2 = (hs[:half], hs[half:])
    bc, bct = prep(per_block, info, pairs, par_bc)

    inner2 = [dot_nn(normed, w).astype(BF16) for w in w_x2]
    gate2 = [dot_nn(normed, w).astype(BF16) for w in w_z2]
    forward = [
        scan_forward(per_block, info, inner2[i], gate2[i], bc, bct, hs2[i], par2[i]) for i in range(2)
    ]
    y2 = [f[0] for f in forward]
    yg2 = [f[1] for f in forward]
    branch = scatter_rows((dot_nn(yg2[0], w_out2[0]) + dot_nn(yg2[1], w_out2[1])).astype(BF16))
    dn2, inner_sums = [], []
    for i in range(2):
        dn = dot_nt(upstream, w_out2[i])
        inner_sums.append(jnp.sum(dn * yg2[i].astype(F32), axis=1))
        dn2.append(dn.astype(BF16))
    square = jnp.sum(forward[0][3] + forward[1][3], axis=1)
    sums = sum_rows(jnp.stack([square, inner_sums[0] + inner_sums[1]]))
    count = (width * HEAD_DIM).astype(F32)
    scale = lax.rsqrt(sums[0] / count + EPSILON)
    fix = scale * scale * scale * sums[1] / count
    sk = jnp.concatenate([scale[None], fix[None], jnp.zeros((6, SEQ_LEN), F32)], axis=0)

    scaled_up = (upstream.astype(F32) * scale[:, None]).astype(BF16)
    mixed = (hidden_in.astype(F32) + branch.astype(F32) * scale[:rows, None]).astype(BF16)

    back = [None, None]
    for i in (1, 0):
        back[i] = scan_backward(
            per_block, info, inner2[i], gate2[i], y2[i], dn2[i], bc, bct, hs2[i], sk, forward[i][2], par2[i]
        )
    d_pairs, g_bc = pair_backward(per_block, info, pairs, back[0][2], back[1][2], par_bc)

    heads_out = [b[4].reshape(-1, 16, SEQ_LEN) for b in back]
    d_step = jnp.concatenate([h[:, :GROUP].reshape(-1, SEQ_LEN) for h in heads_out], axis=0)
    skip_rows = jnp.concatenate([h[:, GROUP : 2 * GROUP].reshape(-1, SEQ_LEN) for h in heads_out], axis=0)
    d_decay = jnp.concatenate([h[:, 8 : 8 + GROUP].reshape(-1, SEQ_LEN) for h in heads_out], axis=0)
    d_rates_pre = (d_step - d_decay * speed) * jax.nn.sigmoid(rates + step_bias)
    head_grads = jnp.stack(
        [jnp.sum(d_rates_pre, axis=1), jnp.sum(d_decay * decay, axis=1), jnp.sum(skip_rows, axis=1)]
    )
    d_rates = d_rates_pre.astype(BF16)
    d_small = jnp.concatenate([d_pairs, d_rates.T], axis=1)

    d_normed_part = dot_nt(d_small, w_small)
    for i in range(2):
        d_normed_part = d_normed_part + dot_nt(back[i][0], w_z2[i]) + dot_nt(back[i][1], w_x2[i])
    d_normed_in = scatter_rows(d_normed_part.astype(BF16)).astype(F32)

    def reduce_pair(own, far):
        far_piece = lax.psum_scatter(far, "batch", scatter_dimension=0, tiled=True)
        own_piece = lax.psum_scatter(own, "batch", scatter_dimension=0, tiled=True)
        total = own_piece + across(far_piece, far_bit)
        return lax.all_gather(total, "batch", axis=0, tiled=True).astype(F32)

    g_w_out = reduce_pair(*[dot_tn(yg2[i], scaled_up).astype(BF16) for i in range(2)])
    g_w_z = reduce_pair(*[dot_tn(normed, back[i][0]).astype(BF16) for i in range(2)])
    g_w_x = reduce_pair(*[dot_tn(normed, back[i][1]).astype(BF16) for i in range(2)])
    g_small = dot_tn(d_small, normed)
    g_w_bc = lax.psum(g_small[: 2 * STATE].astype(BF16), ("batch", "head")).astype(F32).T
    g_bc_total = lax.psum(g_bc, ("batch", "head"))

    def pack(i):
        gp = back[i][3]
        heads = head_grads[:, i * heads_here : (i + 1) * heads_here].reshape(-1)
        heads = jnp.pad(heads, (0, channels - heads.shape[0]))[None]
        start = 2 * STATE + i * heads_here
        return jnp.concatenate(
            [gp[:5], heads, gp[6:7], jnp.zeros((1, channels), F32), g_small[start : start + heads_here].reshape(-1, channels)],
            axis=0,
        )

    packed = lax.psum(pack(0) + across(pack(1), far_bit), "batch")
    heads_total = packed[5]
    g_w_dt = packed[8:].reshape(heads_here, width_in).T

    residual = hidden_in.astype(F32)
    inverse = inverse_all[:rows]
    unit_rows = residual * inverse
    g_norm = lax.psum(jnp.sum(d_normed_in * unit_rows, axis=0), ("batch", "head"))
    d_unit = d_normed_in * norm_gain
    d_residual = inverse * (d_unit - unit_rows * jnp.mean(d_unit * unit_rows, axis=-1, keepdims=True))
    in_grad = (out_grad.astype(F32) + d_residual).astype(BF16)
    return (
        mixed,
        in_grad,
        g_norm,
        g_w_z,
        g_w_x,
        g_w_dt,
        g_w_bc,
        packed[:4],
        packed[4],
        g_bc_total[:4],
        g_bc_total[4],
        heads_total[:heads_here],
        heads_total[heads_here : 2 * heads_here],
        heads_total[2 * heads_here : 3 * heads_here],
        packed[6],
        g_w_out,
    )


def solution(mesh):
    split = P(("batch", "head"), None)
    by_col, by_head, by_row = P(None, "head"), P("head"), P("head", None)
    return jax.shard_map(
        functools.partial(body, (mesh.shape["batch"], mesh.shape["head"])),
        mesh=mesh,
        in_specs=(
            split,
            split,
            P(),
            by_col,
            by_col,
            by_col,
            P(),
            by_col,
            by_head,
            P(),
            P(),
            by_head,
            by_head,
            by_head,
            by_head,
            by_row,
            P("batch", None),
            P("batch"),
        ),
        out_specs=(
            split,
            split,
            P(),
            by_col,
            by_col,
            by_col,
            P(),
            by_col,
            by_head,
            P(),
            P(),
            by_head,
            by_head,
            by_head,
            by_head,
            by_row,
        ),
        check_vma=False,
    )
```

```python
import functools

import jax
import jax.numpy as jnp
from jax import lax
from jax.experimental import pallas as pl
from jax.experimental.pallas import tpu as pltpu
from jax.sharding import PartitionSpec as P

HEAD_DIM = 64
STATE = 128
CONV = 4
SPAN = 256
SEQ_LEN = 1024
DOCS = 4
CHUNKS = SEQ_LEN // SPAN
WIDE = 256
GROUP = WIDE // HEAD_DIM
STRIP = 128
BELOW = [(k * STRIP, -(-(k + 1) * STRIP // 128) * 128) for k in range(SPAN // STRIP)]
ABOVE = [(k * STRIP, k * STRIP // 128 * 128) for k in range(SPAN // STRIP)]
EPSILON = 1e-05
F32 = jnp.float32
BF16 = jnp.bfloat16
VMEM_LIMIT = 48 * 1024 * 1024


PACE = 0.01e9


def lasting(us):
    return pl.CostEstimate(flops=int(us * PACE), bytes_accessed=1000, transcendentals=0)


def dot_nn(a, b):
    return lax.dot_general(a, b, (((1,), (0,)), ((), ())), preferred_element_type=F32)


def dot_nt(a, b):
    return lax.dot_general(a, b, (((1,), (1,)), ((), ())), preferred_element_type=F32)


def dot_tn(a, b):
    return lax.dot_general(a, b, (((0,), (0,)), ((), ())), preferred_element_type=F32)


def sigmoid(v):
    return 0.5 * (1.0 + jnp.tanh(0.5 * v))


def chunk_start(info, c, per_block):
    block = (c // per_block) ^ info[DOCS]
    return pl.multiple_of((block * per_block + c % per_block) * SPAN, SPAN)


def doc_place(info, pos):
    first = jnp.zeros_like(pos)
    last = jnp.full_like(pos, SEQ_LEN)
    for k in range(DOCS):
        first = jnp.where(pos >= info[k], info[k], first)
    for k in reversed(range(DOCS)):
        last = jnp.where(pos < info[k], info[k], last)
    return pos - first, last - 1 - pos


def chunk_masks(info, c):
    local = lax.broadcasted_iota(jnp.int32, (SPAN, 128), 0)
    since, until = doc_place(info, local + c * SPAN)
    return local, since, until


def wide2(v):
    return jnp.concatenate([v, v], axis=1)


def expand(cols):
    rows = cols.shape[0]
    low = lax.broadcasted_iota(jnp.int32, (rows, 128), 1) < HEAD_DIM
    tiles = [
        jnp.where(low, cols[:, 2 * p : 2 * p + 1], cols[:, 2 * p + 1 : 2 * p + 2]) for p in range(WIDE // 128)
    ]
    return jnp.concatenate(tiles, axis=1)


def conv_inputs(src, info, c, per_block, r0):
    now = src[pl.ds(r0, SPAN), :].astype(F32)
    if c == 0:
        before = jnp.zeros((8, now.shape[1]), F32)
    else:
        p0 = chunk_start(info, c - 1, per_block)
        before = src[pl.ds(pl.multiple_of(p0 + SPAN - 16, 16), 16), :].astype(F32)[8:]
    ext = jnp.concatenate([before, now], axis=0)
    return now, [now] + [pltpu.roll(ext, k, 0)[8:] for k in range(1, CONV)]


def conv_apply(lags, taps, bias, masks):
    u = bias + taps[0] * lags[0]
    for k in range(1, CONV):
        u = u + taps[k] * (lags[k] * masks[k])
    return u


def conv_back(du, after, taps, masks_after):
    ext = jnp.concatenate([du, after], axis=0)
    total = taps[0] * du
    for k in range(1, CONV):
        total = total + taps[k] * (pltpu.roll(ext, SPAN + 8 - k, 0)[:SPAN] * masks_after[k])
    return total


def prep_kernel(per_block, info, pairs, par, bc_out, bct_out):
    taps = [par[k : k + 1, :] for k in range(CONV)]
    for c in range(CHUNKS):
        r0 = chunk_start(info, c, per_block)
        _, since, _ = chunk_masks(info, c)
        masks = [wide2((since >= k).astype(F32)) for k in range(CONV)]
        _, lags = conv_inputs(pairs, info, c, per_block, r0)
        u = conv_apply(lags, taps, par[4:5, :], masks)
        low = (u * sigmoid(u)).astype(BF16)
        bc_out[pl.ds(r0, SPAN), :] = low
        bct_out[:, pl.ds(r0, SPAN)] = low.T


def fwd_kernel(
    per_block, info, inner, gate, bc, bct, hs, par, y_out, mk_out, yg_out, st_out, ss_out, score_scr, state_scr
):
    taps = [par[k : k + 1, :] for k in range(CONV)]
    bias, skip, gain, act = par[4:5, :], par[5:6, :], par[6:7, :], par[7:8, :]
    lane = lax.broadcasted_iota(jnp.int32, (1, 128), 1)
    sides = [(lane < HEAD_DIM).astype(BF16), (lane >= HEAD_DIM).astype(BF16)]

    @pl.when(pl.program_id(0) == 0)
    def _():
        ss_out[...] = jnp.zeros_like(ss_out)
        for c in range(CHUNKS):
            r0 = chunk_start(info, c, per_block)
            _, since, _ = chunk_masks(info, c)
            bcv = bc[pl.ds(r0, SPAN), :]
            score = dot_nt(bcv[:, STATE:], bcv[:, :STATE])
            gap = lax.broadcasted_iota(jnp.int32, (SPAN, SPAN), 0) - lax.broadcasted_iota(
                jnp.int32, (SPAN, SPAN), 1
            )
            score_scr[c] = jnp.where((gap >= 0) & (gap <= wide2(since)), score, 0.0)

    state_scr[...] = jnp.zeros_like(state_scr)
    for c in range(CHUNKS):
        r0 = chunk_start(info, c, per_block)
        local, since, until = chunk_masks(info, c)
        masks = [wide2((since >= k).astype(F32)) for k in range(CONV)]
        _, lags = conv_inputs(inner, info, c, per_block, r0)
        u = conv_apply(lags, taps, bias, masks)
        xf = (u * sigmoid(u)).astype(BF16).astype(F32)
        head_rows = hs[:, pl.ds(r0, SPAN)]
        cum_rows = head_rows[:8]
        cum = cum_rows.T
        step = head_rows[8:].T
        local8, since8, until8 = local[:, :8], since[:, :8], until[:, :8]
        cum_end = cum[SPAN - 1 : SPAN, :]
        entry = jnp.where(since8 > local8, jnp.exp(cum), 0.0)
        tail = jnp.where(until8 >= SPAN - 1 - local8, jnp.exp(cum_end - cum), 0.0)
        keep = entry[SPAN - 1 : SPAN, :]
        xs = (xf * expand(step)).astype(BF16)
        xw = (xf * expand(tail * step)).astype(BF16)
        state = state_scr[...]
        state_low = state.astype(BF16)
        st_out[pl.ds(c * STATE, STATE), :] = state_low
        carried = dot_nn(bc[pl.ds(r0, SPAN), STATE:], state_low) * expand(entry)
        state_scr[...] = state * expand(keep) + dot_nn(bct[:STATE, pl.ds(r0, SPAN)], xw)
        tiles = []
        for p in range(WIDE // 128):
            tile = carried[:, p * 128 : (p + 1) * 128]
            for s in range(2):
                h = 2 * p + s
                values = xs[:, p * 128 : (p + 1) * 128] * sides[s]
                strips = []
                for at, end in BELOW:
                    gap = cum[at : at + STRIP, h : h + 1] - cum_rows[h : h + 1, :end]
                    decays = jnp.exp(jnp.minimum(gap, 0.0))
                    mixing = (decays * score_scr[c, at : at + STRIP, :end]).astype(BF16)
                    strips.append(dot_nn(mixing, values[:end]))
                tile = tile + jnp.concatenate(strips, axis=0)
            tiles.append(tile)
        y = jnp.concatenate(tiles, axis=1)
        y_out[pl.ds(r0, SPAN), :] = y.astype(BF16)
        g = gate[pl.ds(r0, SPAN), :].astype(F32)
        masked = (y + skip * xf) * act
        mk_out[pl.ds(r0, SPAN), :] = masked.astype(BF16)
        gated = masked * (g * sigmoid(g))
        yg_out[pl.ds(r0, SPAN), :] = (gated * gain).astype(BF16)
        square = gated * gated
        ss_out[pl.ds(r0, SPAN), :] += square[:, :128] + square[:, 128:]


def split_low(v):
    high = v.astype(BF16)
    return high, (v - high.astype(F32)).astype(BF16)


def gate_kernel(mk, gate, dn_in, sk, par, dgate_out, dy_out, gg_out):
    gain, act = par[6:7, :], par[7:8, :]
    total = jnp.zeros((1, WIDE), F32)
    for c in range(CHUNKS):
        rows = pl.ds(c * SPAN, SPAN)
        row_cols = sk[:, c * SPAN : (c + 1) * SPAN].T
        scale, fix = row_cols[:, 0:1], row_cols[:, 1:2]
        g = gate[rows, :].astype(F32)
        sg = sigmoid(g)
        sw = g * sg
        masked = mk[rows, :].astype(F32)
        gated = masked * sw
        d_scale = dn_in[rows, :].astype(F32) * scale
        d_gated = d_scale * gain - gated * fix
        dgate_out[rows, :] = (d_gated * masked * sg * (1.0 + g * (1.0 - sg))).astype(BF16)
        dy_out[rows, :] = (d_gated * sw * act).astype(BF16)
        total = total + jnp.sum(d_scale * gated, axis=0, keepdims=True)
    gg_out[...] = total + jnp.zeros((8, WIDE), F32)


def bwd_kernel(
    per_block,
    blocks,
    info,
    inner,
    y_in,
    dy_in,
    bc,
    bct,
    hs,
    st,
    par,
    dinner_out,
    dbc_out,
    gp_out,
    hr_out,
    score_scr,
    pair_scr,
    mask_scr,
    adj_scr,
):
    taps = [par[k : k + 1, :] for k in range(CONV)]
    bias, skip = par[4:5, :], par[5:6, :]
    lane = lax.broadcasted_iota(jnp.int32, (1, 128), 1)
    sides = [(lane < HEAD_DIM).astype(BF16), (lane >= HEAD_DIM).astype(BF16)]
    head_of = lax.broadcasted_iota(jnp.int32, (8, WIDE), 1) // HEAD_DIM
    row8 = lax.broadcasted_iota(jnp.int32, (8, WIDE), 0)
    pick = (head_of == row8).astype(BF16)
    pick_up = (head_of + 4 == row8).astype(BF16)

    @pl.when(pl.program_id(0) == 0)
    def _():
        dbc_out[...] = jnp.zeros_like(dbc_out)
        pair_scr[...] = jnp.zeros_like(pair_scr)
        for c in range(CHUNKS):
            r0 = chunk_start(info, c, per_block)
            _, since, until = chunk_masks(info, c)
            bcv = bc[pl.ds(r0, SPAN), :]
            score = dot_nt(bcv[:, :STATE], bcv[:, STATE:])
            gap = lax.broadcasted_iota(jnp.int32, (SPAN, SPAN), 1) - lax.broadcasted_iota(
                jnp.int32, (SPAN, SPAN), 0
            )
            score_scr[c] = jnp.where((gap >= 0) & (gap <= wide2(until)), score, 0.0)
            mask_scr[c] = jnp.where((gap <= 0) & (-gap <= wide2(since)), 1.0, 0.0).astype(BF16)

    adj_scr[...] = jnp.zeros_like(adj_scr)
    after = jnp.zeros((8, WIDE), F32)
    gp = jnp.zeros((8, WIDE), F32)
    for c in reversed(range(CHUNKS)):
        r0 = chunk_start(info, c, per_block)
        local, since, until = chunk_masks(info, c)
        masks = [wide2((since >= k).astype(F32)) for k in range(CONV)]
        masks_after = [wide2((until >= k).astype(F32)) for k in range(CONV)]
        _, lags = conv_inputs(inner, info, c, per_block, r0)
        u = conv_apply(lags, taps, bias, masks)
        su = sigmoid(u)
        xf = (u * su).astype(BF16).astype(F32)
        head_rows = hs[:, pl.ds(r0, SPAN)]
        cum_rows, step_rows = head_rows[:8], head_rows[8:]
        cum = cum_rows.T
        step = step_rows.T
        local8, since8, until8 = local[:, :8], since[:, :8], until[:, :8]
        cum_end = cum[SPAN - 1 : SPAN, :]
        entry = jnp.where(since8 > local8, jnp.exp(cum), 0.0)
        tail = jnp.where(until8 >= SPAN - 1 - local8, jnp.exp(cum_end - cum), 0.0)
        keep = entry[SPAN - 1 : SPAN, :]
        step_wide = expand(step)
        xs = (xf * step_wide).astype(BF16)
        xw = (xf * expand(tail * step)).astype(BF16)
        y = y_in[pl.ds(r0, SPAN), :].astype(F32)
        dy_low = dy_in[pl.ds(r0, SPAN), :]
        dy = dy_low.astype(F32)
        dy_entry = (dy * expand(entry)).astype(BF16)

        adj = adj_scr[...]
        adj_low = adj.astype(BF16)
        bcv = bc[pl.ds(r0, SPAN), :]
        d_c = dot_nt(dy_entry, st[pl.ds(c * STATE, STATE), :])
        d_b = dot_nt(xw, adj_low)
        dbc_out[pl.ds(r0, SPAN), :] += jnp.concatenate([d_b, d_c], axis=1)
        carried = dot_nn(bcv[:, :STATE], adj_low) * expand(tail)
        adj_scr[...] = adj * expand(keep) + dot_nn(bct[STATE:, pl.ds(r0, SPAN)], dy_entry)

        tiles = []
        for p in range(WIDE // 128):
            tile = carried[:, p * 128 : (p + 1) * 128]
            dy_tile = dy_low[:, p * 128 : (p + 1) * 128]
            xs_tile = xs[:, p * 128 : (p + 1) * 128]
            for s in range(2):
                h = 2 * p + s
                dy_side = dy_tile * sides[s]
                xs_side = xs_tile * sides[s]
                strips = []
                for at, begin in ABOVE:
                    rows = slice(at, at + STRIP)
                    gap = cum_rows[h : h + 1, begin:] - cum[rows, h : h + 1]
                    decays = jnp.exp(jnp.minimum(gap, 0.0))
                    mixing = (decays * score_scr[c, rows, begin:]).astype(BF16)
                    strips.append(dot_nn(mixing, dy_side[begin:]))
                    pair_scr[c, rows, begin:] += decays * dot_nt(xs_side[rows], dy_tile[begin:])
                tile = tile + jnp.concatenate(strips, axis=0)
            tiles.append(tile)
        dxu = jnp.concatenate(tiles, axis=1)

        du = (step_wide * dxu + skip * dy) * (su * (1.0 + u * (1.0 - su)))
        dinner_out[pl.ds(r0, SPAN), :] = conv_back(du, after, taps, masks_after).astype(BF16)
        after = du[:8]
        sums = [jnp.sum(du * lags[k] * masks[k], axis=0, keepdims=True) for k in range(CONV)]
        sums += [jnp.sum(du, axis=0, keepdims=True), jnp.zeros((3, WIDE), F32)]
        gp = gp + jnp.concatenate(sums, axis=0)

        q1h, q1l = split_low(dy * y)
        q2h, q2l = split_low(xf * dxu)
        q3h, q3l = split_low(xf * dy)
        row_term = dot_nt(pick, q1h) + dot_nt(pick, q1l)
        steps = dot_nt(pick, q2h) + dot_nt(pick, q2l) + dot_nt(pick_up, q3h) + dot_nt(pick_up, q3l)
        vh, vl = split_low(row_term - step_rows * jnp.where(row8 < GROUP, steps, 0.0))
        d_decay = dot_nn(vh, mask_scr[c]) + dot_nn(vl, mask_scr[c])
        row_local = lax.broadcasted_iota(jnp.int32, (8, SPAN), 1)
        row_since, row_until = doc_place(info, row_local + c * SPAN)
        if c < CHUNKS - 1:
            ph, plow = split_low(st[pl.ds((c + 1) * STATE, STATE), :].astype(F32) * adj)
            cross = jnp.sum(dot_nt(pick, ph) + dot_nt(pick, plow), axis=1, keepdims=True)
            d_decay = d_decay + jnp.where(row_until >= SPAN - 1 - row_local, cross, 0.0)
        d_decay = jnp.where(row_since > 0, d_decay, 0.0)
        hr_out[:, pl.ds(r0, SPAN)] = jnp.concatenate([steps, d_decay], axis=0)
    gp_out[...] = gp

    @pl.when(pl.program_id(0) == blocks - 1)
    def _():
        for c in range(CHUNKS):
            r0 = chunk_start(info, c, per_block)
            _, _, until = chunk_masks(info, c)
            gap = lax.broadcasted_iota(jnp.int32, (SPAN, SPAN), 1) - lax.broadcasted_iota(
                jnp.int32, (SPAN, SPAN), 0
            )
            pair_low = jnp.where((gap >= 0) & (gap <= wide2(until)), pair_scr[c], 0.0).astype(BF16)
            bcv = bc[pl.ds(r0, SPAN), :]
            dbc_out[pl.ds(r0, SPAN), :] += jnp.concatenate(
                [dot_nn(pair_low, bcv[:, STATE:]), dot_tn(pair_low, bcv[:, :STATE])], axis=1
            )


def pair_kernel(per_block, info, pairs, dbc_a, dbc_b, par, dp_out, gp_out):
    taps = [par[k : k + 1, :] for k in range(CONV)]
    after = jnp.zeros((8, WIDE), F32)
    gp = jnp.zeros((8, WIDE), F32)
    for c in reversed(range(CHUNKS)):
        r0 = chunk_start(info, c, per_block)
        _, since, until = chunk_masks(info, c)
        masks = [wide2((since >= k).astype(F32)) for k in range(CONV)]
        masks_after = [wide2((until >= k).astype(F32)) for k in range(CONV)]
        _, lags = conv_inputs(pairs, info, c, per_block, r0)
        u = conv_apply(lags, taps, par[4:5, :], masks)
        su = sigmoid(u)
        rows = pl.ds(r0, SPAN)
        du = (dbc_a[rows, :] + dbc_b[rows, :]) * (su * (1.0 + u * (1.0 - su)))
        dp_out[rows, :] = conv_back(du, after, taps, masks_after).astype(BF16)
        after = du[:8]
        sums = [jnp.sum(du * lags[k] * masks[k], axis=0, keepdims=True) for k in range(CONV)]
        sums += [jnp.sum(du, axis=0, keepdims=True), jnp.zeros((3, WIDE), F32)]
        gp = gp + jnp.concatenate(sums, axis=0)
    gp_out[...] = gp


def whole(shape):
    return pl.BlockSpec(shape, lambda i, info: (0,) * len(shape))


def cols(rows):
    return pl.BlockSpec((rows, WIDE), lambda i, info: (0, i))


def ignore(kernel, at, count):
    if not count:
        return kernel
    return lambda *refs: kernel(*refs[:at], *refs[at + count :])


def unread(later):
    return [pl.BlockSpec(memory_space=pl.ANY) for _ in later]


def call(kernel, grid, in_specs, out_specs, out_shape, scratch, us, info, *operands, later=()):
    kernel = ignore(kernel, 1 + len(operands), len(later))
    in_specs = [*in_specs, *unread(later)]
    operands = [*operands, *later]
    return pl.pallas_call(
        kernel,
        grid_spec=pltpu.PrefetchScalarGridSpec(
            num_scalar_prefetch=1,
            grid=(grid,),
            in_specs=in_specs,
            out_specs=out_specs,
            scratch_shapes=scratch,
        ),
        out_shape=out_shape,
        compiler_params=pltpu.CompilerParams(vmem_limit_bytes=VMEM_LIMIT),
        cost_estimate=lasting(us),
    )(info, *operands)


def shape(dims, kind):
    return jax.ShapeDtypeStruct(dims, kind)


def project(a, b, kind, later):
    rows, depth = a.shape
    b, number = b if isinstance(b, tuple) else (b, 0)
    columns = b.shape[-1]
    wide = min(columns, 512)
    block = pl.BlockSpec((depth, wide), lambda j: (0, j))
    if b.ndim == 4:
        block = pl.BlockSpec((b.shape[0], 1, b.shape[2], wide), lambda j: (0, number, 0, j))

    def kernel(x, w, out):
        out[...] = dot_nn(x[...], w[...].reshape(depth, wide)).astype(kind)

    return pl.pallas_call(
        ignore(kernel, 2, len(later)),
        grid=(columns // wide,),
        in_specs=[
            pl.BlockSpec((rows, depth), lambda j: (0, 0)),
            block,
            *unread(later),
        ],
        out_specs=pl.BlockSpec((rows, wide), lambda j: (0, j)),
        out_shape=shape((rows, columns), kind),
        compiler_params=pltpu.CompilerParams(vmem_limit_bytes=VMEM_LIMIT),
        cost_estimate=lasting(6),
    )(a, b, *later)


def project_few(a, b, later):
    rows, depth = a.shape
    columns = b.shape[1]

    def kernel(x, w, out):
        out[...] = dot_nn(x[...], w[...])

    return pl.pallas_call(
        ignore(kernel, 2, len(later)),
        grid=(rows // 256,),
        in_specs=[
            pl.BlockSpec((256, depth), lambda i: (i, 0)),
            pl.BlockSpec((depth, columns), lambda i: (0, 0)),
            *unread(later),
        ],
        out_specs=pl.BlockSpec((256, columns), lambda i: (i, 0)),
        out_shape=shape((rows, columns), F32),
        compiler_params=pltpu.CompilerParams(vmem_limit_bytes=VMEM_LIMIT),
        cost_estimate=lasting(3),
    )(a, b, *later)


def project_back(up, w, yg, later):
    rows, depth = up.shape
    columns = w.shape[0]
    wide = min(columns, 512)

    def kernel(x, b, y, out, sums):
        value = dot_nt(x[...], b[...])
        out[...] = value.astype(BF16)
        value = value * y[...].astype(F32)
        total = value[:, :128]
        for k in range(1, wide // 128):
            total = total + value[:, k * 128 : (k + 1) * 128]

        @pl.when(pl.program_id(0) == 0)
        def _():
            sums[...] = total

        @pl.when(pl.program_id(0) > 0)
        def _():
            sums[...] += total

    return pl.pallas_call(
        ignore(kernel, 3, len(later)),
        grid=(columns // wide,),
        in_specs=[
            pl.BlockSpec((rows, depth), lambda j: (0, 0)),
            pl.BlockSpec((wide, depth), lambda j: (j, 0)),
            pl.BlockSpec((rows, wide), lambda j: (0, j)),
            *unread(later),
        ],
        out_specs=[pl.BlockSpec((rows, wide), lambda j: (0, j)), pl.BlockSpec((rows, 128), lambda j: (0, 0))],
        out_shape=[shape((rows, columns), BF16), shape((rows, 128), F32)],
        compiler_params=pltpu.CompilerParams(vmem_limit_bytes=VMEM_LIMIT),
        cost_estimate=lasting(8),
    )(up, w, yg, *later)


def rows_forward(lefts, rights, first, rows, later=()):
    columns = rights[0].shape[1]
    wide = 512
    count = len(lefts)
    start = first // rows

    def kernel(*refs):
        total = dot_nn(refs[0][...], refs[count][...])
        for n in range(1, count):
            total = total + dot_nn(refs[n][...], refs[count + n][...])
        refs[-1][...] = total.astype(BF16)

    return pl.pallas_call(
        ignore(kernel, 2 * count, len(later)),
        grid=(columns // wide,),
        in_specs=[pl.BlockSpec((rows, v.shape[1]), lambda j: (start, 0)) for v in lefts]
        + [pl.BlockSpec((v.shape[0], wide), lambda j: (0, j)) for v in rights]
        + unread(later),
        out_specs=pl.BlockSpec((rows, wide), lambda j: (0, j)),
        out_shape=shape((rows, columns), BF16),
        compiler_params=pltpu.CompilerParams(vmem_limit_bytes=VMEM_LIMIT),
        cost_estimate=lasting(5),
    )(*lefts, *rights, *later)


def delayed(v, later):
    flat = v.reshape(-1, v.shape[-1])
    rows, width = flat.shape
    block = rows // 2 if rows % 32 == 0 else rows

    def kernel(a, out):
        out[...] = a[...]

    return pl.pallas_call(
        ignore(kernel, 1, len(later)),
        grid=(rows // block,),
        in_specs=[pl.BlockSpec((block, width), lambda i: (i, 0)), *unread(later)],
        out_specs=pl.BlockSpec((block, width), lambda i: (i, 0)),
        out_shape=shape((rows, width), v.dtype),
        compiler_params=pltpu.CompilerParams(vmem_limit_bytes=VMEM_LIMIT),
        cost_estimate=lasting(2),
    )(flat, *later).reshape(v.shape)


def added(a, b, later):
    def kernel(x, y, out):
        out[...] = (x[...].astype(F32) + y[...].astype(F32)).astype(BF16)

    return pl.pallas_call(
        ignore(kernel, 2, len(later)),
        in_specs=[pl.BlockSpec(memory_space=pltpu.VMEM)] * 2 + unread(later),
        out_specs=pl.BlockSpec(memory_space=pltpu.VMEM),
        out_shape=shape(a.shape, BF16),
        compiler_params=pltpu.CompilerParams(vmem_limit_bytes=VMEM_LIMIT),
        cost_estimate=lasting(1),
    )(a, b, *later)


def norm_rows(own, got, gain, later):
    rows, width = own.shape
    block = min(rows, 256)
    here = rows // block

    def kernel(a, b, gain_row, out):
        def write(v):
            v = v.astype(F32)
            inverse = lax.rsqrt(jnp.mean(v * v, axis=1, keepdims=True) + EPSILON)
            out[...] = (v * inverse * gain_row[...]).astype(BF16)

        @pl.when(pl.program_id(0) < here)
        def _():
            write(a[...])

        @pl.when(pl.program_id(0) >= here)
        def _():
            write(b[...])

    return pl.pallas_call(
        ignore(kernel, 3, len(later)),
        grid=(SEQ_LEN // block,),
        in_specs=[
            pl.BlockSpec((block, width), lambda i: (jnp.minimum(i, here - 1), 0)),
            pl.BlockSpec((block, width), lambda i: (jnp.maximum(i - here, 0), 0)),
            pl.BlockSpec((1, width), lambda i: (0, 0)),
            *unread(later),
        ],
        out_specs=pl.BlockSpec((block, width), lambda i: (i, 0)),
        out_shape=shape((SEQ_LEN, width), BF16),
        compiler_params=pltpu.CompilerParams(vmem_limit_bytes=VMEM_LIMIT),
        cost_estimate=lasting(4),
    )(own, got, gain[None], *later)


def prep(per_block, info, pairs, par):
    t = SEQ_LEN
    return call(
        functools.partial(prep_kernel, per_block),
        1,
        [whole((t, WIDE)), whole((8, WIDE))],
        [whole((t, WIDE)), whole((WIDE, t))],
        [shape((t, WIDE), BF16), shape((WIDE, t), BF16)],
        [],
        2,
        info,
        pairs,
        par,
    )


def scan_forward(per_block, info, inner, gate, bc, bct, hs, par, later):
    t, channels = inner.shape
    blocks = channels // WIDE
    return call(
        functools.partial(fwd_kernel, per_block),
        blocks,
        [
            cols(t),
            cols(t),
            whole((t, WIDE)),
            whole((WIDE, t)),
            pl.BlockSpec((16, t), lambda i, info: (i, 0)),
            cols(8),
        ],
        [cols(t), cols(t), cols(t), cols(CHUNKS * STATE), whole((t, 128))],
        [
            shape((t, channels), BF16),
            shape((t, channels), BF16),
            shape((t, channels), BF16),
            shape((CHUNKS * STATE, channels), BF16),
            shape((t, 128), F32),
        ],
        [pltpu.VMEM((CHUNKS, SPAN, SPAN), F32), pltpu.VMEM((STATE, WIDE), F32)],
        20,
        info,
        inner,
        gate,
        bc,
        bct,
        hs,
        par,
        later=later,
    )


def scan_backward(per_block, info, inner, y, dy, bc, bct, hs, st, par, later):
    t, channels = inner.shape
    blocks = channels // WIDE
    return call(
        functools.partial(bwd_kernel, per_block, blocks),
        blocks,
        [
            cols(t),
            cols(t),
            cols(t),
            whole((t, WIDE)),
            whole((WIDE, t)),
            pl.BlockSpec((16, t), lambda i, info: (i, 0)),
            cols(CHUNKS * STATE),
            cols(8),
        ],
        [
            cols(t),
            whole((t, WIDE)),
            cols(8),
            pl.BlockSpec((16, t), lambda i, info: (i, 0)),
        ],
        [
            shape((t, channels), BF16),
            shape((t, WIDE), F32),
            shape((8, channels), F32),
            shape((blocks * 16, t), F32),
        ],
        [
            pltpu.VMEM((CHUNKS, SPAN, SPAN), F32),
            pltpu.VMEM((CHUNKS, SPAN, SPAN), F32),
            pltpu.VMEM((CHUNKS, SPAN, SPAN), BF16),
            pltpu.VMEM((STATE, WIDE), F32),
        ],
        36,
        info,
        inner,
        y,
        dy,
        bc,
        bct,
        hs,
        st,
        par,
        later=later,
    )


def gate_backward(mk, gate, dn, sk, par, later):
    t, channels = gate.shape
    block = pl.BlockSpec((t, WIDE), lambda i: (0, i))
    small = pl.BlockSpec((8, WIDE), lambda i: (0, i))
    return pl.pallas_call(
        ignore(gate_kernel, 5, len(later)),
        grid=(channels // WIDE,),
        in_specs=[block, block, block, pl.BlockSpec((8, t), lambda i: (0, 0)), small, *unread(later)],
        out_specs=[block, block, small],
        out_shape=[shape((t, channels), BF16)] * 2 + [shape((8, channels), F32)],
        compiler_params=pltpu.CompilerParams(vmem_limit_bytes=VMEM_LIMIT),
        cost_estimate=lasting(8),
    )(mk, gate, dn, sk, par, *later)


def turned(number, bits):
    return sum(((number >> k) & 1) << (bits - 1 - k) for k in range(bits))


def grad_half(lefts, rights, half, more=None, scale=None, later=(), pieces=1, bits=0):
    t, width = lefts[0].shape
    columns = rights[0].shape[1]
    count = max(len(lefts), len(rights))
    tall = width // 2 // pieces
    high, wide = min(width // 2, 256 if bits else 512), min(columns, 1024)
    down, along = width // 2 // high, columns // wide
    group = max(high // tall, 1)
    split = max(tall // high, 1)
    if bits and group > 1:
        high, group = tall, 1
        high = max(high, 128)
        group = high // tall
        down = width // 2 // high
    resident = bits > 0 and group > 1
    if resident:
        block = pl.BlockSpec((pieces, count, tall, wide), lambda j, i, info: (0, 0, 0, j))
    else:
        block = pl.BlockSpec(
            (group, count, tall // split, wide),
            lambda j, i, info: (turned(i // split, bits) if bits else i // split, 0, i % split, j),
        )
    operands = [*lefts, *rights] + ([] if more is None else [more]) + ([] if scale is None else [scale])

    def kernel(info, *refs):
        out = refs[-1]
        for n in range(count):
            left = refs[n % len(lefts)][...]
            if scale is not None:
                left = (left.astype(F32) * refs[-2][...].T[:, 0:1]).astype(BF16)
            total = dot_tn(left, refs[len(lefts) + n % len(rights)][...])
            for g in range(group):
                rows = total if group == 1 else total[g * tall : (g + 1) * tall]
                at = turned(pl.program_id(1) * group + g, bits) if resident else g
                if more is not None:
                    rows = rows + refs[len(lefts) + len(rights)][at, n].astype(F32)
                out[at, n] = rows.astype(BF16)

    return pl.pallas_call(
        ignore(kernel, 1 + len(operands), len(later)),
        grid_spec=pltpu.PrefetchScalarGridSpec(
            num_scalar_prefetch=1,
            grid=(along, down),
            in_specs=[pl.BlockSpec((t, high), lambda j, i, info: (0, info[0] * down + i)) for _ in lefts]
            + [pl.BlockSpec((t, wide), lambda j, i, info: (0, j)) for _ in rights]
            + ([] if more is None else [block])
            + ([] if scale is None else [pl.BlockSpec((8, t), lambda j, i, info: (0, 0))])
            + unread(later),
            out_specs=block,
        ),
        out_shape=shape((pieces, count, tall, columns), BF16),
        compiler_params=pltpu.CompilerParams(vmem_limit_bytes=VMEM_LIMIT),
        cost_estimate=lasting(7),
    )(half[None], *operands, *later)


def grad_pieces(left, right, shared, batches, bits):
    t, width = left.shape
    columns = right.shape[1]
    chips = batches // 2
    tall = width // batches // 2
    high = 256
    group = high // tall

    extra = 0 if shared is None else shared.shape[1]

    def kernel(a, b, *refs):
        out = refs[-1]
        total = dot_tn(a[...], b[...]).astype(BF16)
        for g in range(group):
            block = pl.program_id(0) * group + g
            core, quarter, number = block // (2 * chips), (block // chips) % 2, block % chips
            chip = jnp.where(quarter == 0, number, turned(number, bits))
            rows = pl.ds(pl.multiple_of(quarter * tall, tall), tall)
            out[chip * 2 + core, rows, :] = total[g * tall : (g + 1) * tall]

        if extra:

            @pl.when(pl.program_id(0) == width // high - 1)
            def _():
                out[:, 2 * tall :, :] = refs[0][...]

    return pl.pallas_call(
        kernel,
        grid=(width // high,),
        in_specs=[
            pl.BlockSpec((t, high), lambda i: (0, i)),
            pl.BlockSpec((t, columns), lambda i: (0, 0)),
        ]
        + ([pl.BlockSpec(shared.shape, lambda i: (0, 0, 0))] if extra else []),
        out_specs=pl.BlockSpec((batches, 2 * tall + extra, columns), lambda i: (0, 0, 0)),
        out_shape=shape((batches, 2 * tall + extra, columns), BF16),
        compiler_params=pltpu.CompilerParams(vmem_limit_bytes=VMEM_LIMIT),
        cost_estimate=lasting(10),
    )(left, right, *([shared] if extra else []))


def place_pieces(v, tall, bits, later):
    batches, _, columns = v.shape
    chips = batches // 2

    half = chips * tall
    wide = columns // 4

    def kernel(a, out):
        for core in range(2):
            for chip in range(chips):
                v = a[chip * 2 + core]
                for quarter, number in ((0, chip), (1, turned(chip, bits))):
                    at = (core * 2 + quarter) * half + number * tall
                    out[at : at + tall, :] = v[quarter * tall : (quarter + 1) * tall].astype(F32)

    return pl.pallas_call(
        ignore(kernel, 1, len(later)),
        grid=(4,),
        in_specs=[pl.BlockSpec((batches, 2 * tall, wide), lambda i: (0, 0, i)), *unread(later)],
        out_specs=pl.BlockSpec((4 * half, wide), lambda i: (0, i)),
        out_shape=shape((4 * half, columns), F32),
        compiler_params=pltpu.CompilerParams(vmem_limit_bytes=VMEM_LIMIT),
        cost_estimate=lasting(7),
    )(v, *later)


def place_halves(mine, other, core):
    rows, columns = mine.shape
    high = min(rows, 256)
    per = rows // high

    def kernel(info, a, b, out):
        here = pl.program_id(0) // per == info[0]

        @pl.when(here)
        def _():
            out[...] = a[...].astype(F32)

        @pl.when(jnp.logical_not(here))
        def _():
            out[...] = b[...].astype(F32)

    return pl.pallas_call(
        kernel,
        grid_spec=pltpu.PrefetchScalarGridSpec(
            num_scalar_prefetch=1,
            grid=(2 * per,),
            in_specs=[
                pl.BlockSpec((high, columns), lambda i, info: (jnp.clip(i - info[0] * per, 0, per - 1), 0)),
                pl.BlockSpec((high, columns), lambda i, info: (jnp.clip(i - (1 - info[0]) * per, 0, per - 1), 0)),
            ],
            out_specs=pl.BlockSpec((high, columns), lambda i, info: (i, 0)),
        ),
        out_shape=shape((2 * rows, columns), F32),
        compiler_params=pltpu.CompilerParams(vmem_limit_bytes=VMEM_LIMIT),
        cost_estimate=lasting(6),
    )(core[None], mine, other)


def small_grads(left, right, later):
    t, columns = right.shape
    wide = 512

    def kernel(a, b, out):
        out[...] = dot_tn(a[...], b[...])

    return pl.pallas_call(
        ignore(kernel, 2, len(later)),
        grid=(columns // wide,),
        in_specs=[
            pl.BlockSpec(left.shape, lambda j: (0, 0)),
            pl.BlockSpec((t, wide), lambda j: (0, j)),
            *unread(later),
        ],
        out_specs=pl.BlockSpec((left.shape[1], wide), lambda j: (0, j)),
        out_shape=shape((left.shape[1], columns), F32),
        compiler_params=pltpu.CompilerParams(vmem_limit_bytes=VMEM_LIMIT),
        cost_estimate=lasting(4),
    )(left, right, *later)


def rows_back(lefts, rights, first, rows, gain_rows, later=()):
    columns = rights[0].shape[0]
    wide = 512

    def right_block(v):
        if not isinstance(v, tuple):
            return pl.BlockSpec((wide, v.shape[1]), lambda j: (j, 0))
        v, number = v
        return pl.BlockSpec((wide // v.shape[2], 1, v.shape[2], v.shape[3]), lambda j: (j, number, 0, 0))

    count = len(lefts)
    start = first // rows

    def kernel(*refs):
        total = dot_nt(refs[0][...], refs[count][...].reshape(wide, -1))
        for n in range(1, count):
            total = total + dot_nt(refs[n][...], refs[count + n][...].reshape(wide, -1))
        unit, out, sums = refs[-3:]
        out[...] = total.astype(BF16)
        sums[...] = jnp.sum(total * unit[...].astype(F32), axis=0, keepdims=True) + jnp.zeros((8, wide), F32)

    return pl.pallas_call(
        ignore(kernel, 2 * count + 1, len(later)),
        grid=(columns // wide,),
        in_specs=[pl.BlockSpec((rows, v.shape[1]), lambda j: (start, 0)) for v in lefts]
        + [right_block(v) for v in rights]
        + [pl.BlockSpec((rows, wide), lambda j: (start, j))]
        + unread(later),
        out_specs=[pl.BlockSpec((rows, wide), lambda j: (0, j)), pl.BlockSpec((8, wide), lambda j: (0, j))],
        out_shape=[shape((rows, columns), BF16), shape((8, columns), F32)],
        compiler_params=pltpu.CompilerParams(vmem_limit_bytes=VMEM_LIMIT),
        cost_estimate=lasting(15),
    )(*lefts, *[v[0] if isinstance(v, tuple) else v for v in rights], gain_rows, *later)


def pair_backward(per_block, info, pairs, dbc_a, dbc_b, par):
    t = SEQ_LEN
    return call(
        functools.partial(pair_kernel, per_block),
        1,
        [whole((t, WIDE)), whole((t, WIDE)), whole((t, WIDE)), whole((8, WIDE))],
        [whole((t, WIDE)), whole((8, WIDE))],
        [shape((t, WIDE), BF16), shape((8, WIDE), F32)],
        [],
        4,
        info,
        pairs,
        dbc_a,
        dbc_b,
        par,
    )


def body(
    axis_sizes,
    hidden_in,
    out_grad,
    norm_gain,
    w_z,
    w_x,
    w_dt,
    w_bc,
    conv_x,
    conv_x_bias,
    conv_bc,
    conv_bc_bias,
    dt_bias,
    a_log,
    d_skip,
    gate_gain,
    w_out,
    doc_lengths,
    widths,
):
    batches, stacks = axis_sizes
    rows, width_in = hidden_in.shape
    heads_here = dt_bias.shape[0]
    channels = w_x.shape[1]
    members = stacks // widths.shape[0]
    far_bit = members
    per_block = rows // SPAN
    place = lax.axis_index("head")
    lot = lax.axis_index("batch")
    own_seq = place // members
    ends = jnp.cumsum(lax.dynamic_index_in_dim(doc_lengths, own_seq, 0, keepdims=False))
    width = lax.dynamic_index_in_dim(widths, own_seq, 0, keepdims=False)
    info = jnp.concatenate([ends.astype(jnp.int32), (place % members).astype(jnp.int32)[None]])

    def across(v, bit):
        return lax.ppermute(v, "head", [(i, i ^ bit) for i in range(stacks)])

    def sum_rows(v):
        bit = 1
        while bit < members:
            got = across(v, bit)
            flipped = got.reshape(v.shape[0], -1, 2, bit * rows)[:, :, ::-1, :].reshape(v.shape)
            v = v + flipped
            bit *= 2
        return v

    chip_bits = []
    bit = 2
    while bit < batches:
        chip_bits.append(bit)
        bit *= 2
    chips = batches // 2
    core = lot % 2
    chip_groups = [[2 * i + c for i in range(chips)] for c in range(2)]
    orders = (chip_bits, chip_bits[::-1])

    def planar(v, bit):
        return lax.ppermute(v, "batch", [(i, i ^ bit) for i in range(batches)])

    def side(bit):
        return (lot // bit) % 2

    def join(v, got, bit, axis=0):
        low, high = jnp.concatenate([v, got], axis=axis), jnp.concatenate([got, v], axis=axis)
        return jnp.where(side(bit) == 0, low, high)

    def add(a, b):
        return (a.astype(F32) + b.astype(F32)).astype(BF16)

    def nothing(v):
        return (v[(0,) * v.ndim].astype(F32) * 0.0).astype(jnp.int32)

    def others(v):
        got, bit = across(v, 1), 2
        while bit < members:
            got = jnp.concatenate([got, across(jnp.concatenate([v, got], axis=0), bit)], axis=0)
            bit *= 2
        return got

    hidden_got = others(hidden_in)
    piece = width_in // batches
    far_parts = across(
        jnp.concatenate([lax.dynamic_slice_in_dim(w, lot * piece, piece, 0) for w in (w_x, w_z)], axis=0), far_bit
    )
    w_dt_own = w_dt.T
    w_dt_far = across(w_dt_own, far_bit)
    head_row = jnp.concatenate([dt_bias, a_log])
    par_own = jnp.concatenate(
        [
            conv_x,
            conv_x_bias[None],
            jnp.repeat(d_skip, HEAD_DIM)[None],
            gate_gain[None],
            jnp.pad(head_row, (0, channels - head_row.shape[0]))[None],
        ],
        axis=0,
    )
    par_far = across(par_own, far_bit)
    up_sent = delayed(out_grad, (hidden_got,))
    normed = norm_rows(hidden_in, hidden_got, norm_gain, (far_parts, w_dt_far, par_far, up_sent))
    far_parts = delayed(far_parts, (hidden_got, w_dt_far, par_far))
    far_parts = delayed(far_parts, (hidden_got, w_dt_far, par_far))
    far_both = lax.all_gather(far_parts, "batch", axis=0, tiled=True).reshape(batches, 2, piece, channels)
    out_piece = channels // batches
    w_out_part = across(
        lax.dynamic_slice_in_dim(w_out, lot * out_piece + nothing(normed), out_piece, 0), far_bit
    )
    up_got = others(up_sent)
    upstream = jnp.concatenate([out_grad, up_got], axis=0)
    active = (jnp.arange(channels) // HEAD_DIM < width * heads_here // (heads_here * stacks)).astype(F32)
    rate_par = [(v[7, :heads_here], v[7, heads_here : 2 * heads_here]) for v in (par_own, par_far)]
    par2 = [jnp.concatenate([v[:7], active[None]], axis=0) for v in (par_own, par_far)]
    step_bias = jnp.concatenate([rate_par[0][0], rate_par[1][0]])[:, None]
    speed = jnp.exp(jnp.concatenate([rate_par[0][1], rate_par[1][1]]))[:, None]
    par_bc = jnp.concatenate([conv_bc, conv_bc_bias[None], jnp.zeros((3, 2 * STATE), F32)], axis=0)

    w_small = jnp.concatenate([w_bc, w_dt_own.T, w_dt_far.T], axis=1)
    small_cols = project_few(normed, w_small, ())
    pairs = small_cols[:, : 2 * STATE]
    rates = small_cols[:, 2 * STATE :].T
    step = jax.nn.softplus(rates + step_bias)
    decay = -step * speed
    upper = (jnp.arange(SPAN)[:, None] <= jnp.arange(SPAN)[None, :]).astype(F32)
    cum = lax.dot_general(
        decay.reshape(-1, SPAN), upper, (((1,), (0,)), ((), ())), precision=lax.Precision.HIGHEST
    ).reshape(decay.shape)

    def grouped(v):
        v = v.reshape(-1, GROUP, SEQ_LEN)
        return jnp.pad(v, ((0, 0), (0, 8 - GROUP), (0, 0)))

    hs = jnp.concatenate([grouped(cum), grouped(step)], axis=1).reshape(-1, SEQ_LEN)
    half = hs.shape[0] // 2
    hs2 = (hs[:half], hs[half:])
    bc, bct = prep(per_block, info, pairs, par_bc)

    inner_own = project(normed, w_x, BF16, (bc,))
    gate_own = project(normed, w_z, BF16, (inner_own,))
    forward_own = scan_forward(per_block, info, inner_own, gate_own, bc, bct, hs2[0], par2[0], (up_got,))
    dn_own = project_back(upstream, w_out, forward_own[2], ())
    w_x_far, w_z_far = (far_both, 0), (far_both, 1)
    w_out_far = lax.all_gather(delayed(w_out_part, (forward_own[0],)), "batch", axis=0, tiled=True)
    w_x2 = (w_x, w_x_far)
    w_z2 = (w_z, w_z_far)
    w_out2 = (w_out, w_out_far)
    inner2 = (inner_own, project(normed, w_x_far, BF16, (dn_own[0],)))
    gate2 = (gate_own, project(normed, w_z_far, BF16, (inner2[1],)))
    forward = (forward_own, scan_forward(per_block, info, inner2[1], gate2[1], bc, bct, hs2[1], par2[1], ()))
    y2, mk2, yg2, st2 = [[f[k] for f in forward] for k in range(4)]
    dn_far = project_back(upstream, w_out_far, yg2[1], ())
    dn2 = (dn_own[0], dn_far[0])

    def branch_rows(first, count):
        return rows_forward(yg2, w_out2, first, count, (dn_far[0],) if first else (give_out,))

    def scatter_rows(make):
        if members == 2:
            give = make(rows, rows)
            got = across(give, 1)
            return give, got, lambda: make(0, rows).astype(F32) + got.astype(F32)
        v = make(0, SEQ_LEN)
        bit = members // 2
        while bit >= 1:
            half = v.shape[0] // 2
            v = add(v[:half], across(v[half:], bit))
            bit //= 2
        return v, v, lambda: v.astype(F32)

    give_out = dn_far[0]
    branch_given, branch_got, branch = scatter_rows(branch_rows)
    square = jnp.sum(forward[0][4] + forward[1][4], axis=1)
    sums = sum_rows(jnp.stack([square, jnp.sum(dn_own[1] + dn_far[1], axis=1)]))
    count = (width * HEAD_DIM).astype(F32)
    scale = lax.rsqrt(sums[0] / count + EPSILON)
    fix = scale * scale * scale * sums[1] / count
    sk = jnp.concatenate([scale[None], fix[None], jnp.zeros((6, SEQ_LEN), F32)], axis=0)

    bits = len(chip_bits)

    def swap_halves(lefts, rights, scale=None, later=(), pieces=1, bits=0):
        give = grad_half(lefts, rights, 1 - core, None, scale, later, pieces, bits)
        got = planar(give, 1)
        return give, lambda later=(): grad_half(lefts, rights, core, got, scale, later, pieces, bits)

    def scatter_offloaded(mine):
        flat = mine.reshape(-1, mine.shape[-1])
        part = lax.psum_scatter(flat, "batch", scatter_dimension=0, tiled=True, axis_index_groups=chip_groups)
        return part.reshape(mine.shape[1:])

    def send_far(part, earlier):
        far = lax.dynamic_slice_in_dim(part, 1 + jnp.minimum(nothing(earlier), 0), 1, 0)[0]
        return across(far, far_bit)

    def gather_both(parts, seen):
        for step in range(bits):
            got = [planar(v, order[step]) for v, order in zip(parts, orders)]
            parts = [join(v, g, order[step]) for v, g, order in zip(parts, got, orders)]
            seen.append(parts)
        return parts, [planar(v, 1) for v in parts]

    give_out, keep_out = swap_halves(yg2, [upstream], sk, (branch_given,), pieces=chips)
    gates = [gate_backward(mk2[i], gate2[i], dn2[i], sk, par2[i], (give_out,)) for i in range(2)]
    d_gate2 = [v[0] for v in gates]
    mine_out = keep_out(later=(d_gate2[0],))
    part_out = scatter_offloaded(mine_out)
    give_z, keep_z = swap_halves([normed], d_gate2, later=(mine_out,), pieces=chips, bits=bits)
    give_out = give_z
    branch_sum = branch()
    mixed = (hidden_in.astype(F32) + branch_sum * scale[:rows, None]).astype(BF16)
    mine_z = keep_z(later=(give_z,))
    part_z = scatter_offloaded(mine_z)

    def scan_back(i, later):
        return scan_backward(per_block, info, inner2[i], y2[i], gates[i][1], bc, bct, hs2[i], st2[i], par2[i], later)

    back = [None, None]
    back[1] = scan_back(1, (mine_z,))
    far_cut = grad_pieces(normed, back[1][0], None, batches, bits)
    far_piece = lax.psum_scatter(far_cut.reshape(-1, channels), "batch", scatter_dimension=0, tiled=True)
    far_out = send_far(part_out, back[1][0])
    back[0] = scan_back(0, (far_cut,))
    total_out = added(part_out[0], far_out, (back[0][0],))
    d_pairs, g_bc = pair_backward(per_block, info, pairs, back[0][1], back[1][1], par_bc)
    heads_out = [b[3].reshape(-1, 16, SEQ_LEN) for b in back]
    d_step = jnp.concatenate([h[:, :GROUP].reshape(-1, SEQ_LEN) for h in heads_out], axis=0)
    skip_rows = jnp.concatenate([h[:, GROUP : 2 * GROUP].reshape(-1, SEQ_LEN) for h in heads_out], axis=0)
    d_decay = jnp.concatenate([h[:, 8 : 8 + GROUP].reshape(-1, SEQ_LEN) for h in heads_out], axis=0)
    d_rates_pre = (d_step - d_decay * speed) * jax.nn.sigmoid(rates + step_bias)
    head_grads = jnp.stack(
        [jnp.sum(d_rates_pre, axis=1), jnp.sum(d_decay * decay, axis=1), jnp.sum(skip_rows, axis=1)]
    )
    d_rates = d_rates_pre.astype(BF16)
    d_small = jnp.concatenate([d_pairs, d_rates.T], axis=1)

    g_small = small_grads(d_small, normed, (part_z, total_out, branch_got))

    def pack(i):
        gp = back[i][2]
        heads = head_grads[:, i * heads_here : (i + 1) * heads_here].reshape(-1)
        heads = jnp.pad(heads, (0, channels - heads.shape[0]))[None]
        start = 2 * STATE + i * heads_here
        return jnp.concatenate(
            [gp[:5], heads, gates[i][2][:1], gp[7:], g_small[start : start + heads_here].reshape(-1, channels)], axis=0
        )

    def spread(v):
        v = jnp.pad(v.astype(BF16), ((0, -v.shape[0] % (16 * batches)), (0, 0)))
        return v.reshape(batches, -1, channels)

    far_z = send_far(part_z, g_small)
    norm_sums = []

    def normed_rows(first, count):
        part, total = rows_back(
            [*d_gate2, back[0][0], back[1][0], d_small],
            [*w_z2, *w_x2, w_small],
            first,
            count,
            normed,
            (norm_sums[0], far_z) if norm_sums else (g_small,),
        )
        norm_sums.append(total)
        return part

    _, d_normed_got, d_normed_in = scatter_rows(normed_rows)
    d_normed_in = d_normed_in()
    bc_rows, few_rows = 2 * STATE * width_in // channels, 8 * 2 * STATE // channels
    shared = spread(jnp.concatenate([g_small[: 2 * STATE].reshape(-1, channels), g_bc.reshape(-1, channels), sum(norm_sums)[:1].reshape(-1, channels)], axis=0))
    private = spread(pack(0) + across(pack(1), far_bit))
    own_cut = grad_pieces(normed, back[0][0], jnp.concatenate([shared, private], axis=1), batches, bits)
    own_part = lax.psum_scatter(own_cut.reshape(-1, channels), "batch", scatter_dimension=0, tiled=True)
    seen = []
    total_z = added(part_z[0], far_z, (own_cut,))
    total_out = delayed(total_out, (total_z, d_normed_got))
    halves_here, halves_there = gather_both([total_out, total_z], seen)
    own_part = delayed(own_part, halves_here)

    cut = 2 * (width_in // batches // 2)
    far_sent = across(delayed(far_piece, seen[0]), far_bit)
    bc_piece = own_part[cut : cut + shared.shape[1]]
    bit = 1
    while bit < stacks:
        bc_piece = add(bc_piece, across(bc_piece, bit))
        bit *= 2
    own_total = jnp.concatenate(
        [add(own_part[:cut], far_sent), bc_piece, own_part[cut + shared.shape[1] :]], axis=0
    )
    everything = lax.all_gather(own_total, "batch", axis=0, tiled=True).reshape(batches, -1, channels)
    g_w_out, g_w_z = [place_halves(v, got, core) for v, got in zip(halves_here, halves_there)]
    common = everything[:, cut : cut + shared.shape[1]].reshape(-1, channels).astype(F32)
    packed = everything[:, cut + shared.shape[1] :].reshape(-1, channels).astype(F32)
    g_w_bc = common[:bc_rows].reshape(2 * STATE, width_in).T
    g_bc_total = common[bc_rows : bc_rows + few_rows].reshape(8, -1)
    heads_total = packed[5]
    g_w_dt = packed[8 : 8 + heads_here * width_in // channels].reshape(heads_here, width_in).T
    g_norm = common[bc_rows + few_rows : bc_rows + few_rows + width_in // channels].reshape(-1) / norm_gain

    residual = hidden_in.astype(F32)
    inverse = lax.rsqrt(jnp.mean(residual * residual, axis=-1, keepdims=True) + EPSILON)
    unit_rows = residual * inverse
    d_unit = d_normed_in * norm_gain
    d_residual = inverse * (d_unit - unit_rows * jnp.mean(d_unit * unit_rows, axis=-1, keepdims=True))
    in_grad = (out_grad.astype(F32) + d_residual).astype(BF16)
    g_w_x = place_pieces(everything, cut // 2, bits, (g_w_out, g_w_z, in_grad))
    return (
        mixed,
        in_grad,
        g_norm,
        g_w_z,
        g_w_x,
        g_w_dt,
        g_w_bc,
        packed[:4],
        packed[4],
        g_bc_total[:4],
        g_bc_total[4],
        heads_total[:heads_here],
        heads_total[heads_here : 2 * heads_here],
        heads_total[2 * heads_here : 3 * heads_here],
        packed[6],
        g_w_out,
    )


def solution(mesh):
    split = P(("batch", "head"), None)
    by_col, by_head, by_row = P(None, "head"), P("head"), P("head", None)
    return jax.shard_map(
        functools.partial(body, (mesh.shape["batch"], mesh.shape["head"])),
        mesh=mesh,
        in_specs=(
            split,
            split,
            P(),
            by_col,
            by_col,
            by_col,
            P(),
            by_col,
            by_head,
            P(),
            P(),
            by_head,
            by_head,
            by_head,
            by_head,
            by_row,
            P("batch", None),
            P("batch"),
        ),
        out_specs=(
            split,
            split,
            P(),
            by_col,
            by_col,
            by_col,
            P(),
            by_col,
            by_head,
            P(),
            P(),
            by_head,
            by_head,
            by_head,
            by_head,
            by_row,
        ),
        check_vma=False,
    )
```

```python
import functools

import jax
import jax.numpy as jnp
from jax import lax
from jax.experimental import pallas as pl
from jax.experimental.pallas import tpu as pltpu
from jax.sharding import PartitionSpec as P

HEAD_DIM = 64
STATE = 128
CONV = 4
SPAN = 256
SEQ_LEN = 1024
DOCS = 4
CHUNKS = SEQ_LEN // SPAN
WIDE = 256
GROUP = WIDE // HEAD_DIM
STRIP = 128
BELOW = [(k * STRIP, -(-(k + 1) * STRIP // 128) * 128) for k in range(SPAN // STRIP)]
ABOVE = [(k * STRIP, k * STRIP // 128 * 128) for k in range(SPAN // STRIP)]
EPSILON = 1e-05
F32 = jnp.float32
BF16 = jnp.bfloat16
VMEM_LIMIT = 48 * 1024 * 1024


PACE = 0.01e9


def lasting(us):
    return pl.CostEstimate(flops=int(us * PACE), bytes_accessed=1000, transcendentals=0)


def dot_nn(a, b):
    return lax.dot_general(a, b, (((1,), (0,)), ((), ())), preferred_element_type=F32)


def dot_nt(a, b):
    return lax.dot_general(a, b, (((1,), (1,)), ((), ())), preferred_element_type=F32)


def dot_tn(a, b):
    return lax.dot_general(a, b, (((0,), (0,)), ((), ())), preferred_element_type=F32)


def sigmoid(v):
    return 0.5 * (1.0 + jnp.tanh(0.5 * v))


def chunk_start(info, c, per_block):
    block = (c // per_block) ^ info[DOCS]
    return pl.multiple_of((block * per_block + c % per_block) * SPAN, SPAN)


def doc_place(info, pos):
    first = jnp.zeros_like(pos)
    last = jnp.full_like(pos, SEQ_LEN)
    for k in range(DOCS):
        first = jnp.where(pos >= info[k], info[k], first)
    for k in reversed(range(DOCS)):
        last = jnp.where(pos < info[k], info[k], last)
    return pos - first, last - 1 - pos


def chunk_masks(info, c):
    local = lax.broadcasted_iota(jnp.int32, (SPAN, 128), 0)
    since, until = doc_place(info, local + c * SPAN)
    return local, since, until


def wide2(v):
    return jnp.concatenate([v, v], axis=1)


def expand(cols):
    rows = cols.shape[0]
    low = lax.broadcasted_iota(jnp.int32, (rows, 128), 1) < HEAD_DIM
    tiles = [
        jnp.where(low, cols[:, 2 * p : 2 * p + 1], cols[:, 2 * p + 1 : 2 * p + 2]) for p in range(WIDE // 128)
    ]
    return jnp.concatenate(tiles, axis=1)


def conv_inputs(src, info, c, per_block, r0):
    now = src[pl.ds(r0, SPAN), :].astype(F32)
    if c == 0:
        before = jnp.zeros((8, now.shape[1]), F32)
    else:
        p0 = chunk_start(info, c - 1, per_block)
        before = src[pl.ds(pl.multiple_of(p0 + SPAN - 16, 16), 16), :].astype(F32)[8:]
    ext = jnp.concatenate([before, now], axis=0)
    return now, [now] + [pltpu.roll(ext, k, 0)[8:] for k in range(1, CONV)]


def conv_apply(lags, taps, bias, masks):
    u = bias + taps[0] * lags[0]
    for k in range(1, CONV):
        u = u + taps[k] * (lags[k] * masks[k])
    return u


def conv_back(du, after, taps, masks_after):
    ext = jnp.concatenate([du, after], axis=0)
    total = taps[0] * du
    for k in range(1, CONV):
        total = total + taps[k] * (pltpu.roll(ext, SPAN + 8 - k, 0)[:SPAN] * masks_after[k])
    return total


def prep_kernel(per_block, info, pairs, par, bc_out, bct_out):
    taps = [par[k : k + 1, :] for k in range(CONV)]
    for c in range(CHUNKS):
        r0 = chunk_start(info, c, per_block)
        _, since, _ = chunk_masks(info, c)
        masks = [wide2((since >= k).astype(F32)) for k in range(CONV)]
        _, lags = conv_inputs(pairs, info, c, per_block, r0)
        u = conv_apply(lags, taps, par[4:5, :], masks)
        low = (u * sigmoid(u)).astype(BF16)
        bc_out[pl.ds(r0, SPAN), :] = low
        bct_out[:, pl.ds(r0, SPAN)] = low.T


def fwd_kernel(
    per_block, info, inner, gate, bc, bct, hs, par, y_out, mk_out, yg_out, st_out, ss_out, score_scr, state_scr
):
    taps = [par[k : k + 1, :] for k in range(CONV)]
    bias, skip, gain, act = par[4:5, :], par[5:6, :], par[6:7, :], par[7:8, :]
    lane = lax.broadcasted_iota(jnp.int32, (1, 128), 1)
    sides = [(lane < HEAD_DIM).astype(BF16), (lane >= HEAD_DIM).astype(BF16)]

    @pl.when(pl.program_id(0) == 0)
    def _():
        ss_out[...] = jnp.zeros_like(ss_out)
        for c in range(CHUNKS):
            r0 = chunk_start(info, c, per_block)
            _, since, _ = chunk_masks(info, c)
            bcv = bc[pl.ds(r0, SPAN), :]
            score = dot_nt(bcv[:, STATE:], bcv[:, :STATE])
            gap = lax.broadcasted_iota(jnp.int32, (SPAN, SPAN), 0) - lax.broadcasted_iota(
                jnp.int32, (SPAN, SPAN), 1
            )
            score_scr[c] = jnp.where((gap >= 0) & (gap <= wide2(since)), score, 0.0)

    state_scr[...] = jnp.zeros_like(state_scr)
    for c in range(CHUNKS):
        r0 = chunk_start(info, c, per_block)
        local, since, until = chunk_masks(info, c)
        masks = [wide2((since >= k).astype(F32)) for k in range(CONV)]
        _, lags = conv_inputs(inner, info, c, per_block, r0)
        u = conv_apply(lags, taps, bias, masks)
        xf = (u * sigmoid(u)).astype(BF16).astype(F32)
        head_rows = hs[:, pl.ds(r0, SPAN)]
        cum_rows = head_rows[:8]
        cum = cum_rows.T
        step = head_rows[8:].T
        local8, since8, until8 = local[:, :8], since[:, :8], until[:, :8]
        cum_end = cum[SPAN - 1 : SPAN, :]
        entry = jnp.where(since8 > local8, jnp.exp(cum), 0.0)
        tail = jnp.where(until8 >= SPAN - 1 - local8, jnp.exp(cum_end - cum), 0.0)
        keep = entry[SPAN - 1 : SPAN, :]
        xs = (xf * expand(step)).astype(BF16)
        xw = (xf * expand(tail * step)).astype(BF16)
        state = state_scr[...]
        state_low = state.astype(BF16)
        st_out[pl.ds(c * STATE, STATE), :] = state_low
        carried = dot_nn(bc[pl.ds(r0, SPAN), STATE:], state_low) * expand(entry)
        state_scr[...] = state * expand(keep) + dot_nn(bct[:STATE, pl.ds(r0, SPAN)], xw)
        tiles = []
        for p in range(WIDE // 128):
            tile = carried[:, p * 128 : (p + 1) * 128]
            for s in range(2):
                h = 2 * p + s
                values = xs[:, p * 128 : (p + 1) * 128] * sides[s]
                strips = []
                for at, end in BELOW:
                    gap = cum[at : at + STRIP, h : h + 1] - cum_rows[h : h + 1, :end]
                    decays = jnp.exp(jnp.minimum(gap, 0.0))
                    mixing = (decays * score_scr[c, at : at + STRIP, :end]).astype(BF16)
                    strips.append(dot_nn(mixing, values[:end]))
                tile = tile + jnp.concatenate(strips, axis=0)
            tiles.append(tile)
        y = jnp.concatenate(tiles, axis=1)
        y_out[pl.ds(r0, SPAN), :] = y.astype(BF16)
        g = gate[pl.ds(r0, SPAN), :].astype(F32)
        masked = (y + skip * xf) * act
        mk_out[pl.ds(r0, SPAN), :] = masked.astype(BF16)
        gated = masked * (g * sigmoid(g))
        yg_out[pl.ds(r0, SPAN), :] = (gated * gain).astype(BF16)
        square = gated * gated
        ss_out[pl.ds(r0, SPAN), :] += square[:, :128] + square[:, 128:]


def split_low(v):
    high = v.astype(BF16)
    return high, (v - high.astype(F32)).astype(BF16)


def gate_kernel(mk, gate, dn_in, sk, par, dgate_out, dy_out, gg_out):
    gain, act = par[6:7, :], par[7:8, :]
    total = jnp.zeros((1, WIDE), F32)
    for c in range(CHUNKS):
        rows = pl.ds(c * SPAN, SPAN)
        row_cols = sk[:, c * SPAN : (c + 1) * SPAN].T
        scale, fix = row_cols[:, 0:1], row_cols[:, 1:2]
        g = gate[rows, :].astype(F32)
        sg = sigmoid(g)
        sw = g * sg
        masked = mk[rows, :].astype(F32)
        gated = masked * sw
        d_scale = dn_in[rows, :].astype(F32) * scale
        d_gated = d_scale * gain - gated * fix
        dgate_out[rows, :] = (d_gated * masked * sg * (1.0 + g * (1.0 - sg))).astype(BF16)
        dy_out[rows, :] = (d_gated * sw * act).astype(BF16)
        total = total + jnp.sum(d_scale * gated, axis=0, keepdims=True)
    gg_out[...] = total + jnp.zeros((8, WIDE), F32)


def bwd_kernel(
    per_block,
    blocks,
    info,
    inner,
    y_in,
    dy_in,
    bc,
    bct,
    hs,
    st,
    par,
    dinner_out,
    dbc_out,
    gp_out,
    hr_out,
    score_scr,
    pair_scr,
    mask_scr,
    adj_scr,
):
    taps = [par[k : k + 1, :] for k in range(CONV)]
    bias, skip = par[4:5, :], par[5:6, :]
    lane = lax.broadcasted_iota(jnp.int32, (1, 128), 1)
    sides = [(lane < HEAD_DIM).astype(BF16), (lane >= HEAD_DIM).astype(BF16)]
    head_of = lax.broadcasted_iota(jnp.int32, (8, WIDE), 1) // HEAD_DIM
    row8 = lax.broadcasted_iota(jnp.int32, (8, WIDE), 0)
    pick = (head_of == row8).astype(BF16)
    pick_up = (head_of + 4 == row8).astype(BF16)

    @pl.when(pl.program_id(0) == 0)
    def _():
        dbc_out[...] = jnp.zeros_like(dbc_out)
        pair_scr[...] = jnp.zeros_like(pair_scr)
        for c in range(CHUNKS):
            r0 = chunk_start(info, c, per_block)
            _, since, until = chunk_masks(info, c)
            bcv = bc[pl.ds(r0, SPAN), :]
            score = dot_nt(bcv[:, :STATE], bcv[:, STATE:])
            gap = lax.broadcasted_iota(jnp.int32, (SPAN, SPAN), 1) - lax.broadcasted_iota(
                jnp.int32, (SPAN, SPAN), 0
            )
            score_scr[c] = jnp.where((gap >= 0) & (gap <= wide2(until)), score, 0.0)
            mask_scr[c] = jnp.where((gap <= 0) & (-gap <= wide2(since)), 1.0, 0.0).astype(BF16)

    adj_scr[...] = jnp.zeros_like(adj_scr)
    after = jnp.zeros((8, WIDE), F32)
    gp = jnp.zeros((8, WIDE), F32)
    for c in reversed(range(CHUNKS)):
        r0 = chunk_start(info, c, per_block)
        local, since, until = chunk_masks(info, c)
        masks = [wide2((since >= k).astype(F32)) for k in range(CONV)]
        masks_after = [wide2((until >= k).astype(F32)) for k in range(CONV)]
        _, lags = conv_inputs(inner, info, c, per_block, r0)
        u = conv_apply(lags, taps, bias, masks)
        su = sigmoid(u)
        xf = (u * su).astype(BF16).astype(F32)
        head_rows = hs[:, pl.ds(r0, SPAN)]
        cum_rows, step_rows = head_rows[:8], head_rows[8:]
        cum = cum_rows.T
        step = step_rows.T
        local8, since8, until8 = local[:, :8], since[:, :8], until[:, :8]
        cum_end = cum[SPAN - 1 : SPAN, :]
        entry = jnp.where(since8 > local8, jnp.exp(cum), 0.0)
        tail = jnp.where(until8 >= SPAN - 1 - local8, jnp.exp(cum_end - cum), 0.0)
        keep = entry[SPAN - 1 : SPAN, :]
        step_wide = expand(step)
        xs = (xf * step_wide).astype(BF16)
        xw = (xf * expand(tail * step)).astype(BF16)
        y = y_in[pl.ds(r0, SPAN), :].astype(F32)
        dy_low = dy_in[pl.ds(r0, SPAN), :]
        dy = dy_low.astype(F32)
        dy_entry = (dy * expand(entry)).astype(BF16)

        adj = adj_scr[...]
        adj_low = adj.astype(BF16)
        bcv = bc[pl.ds(r0, SPAN), :]
        d_c = dot_nt(dy_entry, st[pl.ds(c * STATE, STATE), :])
        d_b = dot_nt(xw, adj_low)
        dbc_out[pl.ds(r0, SPAN), :] += jnp.concatenate([d_b, d_c], axis=1)
        carried = dot_nn(bcv[:, :STATE], adj_low) * expand(tail)
        adj_scr[...] = adj * expand(keep) + dot_nn(bct[STATE:, pl.ds(r0, SPAN)], dy_entry)

        tiles = []
        for p in range(WIDE // 128):
            tile = carried[:, p * 128 : (p + 1) * 128]
            dy_tile = dy_low[:, p * 128 : (p + 1) * 128]
            xs_tile = xs[:, p * 128 : (p + 1) * 128]
            for s in range(2):
                h = 2 * p + s
                dy_side = dy_tile * sides[s]
                xs_side = xs_tile * sides[s]
                strips = []
                for at, begin in ABOVE:
                    rows = slice(at, at + STRIP)
                    gap = cum_rows[h : h + 1, begin:] - cum[rows, h : h + 1]
                    decays = jnp.exp(jnp.minimum(gap, 0.0))
                    mixing = (decays * score_scr[c, rows, begin:]).astype(BF16)
                    strips.append(dot_nn(mixing, dy_side[begin:]))
                    pair_scr[c, rows, begin:] += decays * dot_nt(xs_side[rows], dy_tile[begin:])
                tile = tile + jnp.concatenate(strips, axis=0)
            tiles.append(tile)
        dxu = jnp.concatenate(tiles, axis=1)

        du = (step_wide * dxu + skip * dy) * (su * (1.0 + u * (1.0 - su)))
        dinner_out[pl.ds(r0, SPAN), :] = conv_back(du, after, taps, masks_after).astype(BF16)
        after = du[:8]
        sums = [jnp.sum(du * lags[k] * masks[k], axis=0, keepdims=True) for k in range(CONV)]
        sums += [jnp.sum(du, axis=0, keepdims=True), jnp.zeros((3, WIDE), F32)]
        gp = gp + jnp.concatenate(sums, axis=0)

        q1h, q1l = split_low(dy * y)
        q2h, q2l = split_low(xf * dxu)
        q3h, q3l = split_low(xf * dy)
        row_term = dot_nt(pick, q1h) + dot_nt(pick, q1l)
        steps = dot_nt(pick, q2h) + dot_nt(pick, q2l) + dot_nt(pick_up, q3h) + dot_nt(pick_up, q3l)
        vh, vl = split_low(row_term - step_rows * jnp.where(row8 < GROUP, steps, 0.0))
        d_decay = dot_nn(vh, mask_scr[c]) + dot_nn(vl, mask_scr[c])
        row_local = lax.broadcasted_iota(jnp.int32, (8, SPAN), 1)
        row_since, row_until = doc_place(info, row_local + c * SPAN)
        if c < CHUNKS - 1:
            ph, plow = split_low(st[pl.ds((c + 1) * STATE, STATE), :].astype(F32) * adj)
            cross = jnp.sum(dot_nt(pick, ph) + dot_nt(pick, plow), axis=1, keepdims=True)
            d_decay = d_decay + jnp.where(row_until >= SPAN - 1 - row_local, cross, 0.0)
        d_decay = jnp.where(row_since > 0, d_decay, 0.0)
        hr_out[:, pl.ds(r0, SPAN)] = jnp.concatenate([steps, d_decay], axis=0)
    gp_out[...] = gp

    @pl.when(pl.program_id(0) == blocks - 1)
    def _():
        for c in range(CHUNKS):
            r0 = chunk_start(info, c, per_block)
            _, _, until = chunk_masks(info, c)
            gap = lax.broadcasted_iota(jnp.int32, (SPAN, SPAN), 1) - lax.broadcasted_iota(
                jnp.int32, (SPAN, SPAN), 0
            )
            pair_low = jnp.where((gap >= 0) & (gap <= wide2(until)), pair_scr[c], 0.0).astype(BF16)
            bcv = bc[pl.ds(r0, SPAN), :]
            dbc_out[pl.ds(r0, SPAN), :] += jnp.concatenate(
                [dot_nn(pair_low, bcv[:, STATE:]), dot_tn(pair_low, bcv[:, :STATE])], axis=1
            )


def pair_kernel(per_block, info, pairs, dbc_a, dbc_b, par, dp_out, gp_out):
    taps = [par[k : k + 1, :] for k in range(CONV)]
    after = jnp.zeros((8, WIDE), F32)
    gp = jnp.zeros((8, WIDE), F32)
    for c in reversed(range(CHUNKS)):
        r0 = chunk_start(info, c, per_block)
        _, since, until = chunk_masks(info, c)
        masks = [wide2((since >= k).astype(F32)) for k in range(CONV)]
        masks_after = [wide2((until >= k).astype(F32)) for k in range(CONV)]
        _, lags = conv_inputs(pairs, info, c, per_block, r0)
        u = conv_apply(lags, taps, par[4:5, :], masks)
        su = sigmoid(u)
        rows = pl.ds(r0, SPAN)
        du = (dbc_a[rows, :] + dbc_b[rows, :]) * (su * (1.0 + u * (1.0 - su)))
        dp_out[rows, :] = conv_back(du, after, taps, masks_after).astype(BF16)
        after = du[:8]
        sums = [jnp.sum(du * lags[k] * masks[k], axis=0, keepdims=True) for k in range(CONV)]
        sums += [jnp.sum(du, axis=0, keepdims=True), jnp.zeros((3, WIDE), F32)]
        gp = gp + jnp.concatenate(sums, axis=0)
    gp_out[...] = gp


def whole(shape):
    return pl.BlockSpec(shape, lambda i, info: (0,) * len(shape))


def cols(rows):
    return pl.BlockSpec((rows, WIDE), lambda i, info: (0, i))


def ignore(kernel, at, count):
    if not count:
        return kernel
    return lambda *refs: kernel(*refs[:at], *refs[at + count :])


def unread(later):
    return [pl.BlockSpec(memory_space=pl.ANY) for _ in later]


def call(kernel, grid, in_specs, out_specs, out_shape, scratch, us, info, *operands, later=()):
    kernel = ignore(kernel, 1 + len(operands), len(later))
    in_specs = [*in_specs, *unread(later)]
    operands = [*operands, *later]
    return pl.pallas_call(
        kernel,
        grid_spec=pltpu.PrefetchScalarGridSpec(
            num_scalar_prefetch=1,
            grid=(grid,),
            in_specs=in_specs,
            out_specs=out_specs,
            scratch_shapes=scratch,
        ),
        out_shape=out_shape,
        compiler_params=pltpu.CompilerParams(vmem_limit_bytes=VMEM_LIMIT),
        cost_estimate=lasting(us),
    )(info, *operands)


def shape(dims, kind):
    return jax.ShapeDtypeStruct(dims, kind)


def project(a, b, kind, later):
    rows, depth = a.shape
    b, number = b if isinstance(b, tuple) else (b, 0)
    columns = b.shape[-1]
    wide = min(columns, 512)
    block = pl.BlockSpec((depth, wide), lambda j: (0, j))
    if b.ndim == 4:
        block = pl.BlockSpec((b.shape[0], 1, b.shape[2], wide), lambda j: (0, number, 0, j))

    def kernel(x, w, out):
        out[...] = dot_nn(x[...], w[...].reshape(depth, wide)).astype(kind)

    return pl.pallas_call(
        ignore(kernel, 2, len(later)),
        grid=(columns // wide,),
        in_specs=[
            pl.BlockSpec((rows, depth), lambda j: (0, 0)),
            block,
            *unread(later),
        ],
        out_specs=pl.BlockSpec((rows, wide), lambda j: (0, j)),
        out_shape=shape((rows, columns), kind),
        compiler_params=pltpu.CompilerParams(vmem_limit_bytes=VMEM_LIMIT),
        cost_estimate=lasting(6),
    )(a, b, *later)


def project_few(a, b, later):
    rows, depth = a.shape
    columns = b.shape[1]

    def kernel(x, w, out):
        out[...] = dot_nn(x[...], w[...])

    return pl.pallas_call(
        ignore(kernel, 2, len(later)),
        grid=(rows // 256,),
        in_specs=[
            pl.BlockSpec((256, depth), lambda i: (i, 0)),
            pl.BlockSpec((depth, columns), lambda i: (0, 0)),
            *unread(later),
        ],
        out_specs=pl.BlockSpec((256, columns), lambda i: (i, 0)),
        out_shape=shape((rows, columns), F32),
        compiler_params=pltpu.CompilerParams(vmem_limit_bytes=VMEM_LIMIT),
        cost_estimate=lasting(3),
    )(a, b, *later)


def project_back(up, w, yg, later):
    rows, depth = up.shape
    columns = w.shape[0]
    wide = min(columns, 512)

    def kernel(x, b, y, out, sums):
        value = dot_nt(x[...], b[...])
        out[...] = value.astype(BF16)
        value = value * y[...].astype(F32)
        total = value[:, :128]
        for k in range(1, wide // 128):
            total = total + value[:, k * 128 : (k + 1) * 128]

        @pl.when(pl.program_id(0) == 0)
        def _():
            sums[...] = total

        @pl.when(pl.program_id(0) > 0)
        def _():
            sums[...] += total

    return pl.pallas_call(
        ignore(kernel, 3, len(later)),
        grid=(columns // wide,),
        in_specs=[
            pl.BlockSpec((rows, depth), lambda j: (0, 0)),
            pl.BlockSpec((wide, depth), lambda j: (j, 0)),
            pl.BlockSpec((rows, wide), lambda j: (0, j)),
            *unread(later),
        ],
        out_specs=[pl.BlockSpec((rows, wide), lambda j: (0, j)), pl.BlockSpec((rows, 128), lambda j: (0, 0))],
        out_shape=[shape((rows, columns), BF16), shape((rows, 128), F32)],
        compiler_params=pltpu.CompilerParams(vmem_limit_bytes=VMEM_LIMIT),
        cost_estimate=lasting(8),
    )(up, w, yg, *later)


def rows_forward(lefts, rights, first, rows, later=()):
    columns = rights[0].shape[1]
    wide = 512
    count = len(lefts)
    start = first // rows

    def kernel(*refs):
        total = dot_nn(refs[0][...], refs[count][...])
        for n in range(1, count):
            total = total + dot_nn(refs[n][...], refs[count + n][...])
        refs[-1][...] = total.astype(BF16)

    return pl.pallas_call(
        ignore(kernel, 2 * count, len(later)),
        grid=(columns // wide,),
        in_specs=[pl.BlockSpec((rows, v.shape[1]), lambda j: (start, 0)) for v in lefts]
        + [pl.BlockSpec((v.shape[0], wide), lambda j: (0, j)) for v in rights]
        + unread(later),
        out_specs=pl.BlockSpec((rows, wide), lambda j: (0, j)),
        out_shape=shape((rows, columns), BF16),
        compiler_params=pltpu.CompilerParams(vmem_limit_bytes=VMEM_LIMIT),
        cost_estimate=lasting(5),
    )(*lefts, *rights, *later)


def delayed(v, later):
    flat = v.reshape(-1, v.shape[-1])
    rows, width = flat.shape
    block = rows // 2 if rows % 32 == 0 else rows

    def kernel(a, out):
        out[...] = a[...]

    return pl.pallas_call(
        ignore(kernel, 1, len(later)),
        grid=(rows // block,),
        in_specs=[pl.BlockSpec((block, width), lambda i: (i, 0)), *unread(later)],
        out_specs=pl.BlockSpec((block, width), lambda i: (i, 0)),
        out_shape=shape((rows, width), v.dtype),
        compiler_params=pltpu.CompilerParams(vmem_limit_bytes=VMEM_LIMIT),
        cost_estimate=lasting(2),
    )(flat, *later).reshape(v.shape)


def added(a, b, later):
    def kernel(x, y, out):
        out[...] = (x[...].astype(F32) + y[...].astype(F32)).astype(BF16)

    return pl.pallas_call(
        ignore(kernel, 2, len(later)),
        in_specs=[pl.BlockSpec(memory_space=pltpu.VMEM)] * 2 + unread(later),
        out_specs=pl.BlockSpec(memory_space=pltpu.VMEM),
        out_shape=shape(a.shape, BF16),
        compiler_params=pltpu.CompilerParams(vmem_limit_bytes=VMEM_LIMIT),
        cost_estimate=lasting(1),
    )(a, b, *later)


def norm_rows(own, got, gain, later):
    rows, width = own.shape
    block = min(rows, 256)
    here = rows // block

    def kernel(a, b, gain_row, out):
        def write(v):
            v = v.astype(F32)
            inverse = lax.rsqrt(jnp.mean(v * v, axis=1, keepdims=True) + EPSILON)
            out[...] = (v * inverse * gain_row[...]).astype(BF16)

        @pl.when(pl.program_id(0) < here)
        def _():
            write(a[...])

        @pl.when(pl.program_id(0) >= here)
        def _():
            write(b[...])

    return pl.pallas_call(
        ignore(kernel, 3, len(later)),
        grid=(SEQ_LEN // block,),
        in_specs=[
            pl.BlockSpec((block, width), lambda i: (jnp.minimum(i, here - 1), 0)),
            pl.BlockSpec((block, width), lambda i: (jnp.maximum(i - here, 0), 0)),
            pl.BlockSpec((1, width), lambda i: (0, 0)),
            *unread(later),
        ],
        out_specs=pl.BlockSpec((block, width), lambda i: (i, 0)),
        out_shape=shape((SEQ_LEN, width), BF16),
        compiler_params=pltpu.CompilerParams(vmem_limit_bytes=VMEM_LIMIT),
        cost_estimate=lasting(4),
    )(own, got, gain[None], *later)


def prep(per_block, info, pairs, par):
    t = SEQ_LEN
    return call(
        functools.partial(prep_kernel, per_block),
        1,
        [whole((t, WIDE)), whole((8, WIDE))],
        [whole((t, WIDE)), whole((WIDE, t))],
        [shape((t, WIDE), BF16), shape((WIDE, t), BF16)],
        [],
        2,
        info,
        pairs,
        par,
    )


def scan_forward(per_block, info, inner, gate, bc, bct, hs, par, later):
    t, channels = inner.shape
    blocks = channels // WIDE
    return call(
        functools.partial(fwd_kernel, per_block),
        blocks,
        [
            cols(t),
            cols(t),
            whole((t, WIDE)),
            whole((WIDE, t)),
            pl.BlockSpec((16, t), lambda i, info: (i, 0)),
            cols(8),
        ],
        [cols(t), cols(t), cols(t), cols(CHUNKS * STATE), whole((t, 128))],
        [
            shape((t, channels), BF16),
            shape((t, channels), BF16),
            shape((t, channels), BF16),
            shape((CHUNKS * STATE, channels), BF16),
            shape((t, 128), F32),
        ],
        [pltpu.VMEM((CHUNKS, SPAN, SPAN), F32), pltpu.VMEM((STATE, WIDE), F32)],
        20,
        info,
        inner,
        gate,
        bc,
        bct,
        hs,
        par,
        later=later,
    )


def scan_backward(per_block, info, inner, y, dy, bc, bct, hs, st, par, later):
    t, channels = inner.shape
    blocks = channels // WIDE
    return call(
        functools.partial(bwd_kernel, per_block, blocks),
        blocks,
        [
            cols(t),
            cols(t),
            cols(t),
            whole((t, WIDE)),
            whole((WIDE, t)),
            pl.BlockSpec((16, t), lambda i, info: (i, 0)),
            cols(CHUNKS * STATE),
            cols(8),
        ],
        [
            cols(t),
            whole((t, WIDE)),
            cols(8),
            pl.BlockSpec((16, t), lambda i, info: (i, 0)),
        ],
        [
            shape((t, channels), BF16),
            shape((t, WIDE), F32),
            shape((8, channels), F32),
            shape((blocks * 16, t), F32),
        ],
        [
            pltpu.VMEM((CHUNKS, SPAN, SPAN), F32),
            pltpu.VMEM((CHUNKS, SPAN, SPAN), F32),
            pltpu.VMEM((CHUNKS, SPAN, SPAN), BF16),
            pltpu.VMEM((STATE, WIDE), F32),
        ],
        36,
        info,
        inner,
        y,
        dy,
        bc,
        bct,
        hs,
        st,
        par,
        later=later,
    )


def gate_backward(mk, gate, dn, sk, par, later):
    t, channels = gate.shape
    block = pl.BlockSpec((t, WIDE), lambda i: (0, i))
    small = pl.BlockSpec((8, WIDE), lambda i: (0, i))
    return pl.pallas_call(
        ignore(gate_kernel, 5, len(later)),
        grid=(channels // WIDE,),
        in_specs=[block, block, block, pl.BlockSpec((8, t), lambda i: (0, 0)), small, *unread(later)],
        out_specs=[block, block, small],
        out_shape=[shape((t, channels), BF16)] * 2 + [shape((8, channels), F32)],
        compiler_params=pltpu.CompilerParams(vmem_limit_bytes=VMEM_LIMIT),
        cost_estimate=lasting(8),
    )(mk, gate, dn, sk, par, *later)


def turned(number, bits):
    return sum(((number >> k) & 1) << (bits - 1 - k) for k in range(bits))


def grad_half(lefts, rights, half, more=None, scale=None, later=(), pieces=1, bits=0):
    t, width = lefts[0].shape
    columns = rights[0].shape[1]
    count = max(len(lefts), len(rights))
    tall = width // 2 // pieces
    high, wide = min(width // 2, 256 if bits else 512), min(columns, 1024)
    down, along = width // 2 // high, columns // wide
    group = max(high // tall, 1)
    split = max(tall // high, 1)
    if bits and group > 1:
        high, group = tall, 1
        high = max(high, 128)
        group = high // tall
        down = width // 2 // high
    resident = bits > 0 and group > 1
    if resident:
        block = pl.BlockSpec((pieces, count, tall, wide), lambda j, i, info: (0, 0, 0, j))
    else:
        block = pl.BlockSpec(
            (group, count, tall // split, wide),
            lambda j, i, info: (turned(i // split, bits) if bits else i // split, 0, i % split, j),
        )
    operands = [*lefts, *rights] + ([] if more is None else [more]) + ([] if scale is None else [scale])

    def kernel(info, *refs):
        out = refs[-1]
        for n in range(count):
            left = refs[n % len(lefts)][...]
            if scale is not None:
                left = (left.astype(F32) * refs[-2][...].T[:, 0:1]).astype(BF16)
            total = dot_tn(left, refs[len(lefts) + n % len(rights)][...])
            for g in range(group):
                rows = total if group == 1 else total[g * tall : (g + 1) * tall]
                at = turned(pl.program_id(1) * group + g, bits) if resident else g
                if more is not None:
                    rows = rows + refs[len(lefts) + len(rights)][at, n].astype(F32)
                out[at, n] = rows.astype(BF16)

    return pl.pallas_call(
        ignore(kernel, 1 + len(operands), len(later)),
        grid_spec=pltpu.PrefetchScalarGridSpec(
            num_scalar_prefetch=1,
            grid=(along, down),
            in_specs=[pl.BlockSpec((t, high), lambda j, i, info: (0, info[0] * down + i)) for _ in lefts]
            + [pl.BlockSpec((t, wide), lambda j, i, info: (0, j)) for _ in rights]
            + ([] if more is None else [block])
            + ([] if scale is None else [pl.BlockSpec((8, t), lambda j, i, info: (0, 0))])
            + unread(later),
            out_specs=block,
        ),
        out_shape=shape((pieces, count, tall, columns), BF16),
        compiler_params=pltpu.CompilerParams(vmem_limit_bytes=VMEM_LIMIT),
        cost_estimate=lasting(7),
    )(half[None], *operands, *later)


def grad_pieces(left, right, shared, batches, bits, later=()):
    t, width = left.shape
    columns = right.shape[1]
    chips = batches // 2
    tall = width // batches // 2
    high = 256
    group = high // tall

    extra = 0 if shared is None else shared.shape[1]

    def kernel(a, b, *refs):
        out = refs[-1]
        total = dot_tn(a[...], b[...]).astype(BF16)
        for g in range(group):
            block = pl.program_id(0) * group + g
            core, quarter, number = block // (2 * chips), (block // chips) % 2, block % chips
            chip = jnp.where(quarter == 0, number, turned(number, bits))
            rows = pl.ds(pl.multiple_of(quarter * tall, tall), tall)
            out[chip * 2 + core, rows, :] = total[g * tall : (g + 1) * tall]

        if extra:

            @pl.when(pl.program_id(0) == width // high - 1)
            def _():
                out[:, 2 * tall :, :] = refs[0][...]

    return pl.pallas_call(
        ignore(kernel, 3 if extra else 2, len(later)),
        grid=(width // high,),
        in_specs=[
            pl.BlockSpec((t, high), lambda i: (0, i)),
            pl.BlockSpec((t, columns), lambda i: (0, 0)),
        ]
        + ([pl.BlockSpec(shared.shape, lambda i: (0, 0, 0))] if extra else [])
        + unread(later),
        out_specs=pl.BlockSpec((batches, 2 * tall + extra, columns), lambda i: (0, 0, 0)),
        out_shape=shape((batches, 2 * tall + extra, columns), BF16),
        compiler_params=pltpu.CompilerParams(vmem_limit_bytes=VMEM_LIMIT),
        cost_estimate=lasting(10),
    )(left, right, *([shared] if extra else []), *later)


def place_pieces(v, tall, bits, later):
    batches, _, columns = v.shape
    chips = batches // 2

    half = chips * tall
    wide = columns // 4

    def kernel(a, out):
        for core in range(2):
            for chip in range(chips):
                v = a[chip * 2 + core]
                for quarter, number in ((0, chip), (1, turned(chip, bits))):
                    at = (core * 2 + quarter) * half + number * tall
                    out[at : at + tall, :] = v[quarter * tall : (quarter + 1) * tall].astype(F32)

    return pl.pallas_call(
        ignore(kernel, 1, len(later)),
        grid=(4,),
        in_specs=[pl.BlockSpec((batches, 2 * tall, wide), lambda i: (0, 0, i)), *unread(later)],
        out_specs=pl.BlockSpec((4 * half, wide), lambda i: (0, i)),
        out_shape=shape((4 * half, columns), F32),
        compiler_params=pltpu.CompilerParams(vmem_limit_bytes=VMEM_LIMIT),
        cost_estimate=lasting(7),
    )(v, *later)


def place_halves(mine, other, core):
    rows, columns = mine.shape
    high = min(rows, 256)
    per = rows // high

    def kernel(info, a, b, out):
        here = pl.program_id(0) // per == info[0]

        @pl.when(here)
        def _():
            out[...] = a[...].astype(F32)

        @pl.when(jnp.logical_not(here))
        def _():
            out[...] = b[...].astype(F32)

    return pl.pallas_call(
        kernel,
        grid_spec=pltpu.PrefetchScalarGridSpec(
            num_scalar_prefetch=1,
            grid=(2 * per,),
            in_specs=[
                pl.BlockSpec((high, columns), lambda i, info: (jnp.clip(i - info[0] * per, 0, per - 1), 0)),
                pl.BlockSpec((high, columns), lambda i, info: (jnp.clip(i - (1 - info[0]) * per, 0, per - 1), 0)),
            ],
            out_specs=pl.BlockSpec((high, columns), lambda i, info: (i, 0)),
        ),
        out_shape=shape((2 * rows, columns), F32),
        compiler_params=pltpu.CompilerParams(vmem_limit_bytes=VMEM_LIMIT),
        cost_estimate=lasting(6),
    )(core[None], mine, other)


def small_grads(left, right, later):
    t, columns = right.shape
    wide = 512

    def kernel(a, b, out):
        out[...] = dot_tn(a[...], b[...])

    return pl.pallas_call(
        ignore(kernel, 2, len(later)),
        grid=(columns // wide,),
        in_specs=[
            pl.BlockSpec(left.shape, lambda j: (0, 0)),
            pl.BlockSpec((t, wide), lambda j: (0, j)),
            *unread(later),
        ],
        out_specs=pl.BlockSpec((left.shape[1], wide), lambda j: (0, j)),
        out_shape=shape((left.shape[1], columns), F32),
        compiler_params=pltpu.CompilerParams(vmem_limit_bytes=VMEM_LIMIT),
        cost_estimate=lasting(4),
    )(left, right, *later)


def rows_back(lefts, rights, first, rows, gain_rows, later=()):
    columns = rights[0].shape[0]
    wide = 512

    def right_block(v):
        if not isinstance(v, tuple):
            return pl.BlockSpec((wide, v.shape[1]), lambda j: (j, 0))
        v, number = v
        return pl.BlockSpec((wide // v.shape[2], 1, v.shape[2], v.shape[3]), lambda j: (j, number, 0, 0))

    count = len(lefts)
    start = first // rows

    def kernel(*refs):
        total = dot_nt(refs[0][...], refs[count][...].reshape(wide, -1))
        for n in range(1, count):
            total = total + dot_nt(refs[n][...], refs[count + n][...].reshape(wide, -1))
        unit, out, sums = refs[-3:]
        out[...] = total.astype(BF16)
        sums[...] = jnp.sum(total * unit[...].astype(F32), axis=0, keepdims=True) + jnp.zeros((8, wide), F32)

    return pl.pallas_call(
        ignore(kernel, 2 * count + 1, len(later)),
        grid=(columns // wide,),
        in_specs=[pl.BlockSpec((rows, v.shape[1]), lambda j: (start, 0)) for v in lefts]
        + [right_block(v) for v in rights]
        + [pl.BlockSpec((rows, wide), lambda j: (start, j))]
        + unread(later),
        out_specs=[pl.BlockSpec((rows, wide), lambda j: (0, j)), pl.BlockSpec((8, wide), lambda j: (0, j))],
        out_shape=[shape((rows, columns), BF16), shape((8, columns), F32)],
        compiler_params=pltpu.CompilerParams(vmem_limit_bytes=VMEM_LIMIT),
        cost_estimate=lasting(15),
    )(*lefts, *[v[0] if isinstance(v, tuple) else v for v in rights], gain_rows, *later)


def pair_backward(per_block, info, pairs, dbc_a, dbc_b, par):
    t = SEQ_LEN
    return call(
        functools.partial(pair_kernel, per_block),
        1,
        [whole((t, WIDE)), whole((t, WIDE)), whole((t, WIDE)), whole((8, WIDE))],
        [whole((t, WIDE)), whole((8, WIDE))],
        [shape((t, WIDE), BF16), shape((8, WIDE), F32)],
        [],
        4,
        info,
        pairs,
        dbc_a,
        dbc_b,
        par,
    )


def body(
    axis_sizes,
    hidden_in,
    out_grad,
    norm_gain,
    w_z,
    w_x,
    w_dt,
    w_bc,
    conv_x,
    conv_x_bias,
    conv_bc,
    conv_bc_bias,
    dt_bias,
    a_log,
    d_skip,
    gate_gain,
    w_out,
    doc_lengths,
    widths,
):
    batches, stacks = axis_sizes
    rows, width_in = hidden_in.shape
    heads_here = dt_bias.shape[0]
    channels = w_x.shape[1]
    members = stacks // widths.shape[0]
    far_bit = members
    per_block = rows // SPAN
    place = lax.axis_index("head")
    lot = lax.axis_index("batch")
    own_seq = place // members
    ends = jnp.cumsum(lax.dynamic_index_in_dim(doc_lengths, own_seq, 0, keepdims=False))
    width = lax.dynamic_index_in_dim(widths, own_seq, 0, keepdims=False)
    info = jnp.concatenate([ends.astype(jnp.int32), (place % members).astype(jnp.int32)[None]])

    def across(v, bit):
        return lax.ppermute(v, "head", [(i, i ^ bit) for i in range(stacks)])

    def sum_rows(v):
        bit = 1
        while bit < members:
            got = across(v, bit)
            flipped = got.reshape(v.shape[0], -1, 2, bit * rows)[:, :, ::-1, :].reshape(v.shape)
            v = v + flipped
            bit *= 2
        return v

    chip_bits = []
    bit = 2
    while bit < batches:
        chip_bits.append(bit)
        bit *= 2
    chips = batches // 2
    core = lot % 2
    chip_groups = [[2 * i + c for i in range(chips)] for c in range(2)]
    orders = (chip_bits, chip_bits[::-1])

    def planar(v, bit):
        return lax.ppermute(v, "batch", [(i, i ^ bit) for i in range(batches)])

    def side(bit):
        return (lot // bit) % 2

    def join(v, got, bit, axis=0):
        low, high = jnp.concatenate([v, got], axis=axis), jnp.concatenate([got, v], axis=axis)
        return jnp.where(side(bit) == 0, low, high)

    def add(a, b):
        return (a.astype(F32) + b.astype(F32)).astype(BF16)

    def nothing(v):
        return (v[(0,) * v.ndim].astype(F32) * 0.0).astype(jnp.int32)

    def others(v):
        got, bit = across(v, 1), 2
        while bit < members:
            got = jnp.concatenate([got, across(jnp.concatenate([v, got], axis=0), bit)], axis=0)
            bit *= 2
        return got

    hidden_got = others(hidden_in)
    piece = width_in // batches
    far_parts = across(
        jnp.concatenate([lax.dynamic_slice_in_dim(w, lot * piece, piece, 0) for w in (w_x, w_z)], axis=0), far_bit
    )
    w_dt_own = w_dt.T
    w_dt_far = across(w_dt_own, far_bit)
    head_row = jnp.concatenate([dt_bias, a_log])
    par_own = jnp.concatenate(
        [
            conv_x,
            conv_x_bias[None],
            jnp.repeat(d_skip, HEAD_DIM)[None],
            gate_gain[None],
            jnp.pad(head_row, (0, channels - head_row.shape[0]))[None],
        ],
        axis=0,
    )
    par_far = across(par_own, far_bit)
    up_sent = delayed(out_grad, (hidden_got,))
    normed = norm_rows(hidden_in, hidden_got, norm_gain, (far_parts, w_dt_far, par_far, up_sent))
    far_parts = delayed(far_parts, (hidden_got, w_dt_far, par_far))
    far_parts = delayed(far_parts, (hidden_got, w_dt_far, par_far))
    far_both = lax.all_gather(far_parts, "batch", axis=0, tiled=True).reshape(batches, 2, piece, channels)
    out_piece = channels // batches
    w_out_part = across(
        lax.dynamic_slice_in_dim(w_out, lot * out_piece + nothing(normed), out_piece, 0), far_bit
    )
    up_got = others(up_sent)
    upstream = jnp.concatenate([out_grad, up_got], axis=0)
    active = (jnp.arange(channels) // HEAD_DIM < width * heads_here // (heads_here * stacks)).astype(F32)
    rate_par = [(v[7, :heads_here], v[7, heads_here : 2 * heads_here]) for v in (par_own, par_far)]
    par2 = [jnp.concatenate([v[:7], active[None]], axis=0) for v in (par_own, par_far)]
    step_bias = jnp.concatenate([rate_par[0][0], rate_par[1][0]])[:, None]
    speed = jnp.exp(jnp.concatenate([rate_par[0][1], rate_par[1][1]]))[:, None]
    par_bc = jnp.concatenate([conv_bc, conv_bc_bias[None], jnp.zeros((3, 2 * STATE), F32)], axis=0)

    w_small = jnp.concatenate([w_bc, w_dt_own.T, w_dt_far.T], axis=1)
    small_cols = project_few(normed, w_small, ())
    pairs = small_cols[:, : 2 * STATE]
    rates = small_cols[:, 2 * STATE :].T
    step = jax.nn.softplus(rates + step_bias)
    decay = -step * speed
    upper = (jnp.arange(SPAN)[:, None] <= jnp.arange(SPAN)[None, :]).astype(F32)
    cum = lax.dot_general(
        decay.reshape(-1, SPAN), upper, (((1,), (0,)), ((), ())), precision=lax.Precision.HIGHEST
    ).reshape(decay.shape)

    def grouped(v):
        v = v.reshape(-1, GROUP, SEQ_LEN)
        return jnp.pad(v, ((0, 0), (0, 8 - GROUP), (0, 0)))

    hs = jnp.concatenate([grouped(cum), grouped(step)], axis=1).reshape(-1, SEQ_LEN)
    half = hs.shape[0] // 2
    hs2 = (hs[:half], hs[half:])
    bc, bct = prep(per_block, info, pairs, par_bc)

    inner_own = project(normed, w_x, BF16, (bc,))
    gate_own = project(normed, w_z, BF16, (inner_own,))
    forward_own = scan_forward(per_block, info, inner_own, gate_own, bc, bct, hs2[0], par2[0], (up_got,))
    dn_own = project_back(upstream, w_out, forward_own[2], ())
    w_x_far, w_z_far = (far_both, 0), (far_both, 1)
    w_out_far = lax.all_gather(delayed(w_out_part, (forward_own[0],)), "batch", axis=0, tiled=True)
    w_x2 = (w_x, w_x_far)
    w_z2 = (w_z, w_z_far)
    w_out2 = (w_out, w_out_far)
    inner2 = (inner_own, project(normed, w_x_far, BF16, (dn_own[0],)))
    gate2 = (gate_own, project(normed, w_z_far, BF16, (inner2[1],)))
    forward = (forward_own, scan_forward(per_block, info, inner2[1], gate2[1], bc, bct, hs2[1], par2[1], ()))
    y2, mk2, yg2, st2 = [[f[k] for f in forward] for k in range(4)]
    dn_far = project_back(upstream, w_out_far, yg2[1], ())
    dn2 = (dn_own[0], dn_far[0])

    def branch_rows(first, count):
        return rows_forward(yg2, w_out2, first, count, (dn_far[0],) if first else (give_out,))

    def scatter_rows(make):
        if members == 2:
            give = make(rows, rows)
            got = across(give, 1)
            return give, got, lambda: make(0, rows).astype(F32) + got.astype(F32)
        v = make(0, SEQ_LEN)
        bit = members // 2
        while bit >= 1:
            half = v.shape[0] // 2
            v = add(v[:half], across(v[half:], bit))
            bit //= 2
        return v, v, lambda: v.astype(F32)

    give_out = dn_far[0]
    branch_given, branch_got, branch = scatter_rows(branch_rows)
    square = jnp.sum(forward[0][4] + forward[1][4], axis=1)
    sums = sum_rows(jnp.stack([square, jnp.sum(dn_own[1] + dn_far[1], axis=1)]))
    count = (width * HEAD_DIM).astype(F32)
    scale = lax.rsqrt(sums[0] / count + EPSILON)
    fix = scale * scale * scale * sums[1] / count
    sk = jnp.concatenate([scale[None], fix[None], jnp.zeros((6, SEQ_LEN), F32)], axis=0)

    bits = len(chip_bits)

    def swap_halves(lefts, rights, scale=None, later=(), pieces=1, bits=0):
        give = grad_half(lefts, rights, 1 - core, None, scale, later, pieces, bits)
        got = planar(give, 1)
        return give, lambda later=(): grad_half(lefts, rights, core, got, scale, later, pieces, bits)

    def scatter_offloaded(mine):
        flat = mine.reshape(-1, mine.shape[-1])
        part = lax.psum_scatter(flat, "batch", scatter_dimension=0, tiled=True, axis_index_groups=chip_groups)
        return part.reshape(mine.shape[1:])

    def send_far(part, earlier):
        far = lax.dynamic_slice_in_dim(part, 1 + jnp.minimum(nothing(earlier), 0), 1, 0)[0]
        return across(far, far_bit)

    def gather_both(parts, seen):
        for step in range(bits):
            got = [planar(v, order[step]) for v, order in zip(parts, orders)]
            parts = [join(v, g, order[step]) for v, g, order in zip(parts, got, orders)]
            seen.append(parts)
        return parts, [planar(v, 1) for v in parts]

    give_out, keep_out = swap_halves(yg2, [upstream], sk, (branch_given,), pieces=chips)
    gates = [gate_backward(mk2[i], gate2[i], dn2[i], sk, par2[i], (give_out,)) for i in range(2)]
    d_gate2 = [v[0] for v in gates]
    mine_out = keep_out(later=(d_gate2[0],))
    part_out = scatter_offloaded(mine_out)
    give_z, keep_z = swap_halves([normed], d_gate2, later=(mine_out,), pieces=chips, bits=bits)
    give_out = give_z
    branch_sum = branch()
    mixed = (hidden_in.astype(F32) + branch_sum * scale[:rows, None]).astype(BF16)
    mine_z = keep_z(later=(give_z,))
    part_z = scatter_offloaded(mine_z)

    def scan_back(i, later):
        return scan_backward(per_block, info, inner2[i], y2[i], gates[i][1], bc, bct, hs2[i], st2[i], par2[i], later)

    back = [None, None]
    back[1] = scan_back(1, (mine_z,))
    far_cut = grad_pieces(normed, back[1][0], None, batches, bits)
    far_piece = lax.psum_scatter(far_cut.reshape(-1, channels), "batch", scatter_dimension=0, tiled=True)
    far_out = send_far(part_out, back[1][0])
    back[0] = scan_back(0, (far_cut,))
    total_out = added(part_out[0], far_out, (back[0][0],))
    d_pairs, g_bc = pair_backward(per_block, info, pairs, back[0][1], back[1][1], par_bc)
    heads_out = [b[3].reshape(-1, 16, SEQ_LEN) for b in back]
    d_step = jnp.concatenate([h[:, :GROUP].reshape(-1, SEQ_LEN) for h in heads_out], axis=0)
    skip_rows = jnp.concatenate([h[:, GROUP : 2 * GROUP].reshape(-1, SEQ_LEN) for h in heads_out], axis=0)
    d_decay = jnp.concatenate([h[:, 8 : 8 + GROUP].reshape(-1, SEQ_LEN) for h in heads_out], axis=0)
    d_rates_pre = (d_step - d_decay * speed) * jax.nn.sigmoid(rates + step_bias)
    head_grads = jnp.stack(
        [jnp.sum(d_rates_pre, axis=1), jnp.sum(d_decay * decay, axis=1), jnp.sum(skip_rows, axis=1)]
    )
    d_rates = d_rates_pre.astype(BF16)
    d_small = jnp.concatenate([d_pairs, d_rates.T], axis=1)

    g_small = small_grads(d_small, normed, (part_z, total_out, branch_got))

    def pack(i):
        gp = back[i][2]
        heads = head_grads[:, i * heads_here : (i + 1) * heads_here].reshape(-1)
        heads = jnp.pad(heads, (0, channels - heads.shape[0]))[None]
        start = 2 * STATE + i * heads_here
        return jnp.concatenate(
            [gp[:5], heads, gates[i][2][:1], gp[7:], g_small[start : start + heads_here].reshape(-1, channels)], axis=0
        )

    def spread(v):
        v = jnp.pad(v.astype(BF16), ((0, -v.shape[0] % (16 * batches)), (0, 0)))
        return v.reshape(batches, -1, channels)

    far_z = send_far(part_z, g_small)
    norm_sums = []

    def normed_rows(first, count):
        part, total = rows_back(
            [*d_gate2, back[0][0], back[1][0], d_small],
            [*w_z2, *w_x2, w_small],
            first,
            count,
            normed,
            (norm_sums[0],) if norm_sums else (g_small,),
        )
        norm_sums.append(total)
        return part

    _, d_normed_got, d_normed_in = scatter_rows(normed_rows)
    d_normed_in = d_normed_in()
    bc_rows, few_rows = 2 * STATE * width_in // channels, 8 * 2 * STATE // channels
    shared = spread(jnp.concatenate([g_small[: 2 * STATE].reshape(-1, channels), g_bc.reshape(-1, channels), sum(norm_sums)[:1].reshape(-1, channels)], axis=0))
    private = spread(pack(0) + delayed(across(pack(1), far_bit), (norm_sums[-1],)))
    own_cut = grad_pieces(normed, back[0][0], jnp.concatenate([shared, private], axis=1), batches, bits, (d_normed_got,))
    own_part = lax.psum_scatter(own_cut.reshape(-1, channels), "batch", scatter_dimension=0, tiled=True)
    seen = []
    total_z = added(part_z[0], far_z, (norm_sums[-1],))
    total_out = delayed(total_out, (total_z,))
    halves_here, halves_there = gather_both([total_out, total_z], seen)
    own_part = delayed(own_part, halves_here)

    cut = 2 * (width_in // batches // 2)
    far_sent = across(delayed(far_piece, seen[0]), far_bit)
    bc_piece = own_part[cut : cut + shared.shape[1]]
    bit = 1
    while bit < stacks:
        bc_piece = add(bc_piece, across(bc_piece, bit))
        bit *= 2
    own_total = jnp.concatenate(
        [add(own_part[:cut], far_sent), bc_piece, own_part[cut + shared.shape[1] :]], axis=0
    )
    everything = lax.all_gather(own_total, "batch", axis=0, tiled=True).reshape(batches, -1, channels)
    g_w_out, g_w_z = [place_halves(v, got, core) for v, got in zip(halves_here, halves_there)]
    common = everything[:, cut : cut + shared.shape[1]].reshape(-1, channels).astype(F32)
    packed = everything[:, cut + shared.shape[1] :].reshape(-1, channels).astype(F32)
    g_w_bc = common[:bc_rows].reshape(2 * STATE, width_in).T
    g_bc_total = common[bc_rows : bc_rows + few_rows].reshape(8, -1)
    heads_total = packed[5]
    g_w_dt = packed[8 : 8 + heads_here * width_in // channels].reshape(heads_here, width_in).T
    g_norm = common[bc_rows + few_rows : bc_rows + few_rows + width_in // channels].reshape(-1) / norm_gain

    residual = hidden_in.astype(F32)
    inverse = lax.rsqrt(jnp.mean(residual * residual, axis=-1, keepdims=True) + EPSILON)
    unit_rows = residual * inverse
    d_unit = d_normed_in * norm_gain
    d_residual = inverse * (d_unit - unit_rows * jnp.mean(d_unit * unit_rows, axis=-1, keepdims=True))
    in_grad = (out_grad.astype(F32) + d_residual).astype(BF16)
    g_w_x = place_pieces(everything, cut // 2, bits, (g_w_out, g_w_z, in_grad))
    return (
        mixed,
        in_grad,
        g_norm,
        g_w_z,
        g_w_x,
        g_w_dt,
        g_w_bc,
        packed[:4],
        packed[4],
        g_bc_total[:4],
        g_bc_total[4],
        heads_total[:heads_here],
        heads_total[heads_here : 2 * heads_here],
        heads_total[2 * heads_here : 3 * heads_here],
        packed[6],
        g_w_out,
    )


def solution(mesh):
    split = P(("batch", "head"), None)
    by_col, by_head, by_row = P(None, "head"), P("head"), P("head", None)
    return jax.shard_map(
        functools.partial(body, (mesh.shape["batch"], mesh.shape["head"])),
        mesh=mesh,
        in_specs=(
            split,
            split,
            P(),
            by_col,
            by_col,
            by_col,
            P(),
            by_col,
            by_head,
            P(),
            P(),
            by_head,
            by_head,
            by_head,
            by_head,
            by_row,
            P("batch", None),
            P("batch"),
        ),
        out_specs=(
            split,
            split,
            P(),
            by_col,
            by_col,
            by_col,
            P(),
            by_col,
            by_head,
            P(),
            P(),
            by_head,
            by_head,
            by_head,
            by_head,
            by_row,
        ),
        check_vma=False,
    )
```

```python
import functools

import jax
import jax.numpy as jnp
from jax import lax
from jax.experimental import pallas as pl
from jax.experimental.pallas import tpu as pltpu
from jax.sharding import PartitionSpec as P

HEAD_DIM = 64
STATE = 128
CONV = 4
SPAN = 256
SEQ_LEN = 1024
DOCS = 4
CHUNKS = SEQ_LEN // SPAN
WIDE = 256
GROUP = WIDE // HEAD_DIM
STRIP = 128
BELOW = [(k * STRIP, -(-(k + 1) * STRIP // 128) * 128) for k in range(SPAN // STRIP)]
ABOVE = [(k * STRIP, k * STRIP // 128 * 128) for k in range(SPAN // STRIP)]
EPSILON = 1e-05
F32 = jnp.float32
BF16 = jnp.bfloat16
VMEM_LIMIT = 48 * 1024 * 1024


PACE = 0.01e9


def lasting(us):
    return pl.CostEstimate(flops=int(us * PACE), bytes_accessed=1000, transcendentals=0)


def dot_nn(a, b):
    return lax.dot_general(a, b, (((1,), (0,)), ((), ())), preferred_element_type=F32)


def dot_nt(a, b):
    return lax.dot_general(a, b, (((1,), (1,)), ((), ())), preferred_element_type=F32)


def dot_tn(a, b):
    return lax.dot_general(a, b, (((0,), (0,)), ((), ())), preferred_element_type=F32)


def sigmoid(v):
    return 0.5 * (1.0 + jnp.tanh(0.5 * v))


def chunk_start(info, c, per_block):
    block = (c // per_block) ^ info[DOCS]
    return pl.multiple_of((block * per_block + c % per_block) * SPAN, SPAN)


def doc_place(info, pos):
    first = jnp.zeros_like(pos)
    last = jnp.full_like(pos, SEQ_LEN)
    for k in range(DOCS):
        first = jnp.where(pos >= info[k], info[k], first)
    for k in reversed(range(DOCS)):
        last = jnp.where(pos < info[k], info[k], last)
    return pos - first, last - 1 - pos


def chunk_masks(info, c):
    local = lax.broadcasted_iota(jnp.int32, (SPAN, 128), 0)
    since, until = doc_place(info, local + c * SPAN)
    return local, since, until


def wide2(v):
    return jnp.concatenate([v, v], axis=1)


def expand(cols):
    rows = cols.shape[0]
    low = lax.broadcasted_iota(jnp.int32, (rows, 128), 1) < HEAD_DIM
    tiles = [
        jnp.where(low, cols[:, 2 * p : 2 * p + 1], cols[:, 2 * p + 1 : 2 * p + 2]) for p in range(WIDE // 128)
    ]
    return jnp.concatenate(tiles, axis=1)


def conv_inputs(src, info, c, per_block, r0):
    now = src[pl.ds(r0, SPAN), :].astype(F32)
    if c == 0:
        before = jnp.zeros((8, now.shape[1]), F32)
    else:
        p0 = chunk_start(info, c - 1, per_block)
        before = src[pl.ds(pl.multiple_of(p0 + SPAN - 16, 16), 16), :].astype(F32)[8:]
    ext = jnp.concatenate([before, now], axis=0)
    return now, [now] + [pltpu.roll(ext, k, 0)[8:] for k in range(1, CONV)]


def conv_apply(lags, taps, bias, masks):
    u = bias + taps[0] * lags[0]
    for k in range(1, CONV):
        u = u + taps[k] * (lags[k] * masks[k])
    return u


def conv_back(du, after, taps, masks_after):
    ext = jnp.concatenate([du, after], axis=0)
    total = taps[0] * du
    for k in range(1, CONV):
        total = total + taps[k] * (pltpu.roll(ext, SPAN + 8 - k, 0)[:SPAN] * masks_after[k])
    return total


def prep_kernel(per_block, info, pairs, par, bc_out, bct_out):
    taps = [par[k : k + 1, :] for k in range(CONV)]
    for c in range(CHUNKS):
        r0 = chunk_start(info, c, per_block)
        _, since, _ = chunk_masks(info, c)
        masks = [wide2((since >= k).astype(F32)) for k in range(CONV)]
        _, lags = conv_inputs(pairs, info, c, per_block, r0)
        u = conv_apply(lags, taps, par[4:5, :], masks)
        low = (u * sigmoid(u)).astype(BF16)
        bc_out[pl.ds(r0, SPAN), :] = low
        bct_out[:, pl.ds(r0, SPAN)] = low.T


def fwd_kernel(
    per_block, info, inner, gate, bc, bct, hs, par, y_out, mk_out, yg_out, st_out, ss_out, score_scr, state_scr
):
    taps = [par[k : k + 1, :] for k in range(CONV)]
    bias, skip, gain, act = par[4:5, :], par[5:6, :], par[6:7, :], par[7:8, :]
    lane = lax.broadcasted_iota(jnp.int32, (1, 128), 1)
    sides = [(lane < HEAD_DIM).astype(BF16), (lane >= HEAD_DIM).astype(BF16)]

    @pl.when(pl.program_id(0) == 0)
    def _():
        ss_out[...] = jnp.zeros_like(ss_out)
        for c in range(CHUNKS):
            r0 = chunk_start(info, c, per_block)
            _, since, _ = chunk_masks(info, c)
            bcv = bc[pl.ds(r0, SPAN), :]
            score = dot_nt(bcv[:, STATE:], bcv[:, :STATE])
            gap = lax.broadcasted_iota(jnp.int32, (SPAN, SPAN), 0) - lax.broadcasted_iota(
                jnp.int32, (SPAN, SPAN), 1
            )
            score_scr[c] = jnp.where((gap >= 0) & (gap <= wide2(since)), score, 0.0)

    state_scr[...] = jnp.zeros_like(state_scr)
    for c in range(CHUNKS):
        r0 = chunk_start(info, c, per_block)
        local, since, until = chunk_masks(info, c)
        masks = [wide2((since >= k).astype(F32)) for k in range(CONV)]
        _, lags = conv_inputs(inner, info, c, per_block, r0)
        u = conv_apply(lags, taps, bias, masks)
        xf = (u * sigmoid(u)).astype(BF16).astype(F32)
        head_rows = hs[:, pl.ds(r0, SPAN)]
        cum_rows = head_rows[:8]
        cum = cum_rows.T
        step = head_rows[8:].T
        local8, since8, until8 = local[:, :8], since[:, :8], until[:, :8]
        cum_end = cum[SPAN - 1 : SPAN, :]
        entry = jnp.where(since8 > local8, jnp.exp(cum), 0.0)
        tail = jnp.where(until8 >= SPAN - 1 - local8, jnp.exp(cum_end - cum), 0.0)
        keep = entry[SPAN - 1 : SPAN, :]
        xs = (xf * expand(step)).astype(BF16)
        xw = (xf * expand(tail * step)).astype(BF16)
        state = state_scr[...]
        state_low = state.astype(BF16)
        st_out[pl.ds(c * STATE, STATE), :] = state_low
        carried = dot_nn(bc[pl.ds(r0, SPAN), STATE:], state_low) * expand(entry)
        state_scr[...] = state * expand(keep) + dot_nn(bct[:STATE, pl.ds(r0, SPAN)], xw)
        tiles = []
        for p in range(WIDE // 128):
            tile = carried[:, p * 128 : (p + 1) * 128]
            for s in range(2):
                h = 2 * p + s
                values = xs[:, p * 128 : (p + 1) * 128] * sides[s]
                strips = []
                for at, end in BELOW:
                    gap = cum[at : at + STRIP, h : h + 1] - cum_rows[h : h + 1, :end]
                    decays = jnp.exp(jnp.minimum(gap, 0.0))
                    mixing = (decays * score_scr[c, at : at + STRIP, :end]).astype(BF16)
                    strips.append(dot_nn(mixing, values[:end]))
                tile = tile + jnp.concatenate(strips, axis=0)
            tiles.append(tile)
        y = jnp.concatenate(tiles, axis=1)
        y_out[pl.ds(r0, SPAN), :] = y.astype(BF16)
        g = gate[pl.ds(r0, SPAN), :].astype(F32)
        masked = (y + skip * xf) * act
        mk_out[pl.ds(r0, SPAN), :] = masked.astype(BF16)
        gated = masked * (g * sigmoid(g))
        yg_out[pl.ds(r0, SPAN), :] = (gated * gain).astype(BF16)
        square = gated * gated
        ss_out[pl.ds(r0, SPAN), :] += square[:, :128] + square[:, 128:]


def split_low(v):
    high = v.astype(BF16)
    return high, (v - high.astype(F32)).astype(BF16)


def gate_kernel(mk, gate, dn_in, sk, par, dgate_out, dy_out, gg_out):
    gain, act = par[6:7, :], par[7:8, :]
    total = jnp.zeros((1, WIDE), F32)
    for c in range(CHUNKS):
        rows = pl.ds(c * SPAN, SPAN)
        row_cols = sk[:, c * SPAN : (c + 1) * SPAN].T
        scale, fix = row_cols[:, 0:1], row_cols[:, 1:2]
        g = gate[rows, :].astype(F32)
        sg = sigmoid(g)
        sw = g * sg
        masked = mk[rows, :].astype(F32)
        gated = masked * sw
        d_scale = dn_in[rows, :].astype(F32) * scale
        d_gated = d_scale * gain - gated * fix
        dgate_out[rows, :] = (d_gated * masked * sg * (1.0 + g * (1.0 - sg))).astype(BF16)
        dy_out[rows, :] = (d_gated * sw * act).astype(BF16)
        total = total + jnp.sum(d_scale * gated, axis=0, keepdims=True)
    gg_out[...] = total + jnp.zeros((8, WIDE), F32)


def bwd_kernel(
    per_block,
    blocks,
    info,
    inner,
    y_in,
    dy_in,
    bc,
    bct,
    hs,
    st,
    par,
    dinner_out,
    dbc_out,
    gp_out,
    hr_out,
    score_scr,
    pair_scr,
    mask_scr,
    adj_scr,
):
    taps = [par[k : k + 1, :] for k in range(CONV)]
    bias, skip = par[4:5, :], par[5:6, :]
    lane = lax.broadcasted_iota(jnp.int32, (1, 128), 1)
    sides = [(lane < HEAD_DIM).astype(BF16), (lane >= HEAD_DIM).astype(BF16)]
    head_of = lax.broadcasted_iota(jnp.int32, (8, WIDE), 1) // HEAD_DIM
    row8 = lax.broadcasted_iota(jnp.int32, (8, WIDE), 0)
    pick = (head_of == row8).astype(BF16)
    pick_up = (head_of + 4 == row8).astype(BF16)

    @pl.when(pl.program_id(0) == 0)
    def _():
        dbc_out[...] = jnp.zeros_like(dbc_out)
        pair_scr[...] = jnp.zeros_like(pair_scr)
        for c in range(CHUNKS):
            r0 = chunk_start(info, c, per_block)
            _, since, until = chunk_masks(info, c)
            bcv = bc[pl.ds(r0, SPAN), :]
            score = dot_nt(bcv[:, :STATE], bcv[:, STATE:])
            gap = lax.broadcasted_iota(jnp.int32, (SPAN, SPAN), 1) - lax.broadcasted_iota(
                jnp.int32, (SPAN, SPAN), 0
            )
            score_scr[c] = jnp.where((gap >= 0) & (gap <= wide2(until)), score, 0.0)
            mask_scr[c] = jnp.where((gap <= 0) & (-gap <= wide2(since)), 1.0, 0.0).astype(BF16)

    adj_scr[...] = jnp.zeros_like(adj_scr)
    after = jnp.zeros((8, WIDE), F32)
    gp = jnp.zeros((8, WIDE), F32)
    for c in reversed(range(CHUNKS)):
        r0 = chunk_start(info, c, per_block)
        local, since, until = chunk_masks(info, c)
        masks = [wide2((since >= k).astype(F32)) for k in range(CONV)]
        masks_after = [wide2((until >= k).astype(F32)) for k in range(CONV)]
        _, lags = conv_inputs(inner, info, c, per_block, r0)
        u = conv_apply(lags, taps, bias, masks)
        su = sigmoid(u)
        xf = (u * su).astype(BF16).astype(F32)
        head_rows = hs[:, pl.ds(r0, SPAN)]
        cum_rows, step_rows = head_rows[:8], head_rows[8:]
        cum = cum_rows.T
        step = step_rows.T
        local8, since8, until8 = local[:, :8], since[:, :8], until[:, :8]
        cum_end = cum[SPAN - 1 : SPAN, :]
        entry = jnp.where(since8 > local8, jnp.exp(cum), 0.0)
        tail = jnp.where(until8 >= SPAN - 1 - local8, jnp.exp(cum_end - cum), 0.0)
        keep = entry[SPAN - 1 : SPAN, :]
        step_wide = expand(step)
        xs = (xf * step_wide).astype(BF16)
        xw = (xf * expand(tail * step)).astype(BF16)
        y = y_in[pl.ds(r0, SPAN), :].astype(F32)
        dy_low = dy_in[pl.ds(r0, SPAN), :]
        dy = dy_low.astype(F32)
        dy_entry = (dy * expand(entry)).astype(BF16)

        adj = adj_scr[...]
        adj_low = adj.astype(BF16)
        bcv = bc[pl.ds(r0, SPAN), :]
        d_c = dot_nt(dy_entry, st[pl.ds(c * STATE, STATE), :])
        d_b = dot_nt(xw, adj_low)
        dbc_out[pl.ds(r0, SPAN), :] += jnp.concatenate([d_b, d_c], axis=1)
        carried = dot_nn(bcv[:, :STATE], adj_low) * expand(tail)
        adj_scr[...] = adj * expand(keep) + dot_nn(bct[STATE:, pl.ds(r0, SPAN)], dy_entry)

        tiles = []
        for p in range(WIDE // 128):
            tile = carried[:, p * 128 : (p + 1) * 128]
            dy_tile = dy_low[:, p * 128 : (p + 1) * 128]
            xs_tile = xs[:, p * 128 : (p + 1) * 128]
            for s in range(2):
                h = 2 * p + s
                dy_side = dy_tile * sides[s]
                xs_side = xs_tile * sides[s]
                strips = []
                for at, begin in ABOVE:
                    rows = slice(at, at + STRIP)
                    gap = cum_rows[h : h + 1, begin:] - cum[rows, h : h + 1]
                    decays = jnp.exp(jnp.minimum(gap, 0.0))
                    mixing = (decays * score_scr[c, rows, begin:]).astype(BF16)
                    strips.append(dot_nn(mixing, dy_side[begin:]))
                    pair_scr[c, rows, begin:] += decays * dot_nt(xs_side[rows], dy_tile[begin:])
                tile = tile + jnp.concatenate(strips, axis=0)
            tiles.append(tile)
        dxu = jnp.concatenate(tiles, axis=1)

        du = (step_wide * dxu + skip * dy) * (su * (1.0 + u * (1.0 - su)))
        dinner_out[pl.ds(r0, SPAN), :] = conv_back(du, after, taps, masks_after).astype(BF16)
        after = du[:8]
        sums = [jnp.sum(du * lags[k] * masks[k], axis=0, keepdims=True) for k in range(CONV)]
        sums += [jnp.sum(du, axis=0, keepdims=True), jnp.zeros((3, WIDE), F32)]
        gp = gp + jnp.concatenate(sums, axis=0)

        q1h, q1l = split_low(dy * y)
        q2h, q2l = split_low(xf * dxu)
        q3h, q3l = split_low(xf * dy)
        row_term = dot_nt(pick, q1h) + dot_nt(pick, q1l)
        steps = dot_nt(pick, q2h) + dot_nt(pick, q2l) + dot_nt(pick_up, q3h) + dot_nt(pick_up, q3l)
        vh, vl = split_low(row_term - step_rows * jnp.where(row8 < GROUP, steps, 0.0))
        d_decay = dot_nn(vh, mask_scr[c]) + dot_nn(vl, mask_scr[c])
        row_local = lax.broadcasted_iota(jnp.int32, (8, SPAN), 1)
        row_since, row_until = doc_place(info, row_local + c * SPAN)
        if c < CHUNKS - 1:
            ph, plow = split_low(st[pl.ds((c + 1) * STATE, STATE), :].astype(F32) * adj)
            cross = jnp.sum(dot_nt(pick, ph) + dot_nt(pick, plow), axis=1, keepdims=True)
            d_decay = d_decay + jnp.where(row_until >= SPAN - 1 - row_local, cross, 0.0)
        d_decay = jnp.where(row_since > 0, d_decay, 0.0)
        hr_out[:, pl.ds(r0, SPAN)] = jnp.concatenate([steps, d_decay], axis=0)
    gp_out[...] = gp

    @pl.when(pl.program_id(0) == blocks - 1)
    def _():
        for c in range(CHUNKS):
            r0 = chunk_start(info, c, per_block)
            _, _, until = chunk_masks(info, c)
            gap = lax.broadcasted_iota(jnp.int32, (SPAN, SPAN), 1) - lax.broadcasted_iota(
                jnp.int32, (SPAN, SPAN), 0
            )
            pair_low = jnp.where((gap >= 0) & (gap <= wide2(until)), pair_scr[c], 0.0).astype(BF16)
            bcv = bc[pl.ds(r0, SPAN), :]
            dbc_out[pl.ds(r0, SPAN), :] += jnp.concatenate(
                [dot_nn(pair_low, bcv[:, STATE:]), dot_tn(pair_low, bcv[:, :STATE])], axis=1
            )


def pair_kernel(per_block, info, pairs, dbc_a, dbc_b, par, dp_out, gp_out):
    taps = [par[k : k + 1, :] for k in range(CONV)]
    after = jnp.zeros((8, WIDE), F32)
    gp = jnp.zeros((8, WIDE), F32)
    for c in reversed(range(CHUNKS)):
        r0 = chunk_start(info, c, per_block)
        _, since, until = chunk_masks(info, c)
        masks = [wide2((since >= k).astype(F32)) for k in range(CONV)]
        masks_after = [wide2((until >= k).astype(F32)) for k in range(CONV)]
        _, lags = conv_inputs(pairs, info, c, per_block, r0)
        u = conv_apply(lags, taps, par[4:5, :], masks)
        su = sigmoid(u)
        rows = pl.ds(r0, SPAN)
        du = (dbc_a[rows, :] + dbc_b[rows, :]) * (su * (1.0 + u * (1.0 - su)))
        dp_out[rows, :] = conv_back(du, after, taps, masks_after).astype(BF16)
        after = du[:8]
        sums = [jnp.sum(du * lags[k] * masks[k], axis=0, keepdims=True) for k in range(CONV)]
        sums += [jnp.sum(du, axis=0, keepdims=True), jnp.zeros((3, WIDE), F32)]
        gp = gp + jnp.concatenate(sums, axis=0)
    gp_out[...] = gp


def whole(shape):
    return pl.BlockSpec(shape, lambda i, info: (0,) * len(shape))


def cols(rows):
    return pl.BlockSpec((rows, WIDE), lambda i, info: (0, i))


def ignore(kernel, at, count):
    if not count:
        return kernel
    return lambda *refs: kernel(*refs[:at], *refs[at + count :])


def unread(later):
    return [pl.BlockSpec(memory_space=pl.ANY) for _ in later]


def call(kernel, grid, in_specs, out_specs, out_shape, scratch, us, info, *operands, later=()):
    kernel = ignore(kernel, 1 + len(operands), len(later))
    in_specs = [*in_specs, *unread(later)]
    operands = [*operands, *later]
    return pl.pallas_call(
        kernel,
        grid_spec=pltpu.PrefetchScalarGridSpec(
            num_scalar_prefetch=1,
            grid=(grid,),
            in_specs=in_specs,
            out_specs=out_specs,
            scratch_shapes=scratch,
        ),
        out_shape=out_shape,
        compiler_params=pltpu.CompilerParams(vmem_limit_bytes=VMEM_LIMIT),
        cost_estimate=lasting(us),
    )(info, *operands)


def shape(dims, kind):
    return jax.ShapeDtypeStruct(dims, kind)


def project(a, b, kind, later):
    rows, depth = a.shape
    b, number = b if isinstance(b, tuple) else (b, 0)
    columns = b.shape[-1]
    wide = min(columns, 512)
    block = pl.BlockSpec((depth, wide), lambda j: (0, j))
    if b.ndim == 4:
        block = pl.BlockSpec((b.shape[0], 1, b.shape[2], wide), lambda j: (0, number, 0, j))

    def kernel(x, w, out):
        out[...] = dot_nn(x[...], w[...].reshape(depth, wide)).astype(kind)

    return pl.pallas_call(
        ignore(kernel, 2, len(later)),
        grid=(columns // wide,),
        in_specs=[
            pl.BlockSpec((rows, depth), lambda j: (0, 0)),
            block,
            *unread(later),
        ],
        out_specs=pl.BlockSpec((rows, wide), lambda j: (0, j)),
        out_shape=shape((rows, columns), kind),
        compiler_params=pltpu.CompilerParams(vmem_limit_bytes=VMEM_LIMIT),
        cost_estimate=lasting(6),
    )(a, b, *later)


def project_few(a, b, later):
    rows, depth = a.shape
    columns = b.shape[1]

    def kernel(x, w, out):
        out[...] = dot_nn(x[...], w[...])

    return pl.pallas_call(
        ignore(kernel, 2, len(later)),
        grid=(rows // 256,),
        in_specs=[
            pl.BlockSpec((256, depth), lambda i: (i, 0)),
            pl.BlockSpec((depth, columns), lambda i: (0, 0)),
            *unread(later),
        ],
        out_specs=pl.BlockSpec((256, columns), lambda i: (i, 0)),
        out_shape=shape((rows, columns), F32),
        compiler_params=pltpu.CompilerParams(vmem_limit_bytes=VMEM_LIMIT),
        cost_estimate=lasting(3),
    )(a, b, *later)


def project_back(up, w, yg, later):
    rows, depth = up.shape
    columns = w.shape[0]
    wide = min(columns, 512)

    def kernel(x, b, y, out, sums):
        value = dot_nt(x[...], b[...])
        out[...] = value.astype(BF16)
        value = value * y[...].astype(F32)
        total = value[:, :128]
        for k in range(1, wide // 128):
            total = total + value[:, k * 128 : (k + 1) * 128]

        @pl.when(pl.program_id(0) == 0)
        def _():
            sums[...] = total

        @pl.when(pl.program_id(0) > 0)
        def _():
            sums[...] += total

    return pl.pallas_call(
        ignore(kernel, 3, len(later)),
        grid=(columns // wide,),
        in_specs=[
            pl.BlockSpec((rows, depth), lambda j: (0, 0)),
            pl.BlockSpec((wide, depth), lambda j: (j, 0)),
            pl.BlockSpec((rows, wide), lambda j: (0, j)),
            *unread(later),
        ],
        out_specs=[pl.BlockSpec((rows, wide), lambda j: (0, j)), pl.BlockSpec((rows, 128), lambda j: (0, 0))],
        out_shape=[shape((rows, columns), BF16), shape((rows, 128), F32)],
        compiler_params=pltpu.CompilerParams(vmem_limit_bytes=VMEM_LIMIT),
        cost_estimate=lasting(8),
    )(up, w, yg, *later)


def rows_forward(lefts, rights, first, rows, later=()):
    columns = rights[0].shape[1]
    wide = 512
    count = len(lefts)
    start = first // rows

    def kernel(*refs):
        total = dot_nn(refs[0][...], refs[count][...])
        for n in range(1, count):
            total = total + dot_nn(refs[n][...], refs[count + n][...])
        refs[-1][...] = total.astype(BF16)

    return pl.pallas_call(
        ignore(kernel, 2 * count, len(later)),
        grid=(columns // wide,),
        in_specs=[pl.BlockSpec((rows, v.shape[1]), lambda j: (start, 0)) for v in lefts]
        + [pl.BlockSpec((v.shape[0], wide), lambda j: (0, j)) for v in rights]
        + unread(later),
        out_specs=pl.BlockSpec((rows, wide), lambda j: (0, j)),
        out_shape=shape((rows, columns), BF16),
        compiler_params=pltpu.CompilerParams(vmem_limit_bytes=VMEM_LIMIT),
        cost_estimate=lasting(5),
    )(*lefts, *rights, *later)


def delayed(v, later):
    flat = v.reshape(-1, v.shape[-1])
    rows, width = flat.shape
    block = rows // 2 if rows % 32 == 0 else rows

    def kernel(a, out):
        out[...] = a[...]

    return pl.pallas_call(
        ignore(kernel, 1, len(later)),
        grid=(rows // block,),
        in_specs=[pl.BlockSpec((block, width), lambda i: (i, 0)), *unread(later)],
        out_specs=pl.BlockSpec((block, width), lambda i: (i, 0)),
        out_shape=shape((rows, width), v.dtype),
        compiler_params=pltpu.CompilerParams(vmem_limit_bytes=VMEM_LIMIT),
        cost_estimate=lasting(2),
    )(flat, *later).reshape(v.shape)


def added(a, b, later):
    def kernel(x, y, out):
        out[...] = (x[...].astype(F32) + y[...].astype(F32)).astype(BF16)

    return pl.pallas_call(
        ignore(kernel, 2, len(later)),
        in_specs=[pl.BlockSpec(memory_space=pltpu.VMEM)] * 2 + unread(later),
        out_specs=pl.BlockSpec(memory_space=pltpu.VMEM),
        out_shape=shape(a.shape, BF16),
        compiler_params=pltpu.CompilerParams(vmem_limit_bytes=VMEM_LIMIT),
        cost_estimate=lasting(1),
    )(a, b, *later)


def norm_rows(own, got, gain, later):
    rows, width = own.shape
    block = min(rows, 256)
    here = rows // block

    def kernel(a, b, gain_row, out):
        def write(v):
            v = v.astype(F32)
            inverse = lax.rsqrt(jnp.mean(v * v, axis=1, keepdims=True) + EPSILON)
            out[...] = (v * inverse * gain_row[...]).astype(BF16)

        @pl.when(pl.program_id(0) < here)
        def _():
            write(a[...])

        @pl.when(pl.program_id(0) >= here)
        def _():
            write(b[...])

    return pl.pallas_call(
        ignore(kernel, 3, len(later)),
        grid=(SEQ_LEN // block,),
        in_specs=[
            pl.BlockSpec((block, width), lambda i: (jnp.minimum(i, here - 1), 0)),
            pl.BlockSpec((block, width), lambda i: (jnp.maximum(i - here, 0), 0)),
            pl.BlockSpec((1, width), lambda i: (0, 0)),
            *unread(later),
        ],
        out_specs=pl.BlockSpec((block, width), lambda i: (i, 0)),
        out_shape=shape((SEQ_LEN, width), BF16),
        compiler_params=pltpu.CompilerParams(vmem_limit_bytes=VMEM_LIMIT),
        cost_estimate=lasting(4),
    )(own, got, gain[None], *later)


def prep(per_block, info, pairs, par):
    t = SEQ_LEN
    return call(
        functools.partial(prep_kernel, per_block),
        1,
        [whole((t, WIDE)), whole((8, WIDE))],
        [whole((t, WIDE)), whole((WIDE, t))],
        [shape((t, WIDE), BF16), shape((WIDE, t), BF16)],
        [],
        2,
        info,
        pairs,
        par,
    )


def scan_forward(per_block, info, inner, gate, bc, bct, hs, par, later):
    t, channels = inner.shape
    blocks = channels // WIDE
    return call(
        functools.partial(fwd_kernel, per_block),
        blocks,
        [
            cols(t),
            cols(t),
            whole((t, WIDE)),
            whole((WIDE, t)),
            pl.BlockSpec((16, t), lambda i, info: (i, 0)),
            cols(8),
        ],
        [cols(t), cols(t), cols(t), cols(CHUNKS * STATE), whole((t, 128))],
        [
            shape((t, channels), BF16),
            shape((t, channels), BF16),
            shape((t, channels), BF16),
            shape((CHUNKS * STATE, channels), BF16),
            shape((t, 128), F32),
        ],
        [pltpu.VMEM((CHUNKS, SPAN, SPAN), F32), pltpu.VMEM((STATE, WIDE), F32)],
        20,
        info,
        inner,
        gate,
        bc,
        bct,
        hs,
        par,
        later=later,
    )


def scan_backward(per_block, info, inner, y, dy, bc, bct, hs, st, par, later):
    t, channels = inner.shape
    blocks = channels // WIDE
    return call(
        functools.partial(bwd_kernel, per_block, blocks),
        blocks,
        [
            cols(t),
            cols(t),
            cols(t),
            whole((t, WIDE)),
            whole((WIDE, t)),
            pl.BlockSpec((16, t), lambda i, info: (i, 0)),
            cols(CHUNKS * STATE),
            cols(8),
        ],
        [
            cols(t),
            whole((t, WIDE)),
            cols(8),
            pl.BlockSpec((16, t), lambda i, info: (i, 0)),
        ],
        [
            shape((t, channels), BF16),
            shape((t, WIDE), F32),
            shape((8, channels), F32),
            shape((blocks * 16, t), F32),
        ],
        [
            pltpu.VMEM((CHUNKS, SPAN, SPAN), F32),
            pltpu.VMEM((CHUNKS, SPAN, SPAN), F32),
            pltpu.VMEM((CHUNKS, SPAN, SPAN), BF16),
            pltpu.VMEM((STATE, WIDE), F32),
        ],
        36,
        info,
        inner,
        y,
        dy,
        bc,
        bct,
        hs,
        st,
        par,
        later=later,
    )


def gate_backward(mk, gate, dn, sk, par, later):
    t, channels = gate.shape
    block = pl.BlockSpec((t, WIDE), lambda i: (0, i))
    small = pl.BlockSpec((8, WIDE), lambda i: (0, i))
    return pl.pallas_call(
        ignore(gate_kernel, 5, len(later)),
        grid=(channels // WIDE,),
        in_specs=[block, block, block, pl.BlockSpec((8, t), lambda i: (0, 0)), small, *unread(later)],
        out_specs=[block, block, small],
        out_shape=[shape((t, channels), BF16)] * 2 + [shape((8, channels), F32)],
        compiler_params=pltpu.CompilerParams(vmem_limit_bytes=VMEM_LIMIT),
        cost_estimate=lasting(8),
    )(mk, gate, dn, sk, par, *later)


def turned(number, bits):
    return sum(((number >> k) & 1) << (bits - 1 - k) for k in range(bits))


def grad_half(lefts, rights, half, more=None, scale=None, later=(), pieces=1, bits=0):
    t, width = lefts[0].shape
    columns = rights[0].shape[1]
    count = max(len(lefts), len(rights))
    tall = width // 2 // pieces
    high, wide = min(width // 2, 256 if bits else 512), min(columns, 1024)
    down, along = width // 2 // high, columns // wide
    group = max(high // tall, 1)
    split = max(tall // high, 1)
    if bits and group > 1:
        high, group = tall, 1
        high = max(high, 128)
        group = high // tall
        down = width // 2 // high
    resident = bits > 0 and group > 1
    if resident:
        block = pl.BlockSpec((pieces, count, tall, wide), lambda j, i, info: (0, 0, 0, j))
    else:
        block = pl.BlockSpec(
            (group, count, tall // split, wide),
            lambda j, i, info: (turned(i // split, bits) if bits else i // split, 0, i % split, j),
        )
    operands = [*lefts, *rights] + ([] if more is None else [more]) + ([] if scale is None else [scale])

    def kernel(info, *refs):
        out = refs[-1]
        for n in range(count):
            left = refs[n % len(lefts)][...]
            if scale is not None:
                left = (left.astype(F32) * refs[-2][...].T[:, 0:1]).astype(BF16)
            total = dot_tn(left, refs[len(lefts) + n % len(rights)][...])
            for g in range(group):
                rows = total if group == 1 else total[g * tall : (g + 1) * tall]
                at = turned(pl.program_id(1) * group + g, bits) if resident else g
                if more is not None:
                    rows = rows + refs[len(lefts) + len(rights)][at, n].astype(F32)
                out[at, n] = rows.astype(BF16)

    return pl.pallas_call(
        ignore(kernel, 1 + len(operands), len(later)),
        grid_spec=pltpu.PrefetchScalarGridSpec(
            num_scalar_prefetch=1,
            grid=(along, down),
            in_specs=[pl.BlockSpec((t, high), lambda j, i, info: (0, info[0] * down + i)) for _ in lefts]
            + [pl.BlockSpec((t, wide), lambda j, i, info: (0, j)) for _ in rights]
            + ([] if more is None else [block])
            + ([] if scale is None else [pl.BlockSpec((8, t), lambda j, i, info: (0, 0))])
            + unread(later),
            out_specs=block,
        ),
        out_shape=shape((pieces, count, tall, columns), BF16),
        compiler_params=pltpu.CompilerParams(vmem_limit_bytes=VMEM_LIMIT),
        cost_estimate=lasting(7),
    )(half[None], *operands, *later)


def grad_pieces(left, right, shared, batches, bits, later=()):
    t, width = left.shape
    columns = right.shape[1]
    chips = batches // 2
    tall = width // batches // 2
    high = 256
    group = high // tall

    extra = 0 if shared is None else shared.shape[1]

    def kernel(a, b, *refs):
        out = refs[-1]
        total = dot_tn(a[...], b[...]).astype(BF16)
        for g in range(group):
            block = pl.program_id(0) * group + g
            core, quarter, number = block // (2 * chips), (block // chips) % 2, block % chips
            chip = jnp.where(quarter == 0, number, turned(number, bits))
            rows = pl.ds(pl.multiple_of(quarter * tall, tall), tall)
            out[chip * 2 + core, rows, :] = total[g * tall : (g + 1) * tall]

        if extra:

            @pl.when(pl.program_id(0) == width // high - 1)
            def _():
                out[:, 2 * tall :, :] = refs[0][...]

    return pl.pallas_call(
        ignore(kernel, 3 if extra else 2, len(later)),
        grid=(width // high,),
        in_specs=[
            pl.BlockSpec((t, high), lambda i: (0, i)),
            pl.BlockSpec((t, columns), lambda i: (0, 0)),
        ]
        + ([pl.BlockSpec(shared.shape, lambda i: (0, 0, 0))] if extra else [])
        + unread(later),
        out_specs=pl.BlockSpec((batches, 2 * tall + extra, columns), lambda i: (0, 0, 0)),
        out_shape=shape((batches, 2 * tall + extra, columns), BF16),
        compiler_params=pltpu.CompilerParams(vmem_limit_bytes=VMEM_LIMIT),
        cost_estimate=lasting(10),
    )(left, right, *([shared] if extra else []), *later)


def place_pieces(v, tall, bits, later):
    batches, _, columns = v.shape
    chips = batches // 2

    half = chips * tall
    wide = columns // 4

    def kernel(a, out):
        for core in range(2):
            for chip in range(chips):
                v = a[chip * 2 + core]
                for quarter, number in ((0, chip), (1, turned(chip, bits))):
                    at = (core * 2 + quarter) * half + number * tall
                    out[at : at + tall, :] = v[quarter * tall : (quarter + 1) * tall].astype(F32)

    return pl.pallas_call(
        ignore(kernel, 1, len(later)),
        grid=(4,),
        in_specs=[pl.BlockSpec((batches, 2 * tall, wide), lambda i: (0, 0, i)), *unread(later)],
        out_specs=pl.BlockSpec((4 * half, wide), lambda i: (0, i)),
        out_shape=shape((4 * half, columns), F32),
        compiler_params=pltpu.CompilerParams(vmem_limit_bytes=VMEM_LIMIT),
        cost_estimate=lasting(7),
    )(v, *later)


def place_halves(mine, other, core):
    rows, columns = mine.shape
    high = min(rows, 256)
    per = rows // high

    def kernel(info, a, b, out):
        here = pl.program_id(0) // per == info[0]

        @pl.when(here)
        def _():
            out[...] = a[...].astype(F32)

        @pl.when(jnp.logical_not(here))
        def _():
            out[...] = b[...].astype(F32)

    return pl.pallas_call(
        kernel,
        grid_spec=pltpu.PrefetchScalarGridSpec(
            num_scalar_prefetch=1,
            grid=(2 * per,),
            in_specs=[
                pl.BlockSpec((high, columns), lambda i, info: (jnp.clip(i - info[0] * per, 0, per - 1), 0)),
                pl.BlockSpec((high, columns), lambda i, info: (jnp.clip(i - (1 - info[0]) * per, 0, per - 1), 0)),
            ],
            out_specs=pl.BlockSpec((high, columns), lambda i, info: (i, 0)),
        ),
        out_shape=shape((2 * rows, columns), F32),
        compiler_params=pltpu.CompilerParams(vmem_limit_bytes=VMEM_LIMIT),
        cost_estimate=lasting(6),
    )(core[None], mine, other)


def small_grads(left, right, later):
    t, columns = right.shape
    wide = 512

    def kernel(a, b, out):
        out[...] = dot_tn(a[...], b[...])

    return pl.pallas_call(
        ignore(kernel, 2, len(later)),
        grid=(columns // wide,),
        in_specs=[
            pl.BlockSpec(left.shape, lambda j: (0, 0)),
            pl.BlockSpec((t, wide), lambda j: (0, j)),
            *unread(later),
        ],
        out_specs=pl.BlockSpec((left.shape[1], wide), lambda j: (0, j)),
        out_shape=shape((left.shape[1], columns), F32),
        compiler_params=pltpu.CompilerParams(vmem_limit_bytes=VMEM_LIMIT),
        cost_estimate=lasting(4),
    )(left, right, *later)


def rows_back(lefts, rights, first, rows, gain_rows, later=()):
    columns = rights[0].shape[0]
    wide = 512

    def right_block(v):
        if not isinstance(v, tuple):
            return pl.BlockSpec((wide, v.shape[1]), lambda j: (j, 0))
        v, number = v
        return pl.BlockSpec((wide // v.shape[2], 1, v.shape[2], v.shape[3]), lambda j: (j, number, 0, 0))

    count = len(lefts)
    start = first // rows

    def kernel(*refs):
        total = dot_nt(refs[0][...], refs[count][...].reshape(wide, -1))
        for n in range(1, count):
            total = total + dot_nt(refs[n][...], refs[count + n][...].reshape(wide, -1))
        unit, out, sums = refs[-3:]
        out[...] = total.astype(BF16)
        sums[...] = jnp.sum(total * unit[...].astype(F32), axis=0, keepdims=True) + jnp.zeros((8, wide), F32)

    return pl.pallas_call(
        ignore(kernel, 2 * count + 1, len(later)),
        grid=(columns // wide,),
        in_specs=[pl.BlockSpec((rows, v.shape[1]), lambda j: (start, 0)) for v in lefts]
        + [right_block(v) for v in rights]
        + [pl.BlockSpec((rows, wide), lambda j: (start, j))]
        + unread(later),
        out_specs=[pl.BlockSpec((rows, wide), lambda j: (0, j)), pl.BlockSpec((8, wide), lambda j: (0, j))],
        out_shape=[shape((rows, columns), BF16), shape((8, columns), F32)],
        compiler_params=pltpu.CompilerParams(vmem_limit_bytes=VMEM_LIMIT),
        cost_estimate=lasting(15),
    )(*lefts, *[v[0] if isinstance(v, tuple) else v for v in rights], gain_rows, *later)


def pair_backward(per_block, info, pairs, dbc_a, dbc_b, par):
    t = SEQ_LEN
    return call(
        functools.partial(pair_kernel, per_block),
        1,
        [whole((t, WIDE)), whole((t, WIDE)), whole((t, WIDE)), whole((8, WIDE))],
        [whole((t, WIDE)), whole((8, WIDE))],
        [shape((t, WIDE), BF16), shape((8, WIDE), F32)],
        [],
        4,
        info,
        pairs,
        dbc_a,
        dbc_b,
        par,
    )


def body(
    axis_sizes,
    hidden_in,
    out_grad,
    norm_gain,
    w_z,
    w_x,
    w_dt,
    w_bc,
    conv_x,
    conv_x_bias,
    conv_bc,
    conv_bc_bias,
    dt_bias,
    a_log,
    d_skip,
    gate_gain,
    w_out,
    doc_lengths,
    widths,
):
    batches, stacks = axis_sizes
    rows, width_in = hidden_in.shape
    heads_here = dt_bias.shape[0]
    channels = w_x.shape[1]
    members = stacks // widths.shape[0]
    far_bit = members
    per_block = rows // SPAN
    place = lax.axis_index("head")
    lot = lax.axis_index("batch")
    own_seq = place // members
    ends = jnp.cumsum(lax.dynamic_index_in_dim(doc_lengths, own_seq, 0, keepdims=False))
    width = lax.dynamic_index_in_dim(widths, own_seq, 0, keepdims=False)
    info = jnp.concatenate([ends.astype(jnp.int32), (place % members).astype(jnp.int32)[None]])

    def across(v, bit):
        return lax.ppermute(v, "head", [(i, i ^ bit) for i in range(stacks)])

    def sum_rows(v):
        bit = 1
        while bit < members:
            got = across(v, bit)
            flipped = got.reshape(v.shape[0], -1, 2, bit * rows)[:, :, ::-1, :].reshape(v.shape)
            v = v + flipped
            bit *= 2
        return v

    chip_bits = []
    bit = 2
    while bit < batches:
        chip_bits.append(bit)
        bit *= 2
    chips = batches // 2
    core = lot % 2
    chip_groups = [[2 * i + c for i in range(chips)] for c in range(2)]
    orders = (chip_bits, chip_bits[::-1])

    def planar(v, bit):
        return lax.ppermute(v, "batch", [(i, i ^ bit) for i in range(batches)])

    def side(bit):
        return (lot // bit) % 2

    def join(v, got, bit, axis=0):
        low, high = jnp.concatenate([v, got], axis=axis), jnp.concatenate([got, v], axis=axis)
        return jnp.where(side(bit) == 0, low, high)

    def add(a, b):
        return (a.astype(F32) + b.astype(F32)).astype(BF16)

    def nothing(v):
        return (v[(0,) * v.ndim].astype(F32) * 0.0).astype(jnp.int32)

    def others(v):
        got, bit = across(v, 1), 2
        while bit < members:
            got = jnp.concatenate([got, across(jnp.concatenate([v, got], axis=0), bit)], axis=0)
            bit *= 2
        return got

    hidden_got = others(hidden_in)
    piece = width_in // batches
    far_parts = across(
        jnp.concatenate([lax.dynamic_slice_in_dim(w, lot * piece, piece, 0) for w in (w_x, w_z)], axis=0), far_bit
    )
    w_dt_own = w_dt.T
    w_dt_far = across(w_dt_own, far_bit)
    head_row = jnp.concatenate([dt_bias, a_log])
    par_own = jnp.concatenate(
        [
            conv_x,
            conv_x_bias[None],
            jnp.repeat(d_skip, HEAD_DIM)[None],
            gate_gain[None],
            jnp.pad(head_row, (0, channels - head_row.shape[0]))[None],
        ],
        axis=0,
    )
    par_far = across(par_own, far_bit)
    up_sent = delayed(out_grad, (hidden_got,))
    normed = norm_rows(hidden_in, hidden_got, norm_gain, (far_parts, w_dt_far, par_far, up_sent))
    far_parts = delayed(far_parts, (hidden_got, w_dt_far, par_far))
    far_parts = delayed(far_parts, (hidden_got, w_dt_far, par_far))
    far_both = lax.all_gather(far_parts, "batch", axis=0, tiled=True).reshape(batches, 2, piece, channels)
    out_piece = channels // batches
    w_out_part = across(
        lax.dynamic_slice_in_dim(w_out, lot * out_piece + nothing(normed), out_piece, 0), far_bit
    )
    up_got = others(up_sent)
    upstream = jnp.concatenate([out_grad, up_got], axis=0)
    active = (jnp.arange(channels) // HEAD_DIM < width * heads_here // (heads_here * stacks)).astype(F32)
    rate_par = [(v[7, :heads_here], v[7, heads_here : 2 * heads_here]) for v in (par_own, par_far)]
    par2 = [jnp.concatenate([v[:7], active[None]], axis=0) for v in (par_own, par_far)]
    step_bias = jnp.concatenate([rate_par[0][0], rate_par[1][0]])[:, None]
    speed = jnp.exp(jnp.concatenate([rate_par[0][1], rate_par[1][1]]))[:, None]
    par_bc = jnp.concatenate([conv_bc, conv_bc_bias[None], jnp.zeros((3, 2 * STATE), F32)], axis=0)

    w_small = jnp.concatenate([w_bc, w_dt_own.T, w_dt_far.T], axis=1)
    small_cols = project_few(normed, w_small, ())
    pairs = small_cols[:, : 2 * STATE]
    rates = small_cols[:, 2 * STATE :].T
    step = jax.nn.softplus(rates + step_bias)
    decay = -step * speed
    upper = (jnp.arange(SPAN)[:, None] <= jnp.arange(SPAN)[None, :]).astype(F32)
    cum = lax.dot_general(
        decay.reshape(-1, SPAN), upper, (((1,), (0,)), ((), ())), precision=lax.Precision.HIGHEST
    ).reshape(decay.shape)

    def grouped(v):
        v = v.reshape(-1, GROUP, SEQ_LEN)
        return jnp.pad(v, ((0, 0), (0, 8 - GROUP), (0, 0)))

    hs = jnp.concatenate([grouped(cum), grouped(step)], axis=1).reshape(-1, SEQ_LEN)
    half = hs.shape[0] // 2
    hs2 = (hs[:half], hs[half:])
    bc, bct = prep(per_block, info, pairs, par_bc)

    inner_own = project(normed, w_x, BF16, (bc,))
    gate_own = project(normed, w_z, BF16, (inner_own,))
    forward_own = scan_forward(per_block, info, inner_own, gate_own, bc, bct, hs2[0], par2[0], (up_got,))
    dn_own = project_back(upstream, w_out, forward_own[2], ())
    w_x_far, w_z_far = (far_both, 0), (far_both, 1)
    w_out_far = lax.all_gather(delayed(w_out_part, (forward_own[0],)), "batch", axis=0, tiled=True)
    w_x2 = (w_x, w_x_far)
    w_z2 = (w_z, w_z_far)
    w_out2 = (w_out, w_out_far)
    inner2 = (inner_own, project(normed, w_x_far, BF16, (dn_own[0],)))
    gate2 = (gate_own, project(normed, w_z_far, BF16, (inner2[1],)))
    forward = (forward_own, scan_forward(per_block, info, inner2[1], gate2[1], bc, bct, hs2[1], par2[1], ()))
    y2, mk2, yg2, st2 = [[f[k] for f in forward] for k in range(4)]
    dn_far = project_back(upstream, w_out_far, yg2[1], ())
    dn2 = (dn_own[0], dn_far[0])

    def branch_rows(first, count):
        return rows_forward(yg2, w_out2, first, count, (dn_far[0],) if first else (give_out,))

    def scatter_rows(make):
        if members == 2:
            give = make(rows, rows)
            got = across(give, 1)
            return give, got, lambda: make(0, rows).astype(F32) + got.astype(F32)
        v = make(0, SEQ_LEN)
        bit = members // 2
        while bit >= 1:
            half = v.shape[0] // 2
            v = add(v[:half], across(v[half:], bit))
            bit //= 2
        return v, v, lambda: v.astype(F32)

    give_out = dn_far[0]
    branch_given, branch_got, branch = scatter_rows(branch_rows)
    square = jnp.sum(forward[0][4] + forward[1][4], axis=1)
    sums = sum_rows(jnp.stack([square, jnp.sum(dn_own[1] + dn_far[1], axis=1)]))
    count = (width * HEAD_DIM).astype(F32)
    scale = lax.rsqrt(sums[0] / count + EPSILON)
    fix = scale * scale * scale * sums[1] / count
    sk = jnp.concatenate([scale[None], fix[None], jnp.zeros((6, SEQ_LEN), F32)], axis=0)

    bits = len(chip_bits)

    def swap_halves(lefts, rights, scale=None, later=(), pieces=1, bits=0):
        give = grad_half(lefts, rights, 1 - core, None, scale, later, pieces, bits)
        got = planar(give, 1)
        return give, lambda later=(): grad_half(lefts, rights, core, got, scale, later, pieces, bits)

    def scatter_offloaded(mine):
        flat = mine.reshape(-1, mine.shape[-1])
        part = lax.psum_scatter(flat, "batch", scatter_dimension=0, tiled=True, axis_index_groups=chip_groups)
        return part.reshape(mine.shape[1:])

    def send_far(part, earlier):
        far = lax.dynamic_slice_in_dim(part, 1 + jnp.minimum(nothing(earlier), 0), 1, 0)[0]
        return across(far, far_bit)

    def gather_both(parts, seen):
        for step in range(bits):
            got = [planar(v, order[step]) for v, order in zip(parts, orders)]
            parts = [join(v, g, order[step]) for v, g, order in zip(parts, got, orders)]
            seen.append(parts)
        return parts, [planar(v, 1) for v in parts]

    give_out, keep_out = swap_halves(yg2, [upstream], sk, (branch_given,), pieces=chips)
    gates = [gate_backward(mk2[i], gate2[i], dn2[i], sk, par2[i], (give_out,)) for i in range(2)]
    d_gate2 = [v[0] for v in gates]
    mine_out = keep_out(later=(d_gate2[0],))
    part_out = scatter_offloaded(mine_out)
    give_z, keep_z = swap_halves([normed], d_gate2, later=(mine_out,), pieces=chips, bits=bits)
    give_out = give_z
    branch_sum = branch()
    mixed = (hidden_in.astype(F32) + branch_sum * scale[:rows, None]).astype(BF16)
    mine_z = keep_z(later=(give_z,))
    part_z = scatter_offloaded(mine_z)

    def scan_back(i, later):
        return scan_backward(per_block, info, inner2[i], y2[i], gates[i][1], bc, bct, hs2[i], st2[i], par2[i], later)

    back = [None, None]
    back[1] = scan_back(1, (mine_z,))
    far_cut = grad_pieces(normed, back[1][0], None, batches, bits)
    far_piece = lax.psum_scatter(far_cut.reshape(-1, channels), "batch", scatter_dimension=0, tiled=True)
    far_out = send_far(part_out, back[1][0])
    back[0] = scan_back(0, (far_cut,))
    d_pairs, g_bc = pair_backward(per_block, info, pairs, back[0][1], back[1][1], par_bc)
    heads_out = [b[3].reshape(-1, 16, SEQ_LEN) for b in back]
    d_step = jnp.concatenate([h[:, :GROUP].reshape(-1, SEQ_LEN) for h in heads_out], axis=0)
    skip_rows = jnp.concatenate([h[:, GROUP : 2 * GROUP].reshape(-1, SEQ_LEN) for h in heads_out], axis=0)
    d_decay = jnp.concatenate([h[:, 8 : 8 + GROUP].reshape(-1, SEQ_LEN) for h in heads_out], axis=0)
    d_rates_pre = (d_step - d_decay * speed) * jax.nn.sigmoid(rates + step_bias)
    head_grads = jnp.stack(
        [jnp.sum(d_rates_pre, axis=1), jnp.sum(d_decay * decay, axis=1), jnp.sum(skip_rows, axis=1)]
    )
    d_rates = d_rates_pre.astype(BF16)
    d_small = jnp.concatenate([d_pairs, d_rates.T], axis=1)

    g_small = small_grads(d_small, normed, (part_z, branch_got))

    def pack(i):
        gp = back[i][2]
        heads = head_grads[:, i * heads_here : (i + 1) * heads_here].reshape(-1)
        heads = jnp.pad(heads, (0, channels - heads.shape[0]))[None]
        start = 2 * STATE + i * heads_here
        return jnp.concatenate(
            [gp[:5], heads, gates[i][2][:1], gp[7:], g_small[start : start + heads_here].reshape(-1, channels)], axis=0
        )

    def spread(v):
        v = jnp.pad(v.astype(BF16), ((0, -v.shape[0] % (16 * batches)), (0, 0)))
        return v.reshape(batches, -1, channels)

    far_z = send_far(part_z, g_small)
    norm_sums = []

    def normed_rows(first, count):
        part, total = rows_back(
            [*d_gate2, back[0][0], back[1][0], d_small],
            [*w_z2, *w_x2, w_small],
            first,
            count,
            normed,
            (norm_sums[0],) if norm_sums else (g_small,),
        )
        norm_sums.append(total)
        return part

    _, d_normed_got, d_normed_in = scatter_rows(normed_rows)
    d_normed_in = d_normed_in()
    bc_rows, few_rows = 2 * STATE * width_in // channels, 8 * 2 * STATE // channels
    shared = spread(jnp.concatenate([g_small[: 2 * STATE].reshape(-1, channels), g_bc.reshape(-1, channels), sum(norm_sums)[:1].reshape(-1, channels)], axis=0))
    private = spread(pack(0) + delayed(across(pack(1), far_bit), (norm_sums[-1],)))
    own_cut = grad_pieces(normed, back[0][0], jnp.concatenate([shared, private], axis=1), batches, bits, (d_normed_got, far_z, far_out))
    own_part = lax.psum_scatter(own_cut.reshape(-1, channels), "batch", scatter_dimension=0, tiled=True)
    seen = []
    total_z = added(part_z[0], far_z, (norm_sums[-1],))
    total_out = added(part_out[0], far_out, (norm_sums[-1],))
    total_out = delayed(total_out, (total_z,))
    halves_here, halves_there = gather_both([total_out, total_z], seen)
    own_part = delayed(own_part, halves_here)

    cut = 2 * (width_in // batches // 2)
    far_sent = across(delayed(far_piece, seen[0]), far_bit)
    bc_piece = own_part[cut : cut + shared.shape[1]]
    bit = 1
    while bit < stacks:
        bc_piece = add(bc_piece, across(bc_piece, bit))
        bit *= 2
    own_total = jnp.concatenate(
        [add(own_part[:cut], far_sent), bc_piece, own_part[cut + shared.shape[1] :]], axis=0
    )
    everything = lax.all_gather(own_total, "batch", axis=0, tiled=True).reshape(batches, -1, channels)
    g_w_out, g_w_z = [place_halves(v, got, core) for v, got in zip(halves_here, halves_there)]
    common = everything[:, cut : cut + shared.shape[1]].reshape(-1, channels).astype(F32)
    packed = everything[:, cut + shared.shape[1] :].reshape(-1, channels).astype(F32)
    g_w_bc = common[:bc_rows].reshape(2 * STATE, width_in).T
    g_bc_total = common[bc_rows : bc_rows + few_rows].reshape(8, -1)
    heads_total = packed[5]
    g_w_dt = packed[8 : 8 + heads_here * width_in // channels].reshape(heads_here, width_in).T
    g_norm = common[bc_rows + few_rows : bc_rows + few_rows + width_in // channels].reshape(-1) / norm_gain

    residual = hidden_in.astype(F32)
    inverse = lax.rsqrt(jnp.mean(residual * residual, axis=-1, keepdims=True) + EPSILON)
    unit_rows = residual * inverse
    d_unit = d_normed_in * norm_gain
    d_residual = inverse * (d_unit - unit_rows * jnp.mean(d_unit * unit_rows, axis=-1, keepdims=True))
    in_grad = (out_grad.astype(F32) + d_residual).astype(BF16)
    g_w_x = place_pieces(everything, cut // 2, bits, (g_w_out, g_w_z, in_grad))
    return (
        mixed,
        in_grad,
        g_norm,
        g_w_z,
        g_w_x,
        g_w_dt,
        g_w_bc,
        packed[:4],
        packed[4],
        g_bc_total[:4],
        g_bc_total[4],
        heads_total[:heads_here],
        heads_total[heads_here : 2 * heads_here],
        heads_total[2 * heads_here : 3 * heads_here],
        packed[6],
        g_w_out,
    )


def solution(mesh):
    split = P(("batch", "head"), None)
    by_col, by_head, by_row = P(None, "head"), P("head"), P("head", None)
    return jax.shard_map(
        functools.partial(body, (mesh.shape["batch"], mesh.shape["head"])),
        mesh=mesh,
        in_specs=(
            split,
            split,
            P(),
            by_col,
            by_col,
            by_col,
            P(),
            by_col,
            by_head,
            P(),
            P(),
            by_head,
            by_head,
            by_head,
            by_head,
            by_row,
            P("batch", None),
            P("batch"),
        ),
        out_specs=(
            split,
            split,
            P(),
            by_col,
            by_col,
            by_col,
            P(),
            by_col,
            by_head,
            P(),
            P(),
            by_head,
            by_head,
            by_head,
            by_head,
            by_row,
        ),
        check_vma=False,
    )
```

```python
import functools

import jax
import jax.numpy as jnp
from jax import lax
from jax.experimental import pallas as pl
from jax.experimental.pallas import tpu as pltpu
from jax.sharding import PartitionSpec as P

HEAD_DIM = 64
STATE = 128
CONV = 4
SPAN = 256
SEQ_LEN = 1024
DOCS = 4
CHUNKS = SEQ_LEN // SPAN
WIDE = 256
GROUP = WIDE // HEAD_DIM
STRIP = 128
BELOW = [(k * STRIP, -(-(k + 1) * STRIP // 128) * 128) for k in range(SPAN // STRIP)]
ABOVE = [(k * STRIP, k * STRIP // 128 * 128) for k in range(SPAN // STRIP)]
EPSILON = 1e-05
F32 = jnp.float32
BF16 = jnp.bfloat16
VMEM_LIMIT = 48 * 1024 * 1024


PACE = 0.01e9


def lasting(us):
    return pl.CostEstimate(flops=int(us * PACE), bytes_accessed=1000, transcendentals=0)


def dot_nn(a, b):
    return lax.dot_general(a, b, (((1,), (0,)), ((), ())), preferred_element_type=F32)


def dot_nt(a, b):
    return lax.dot_general(a, b, (((1,), (1,)), ((), ())), preferred_element_type=F32)


def dot_tn(a, b):
    return lax.dot_general(a, b, (((0,), (0,)), ((), ())), preferred_element_type=F32)


def sigmoid(v):
    return 0.5 * (1.0 + jnp.tanh(0.5 * v))


def chunk_start(info, c, per_block):
    block = (c // per_block) ^ info[DOCS]
    return pl.multiple_of((block * per_block + c % per_block) * SPAN, SPAN)


def doc_place(info, pos):
    first = jnp.zeros_like(pos)
    last = jnp.full_like(pos, SEQ_LEN)
    for k in range(DOCS):
        first = jnp.where(pos >= info[k], info[k], first)
    for k in reversed(range(DOCS)):
        last = jnp.where(pos < info[k], info[k], last)
    return pos - first, last - 1 - pos


def chunk_masks(info, c):
    local = lax.broadcasted_iota(jnp.int32, (SPAN, 128), 0)
    since, until = doc_place(info, local + c * SPAN)
    return local, since, until


def wide2(v):
    return jnp.concatenate([v, v], axis=1)


def expand(cols):
    rows = cols.shape[0]
    low = lax.broadcasted_iota(jnp.int32, (rows, 128), 1) < HEAD_DIM
    tiles = [
        jnp.where(low, cols[:, 2 * p : 2 * p + 1], cols[:, 2 * p + 1 : 2 * p + 2]) for p in range(WIDE // 128)
    ]
    return jnp.concatenate(tiles, axis=1)


def conv_inputs(src, info, c, per_block, r0):
    now = src[pl.ds(r0, SPAN), :].astype(F32)
    if c == 0:
        before = jnp.zeros((8, now.shape[1]), F32)
    else:
        p0 = chunk_start(info, c - 1, per_block)
        before = src[pl.ds(pl.multiple_of(p0 + SPAN - 16, 16), 16), :].astype(F32)[8:]
    ext = jnp.concatenate([before, now], axis=0)
    return now, [now] + [pltpu.roll(ext, k, 0)[8:] for k in range(1, CONV)]


def conv_apply(lags, taps, bias, masks):
    u = bias + taps[0] * lags[0]
    for k in range(1, CONV):
        u = u + taps[k] * (lags[k] * masks[k])
    return u


def conv_back(du, after, taps, masks_after):
    ext = jnp.concatenate([du, after], axis=0)
    total = taps[0] * du
    for k in range(1, CONV):
        total = total + taps[k] * (pltpu.roll(ext, SPAN + 8 - k, 0)[:SPAN] * masks_after[k])
    return total


def prep_kernel(per_block, info, pairs, par, bc_out, bct_out):
    taps = [par[k : k + 1, :] for k in range(CONV)]
    for c in range(CHUNKS):
        r0 = chunk_start(info, c, per_block)
        _, since, _ = chunk_masks(info, c)
        masks = [wide2((since >= k).astype(F32)) for k in range(CONV)]
        _, lags = conv_inputs(pairs, info, c, per_block, r0)
        u = conv_apply(lags, taps, par[4:5, :], masks)
        low = (u * sigmoid(u)).astype(BF16)
        bc_out[pl.ds(r0, SPAN), :] = low
        bct_out[:, pl.ds(r0, SPAN)] = low.T


def fwd_kernel(
    per_block, info, inner, gate, bc, bct, hs, par, y_out, mk_out, yg_out, st_out, ss_out, score_scr, state_scr
):
    taps = [par[k : k + 1, :] for k in range(CONV)]
    bias, skip, gain, act = par[4:5, :], par[5:6, :], par[6:7, :], par[7:8, :]
    lane = lax.broadcasted_iota(jnp.int32, (1, 128), 1)
    sides = [(lane < HEAD_DIM).astype(BF16), (lane >= HEAD_DIM).astype(BF16)]

    @pl.when(pl.program_id(0) == 0)
    def _():
        ss_out[...] = jnp.zeros_like(ss_out)
        for c in range(CHUNKS):
            r0 = chunk_start(info, c, per_block)
            _, since, _ = chunk_masks(info, c)
            bcv = bc[pl.ds(r0, SPAN), :]
            score = dot_nt(bcv[:, STATE:], bcv[:, :STATE])
            gap = lax.broadcasted_iota(jnp.int32, (SPAN, SPAN), 0) - lax.broadcasted_iota(
                jnp.int32, (SPAN, SPAN), 1
            )
            score_scr[c] = jnp.where((gap >= 0) & (gap <= wide2(since)), score, 0.0)

    state_scr[...] = jnp.zeros_like(state_scr)
    for c in range(CHUNKS):
        r0 = chunk_start(info, c, per_block)
        local, since, until = chunk_masks(info, c)
        masks = [wide2((since >= k).astype(F32)) for k in range(CONV)]
        _, lags = conv_inputs(inner, info, c, per_block, r0)
        u = conv_apply(lags, taps, bias, masks)
        xf = (u * sigmoid(u)).astype(BF16).astype(F32)
        head_rows = hs[:, pl.ds(r0, SPAN)]
        cum_rows = head_rows[:8]
        cum = cum_rows.T
        step = head_rows[8:].T
        local8, since8, until8 = local[:, :8], since[:, :8], until[:, :8]
        cum_end = cum[SPAN - 1 : SPAN, :]
        entry = jnp.where(since8 > local8, jnp.exp(cum), 0.0)
        tail = jnp.where(until8 >= SPAN - 1 - local8, jnp.exp(cum_end - cum), 0.0)
        keep = entry[SPAN - 1 : SPAN, :]
        xs = (xf * expand(step)).astype(BF16)
        xw = (xf * expand(tail * step)).astype(BF16)
        state = state_scr[...]
        state_low = state.astype(BF16)
        st_out[pl.ds(c * STATE, STATE), :] = state_low
        carried = dot_nn(bc[pl.ds(r0, SPAN), STATE:], state_low) * expand(entry)
        state_scr[...] = state * expand(keep) + dot_nn(bct[:STATE, pl.ds(r0, SPAN)], xw)
        tiles = []
        for p in range(WIDE // 128):
            tile = carried[:, p * 128 : (p + 1) * 128]
            for s in range(2):
                h = 2 * p + s
                values = xs[:, p * 128 : (p + 1) * 128] * sides[s]
                strips = []
                for at, end in BELOW:
                    gap = cum[at : at + STRIP, h : h + 1] - cum_rows[h : h + 1, :end]
                    decays = jnp.exp(jnp.minimum(gap, 0.0))
                    mixing = (decays * score_scr[c, at : at + STRIP, :end]).astype(BF16)
                    strips.append(dot_nn(mixing, values[:end]))
                tile = tile + jnp.concatenate(strips, axis=0)
            tiles.append(tile)
        y = jnp.concatenate(tiles, axis=1)
        y_out[pl.ds(r0, SPAN), :] = y.astype(BF16)
        g = gate[pl.ds(r0, SPAN), :].astype(F32)
        masked = (y + skip * xf) * act
        mk_out[pl.ds(r0, SPAN), :] = masked.astype(BF16)
        gated = masked * (g * sigmoid(g))
        yg_out[pl.ds(r0, SPAN), :] = (gated * gain).astype(BF16)
        square = gated * gated
        ss_out[pl.ds(r0, SPAN), :] += square[:, :128] + square[:, 128:]


def split_low(v):
    high = v.astype(BF16)
    return high, (v - high.astype(F32)).astype(BF16)


def gate_kernel(mk, gate, dn_in, sk, par, dgate_out, dy_out, gg_out):
    gain, act = par[6:7, :], par[7:8, :]
    total = jnp.zeros((1, WIDE), F32)
    for c in range(CHUNKS):
        rows = pl.ds(c * SPAN, SPAN)
        row_cols = sk[:, c * SPAN : (c + 1) * SPAN].T
        scale, fix = row_cols[:, 0:1], row_cols[:, 1:2]
        g = gate[rows, :].astype(F32)
        sg = sigmoid(g)
        sw = g * sg
        masked = mk[rows, :].astype(F32)
        gated = masked * sw
        d_scale = dn_in[rows, :].astype(F32) * scale
        d_gated = d_scale * gain - gated * fix
        dgate_out[rows, :] = (d_gated * masked * sg * (1.0 + g * (1.0 - sg))).astype(BF16)
        dy_out[rows, :] = (d_gated * sw * act).astype(BF16)
        total = total + jnp.sum(d_scale * gated, axis=0, keepdims=True)
    gg_out[...] = total + jnp.zeros((8, WIDE), F32)


def bwd_kernel(
    per_block,
    blocks,
    info,
    inner,
    y_in,
    dy_in,
    bc,
    bct,
    hs,
    st,
    par,
    dinner_out,
    dbc_out,
    gp_out,
    hr_out,
    score_scr,
    pair_scr,
    mask_scr,
    adj_scr,
):
    taps = [par[k : k + 1, :] for k in range(CONV)]
    bias, skip = par[4:5, :], par[5:6, :]
    lane = lax.broadcasted_iota(jnp.int32, (1, 128), 1)
    sides = [(lane < HEAD_DIM).astype(BF16), (lane >= HEAD_DIM).astype(BF16)]
    head_of = lax.broadcasted_iota(jnp.int32, (8, WIDE), 1) // HEAD_DIM
    row8 = lax.broadcasted_iota(jnp.int32, (8, WIDE), 0)
    pick = (head_of == row8).astype(BF16)
    pick_up = (head_of + 4 == row8).astype(BF16)

    @pl.when(pl.program_id(0) == 0)
    def _():
        dbc_out[...] = jnp.zeros_like(dbc_out)
        pair_scr[...] = jnp.zeros_like(pair_scr)
        for c in range(CHUNKS):
            r0 = chunk_start(info, c, per_block)
            _, since, until = chunk_masks(info, c)
            bcv = bc[pl.ds(r0, SPAN), :]
            score = dot_nt(bcv[:, :STATE], bcv[:, STATE:])
            gap = lax.broadcasted_iota(jnp.int32, (SPAN, SPAN), 1) - lax.broadcasted_iota(
                jnp.int32, (SPAN, SPAN), 0
            )
            score_scr[c] = jnp.where((gap >= 0) & (gap <= wide2(until)), score, 0.0)
            mask_scr[c] = jnp.where((gap <= 0) & (-gap <= wide2(since)), 1.0, 0.0).astype(BF16)

    adj_scr[...] = jnp.zeros_like(adj_scr)
    after = jnp.zeros((8, WIDE), F32)
    gp = jnp.zeros((8, WIDE), F32)
    for c in reversed(range(CHUNKS)):
        r0 = chunk_start(info, c, per_block)
        local, since, until = chunk_masks(info, c)
        masks = [wide2((since >= k).astype(F32)) for k in range(CONV)]
        masks_after = [wide2((until >= k).astype(F32)) for k in range(CONV)]
        _, lags = conv_inputs(inner, info, c, per_block, r0)
        u = conv_apply(lags, taps, bias, masks)
        su = sigmoid(u)
        xf = (u * su).astype(BF16).astype(F32)
        head_rows = hs[:, pl.ds(r0, SPAN)]
        cum_rows, step_rows = head_rows[:8], head_rows[8:]
        cum = cum_rows.T
        step = step_rows.T
        local8, since8, until8 = local[:, :8], since[:, :8], until[:, :8]
        cum_end = cum[SPAN - 1 : SPAN, :]
        entry = jnp.where(since8 > local8, jnp.exp(cum), 0.0)
        tail = jnp.where(until8 >= SPAN - 1 - local8, jnp.exp(cum_end - cum), 0.0)
        keep = entry[SPAN - 1 : SPAN, :]
        step_wide = expand(step)
        xs = (xf * step_wide).astype(BF16)
        xw = (xf * expand(tail * step)).astype(BF16)
        y = y_in[pl.ds(r0, SPAN), :].astype(F32)
        dy_low = dy_in[pl.ds(r0, SPAN), :]
        dy = dy_low.astype(F32)
        dy_entry = (dy * expand(entry)).astype(BF16)

        adj = adj_scr[...]
        adj_low = adj.astype(BF16)
        bcv = bc[pl.ds(r0, SPAN), :]
        d_c = dot_nt(dy_entry, st[pl.ds(c * STATE, STATE), :])
        d_b = dot_nt(xw, adj_low)
        dbc_out[pl.ds(r0, SPAN), :] += jnp.concatenate([d_b, d_c], axis=1)
        carried = dot_nn(bcv[:, :STATE], adj_low) * expand(tail)
        adj_scr[...] = adj * expand(keep) + dot_nn(bct[STATE:, pl.ds(r0, SPAN)], dy_entry)

        tiles = []
        for p in range(WIDE // 128):
            tile = carried[:, p * 128 : (p + 1) * 128]
            dy_tile = dy_low[:, p * 128 : (p + 1) * 128]
            xs_tile = xs[:, p * 128 : (p + 1) * 128]
            for s in range(2):
                h = 2 * p + s
                dy_side = dy_tile * sides[s]
                xs_side = xs_tile * sides[s]
                strips = []
                for at, begin in ABOVE:
                    rows = slice(at, at + STRIP)
                    gap = cum_rows[h : h + 1, begin:] - cum[rows, h : h + 1]
                    decays = jnp.exp(jnp.minimum(gap, 0.0))
                    mixing = (decays * score_scr[c, rows, begin:]).astype(BF16)
                    strips.append(dot_nn(mixing, dy_side[begin:]))
                    pair_scr[c, rows, begin:] += decays * dot_nt(xs_side[rows], dy_tile[begin:])
                tile = tile + jnp.concatenate(strips, axis=0)
            tiles.append(tile)
        dxu = jnp.concatenate(tiles, axis=1)

        du = (step_wide * dxu + skip * dy) * (su * (1.0 + u * (1.0 - su)))
        dinner_out[pl.ds(r0, SPAN), :] = conv_back(du, after, taps, masks_after).astype(BF16)
        after = du[:8]
        sums = [jnp.sum(du * lags[k] * masks[k], axis=0, keepdims=True) for k in range(CONV)]
        sums += [jnp.sum(du, axis=0, keepdims=True), jnp.zeros((3, WIDE), F32)]
        gp = gp + jnp.concatenate(sums, axis=0)

        q1h, q1l = split_low(dy * y)
        q2h, q2l = split_low(xf * dxu)
        q3h, q3l = split_low(xf * dy)
        row_term = dot_nt(pick, q1h) + dot_nt(pick, q1l)
        steps = dot_nt(pick, q2h) + dot_nt(pick, q2l) + dot_nt(pick_up, q3h) + dot_nt(pick_up, q3l)
        vh, vl = split_low(row_term - step_rows * jnp.where(row8 < GROUP, steps, 0.0))
        d_decay = dot_nn(vh, mask_scr[c]) + dot_nn(vl, mask_scr[c])
        row_local = lax.broadcasted_iota(jnp.int32, (8, SPAN), 1)
        row_since, row_until = doc_place(info, row_local + c * SPAN)
        if c < CHUNKS - 1:
            ph, plow = split_low(st[pl.ds((c + 1) * STATE, STATE), :].astype(F32) * adj)
            cross = jnp.sum(dot_nt(pick, ph) + dot_nt(pick, plow), axis=1, keepdims=True)
            d_decay = d_decay + jnp.where(row_until >= SPAN - 1 - row_local, cross, 0.0)
        d_decay = jnp.where(row_since > 0, d_decay, 0.0)
        hr_out[:, pl.ds(r0, SPAN)] = jnp.concatenate([steps, d_decay], axis=0)
    gp_out[...] = gp

    @pl.when(pl.program_id(0) == blocks - 1)
    def _():
        for c in range(CHUNKS):
            r0 = chunk_start(info, c, per_block)
            _, _, until = chunk_masks(info, c)
            gap = lax.broadcasted_iota(jnp.int32, (SPAN, SPAN), 1) - lax.broadcasted_iota(
                jnp.int32, (SPAN, SPAN), 0
            )
            pair_low = jnp.where((gap >= 0) & (gap <= wide2(until)), pair_scr[c], 0.0).astype(BF16)
            bcv = bc[pl.ds(r0, SPAN), :]
            dbc_out[pl.ds(r0, SPAN), :] += jnp.concatenate(
                [dot_nn(pair_low, bcv[:, STATE:]), dot_tn(pair_low, bcv[:, :STATE])], axis=1
            )


def pair_kernel(per_block, info, pairs, dbc_a, dbc_b, par, dp_out, gp_out):
    taps = [par[k : k + 1, :] for k in range(CONV)]
    after = jnp.zeros((8, WIDE), F32)
    gp = jnp.zeros((8, WIDE), F32)
    for c in reversed(range(CHUNKS)):
        r0 = chunk_start(info, c, per_block)
        _, since, until = chunk_masks(info, c)
        masks = [wide2((since >= k).astype(F32)) for k in range(CONV)]
        masks_after = [wide2((until >= k).astype(F32)) for k in range(CONV)]
        _, lags = conv_inputs(pairs, info, c, per_block, r0)
        u = conv_apply(lags, taps, par[4:5, :], masks)
        su = sigmoid(u)
        rows = pl.ds(r0, SPAN)
        du = (dbc_a[rows, :] + dbc_b[rows, :]) * (su * (1.0 + u * (1.0 - su)))
        dp_out[rows, :] = conv_back(du, after, taps, masks_after).astype(BF16)
        after = du[:8]
        sums = [jnp.sum(du * lags[k] * masks[k], axis=0, keepdims=True) for k in range(CONV)]
        sums += [jnp.sum(du, axis=0, keepdims=True), jnp.zeros((3, WIDE), F32)]
        gp = gp + jnp.concatenate(sums, axis=0)
    gp_out[...] = gp


def whole(shape):
    return pl.BlockSpec(shape, lambda i, info: (0,) * len(shape))


def cols(rows):
    return pl.BlockSpec((rows, WIDE), lambda i, info: (0, i))


def ignore(kernel, at, count):
    if not count:
        return kernel
    return lambda *refs: kernel(*refs[:at], *refs[at + count :])


def unread(later):
    return [pl.BlockSpec(memory_space=pl.ANY) for _ in later]


def call(kernel, grid, in_specs, out_specs, out_shape, scratch, us, info, *operands, later=()):
    kernel = ignore(kernel, 1 + len(operands), len(later))
    in_specs = [*in_specs, *unread(later)]
    operands = [*operands, *later]
    return pl.pallas_call(
        kernel,
        grid_spec=pltpu.PrefetchScalarGridSpec(
            num_scalar_prefetch=1,
            grid=(grid,),
            in_specs=in_specs,
            out_specs=out_specs,
            scratch_shapes=scratch,
        ),
        out_shape=out_shape,
        compiler_params=pltpu.CompilerParams(vmem_limit_bytes=VMEM_LIMIT),
        cost_estimate=lasting(us),
    )(info, *operands)


def shape(dims, kind):
    return jax.ShapeDtypeStruct(dims, kind)


def project(a, b, kind, later):
    rows, depth = a.shape
    b, number = b if isinstance(b, tuple) else (b, 0)
    columns = b.shape[-1]
    wide = min(columns, 512)
    block = pl.BlockSpec((depth, wide), lambda j: (0, j))
    if b.ndim == 4:
        block = pl.BlockSpec((b.shape[0], 1, b.shape[2], wide), lambda j: (0, number, 0, j))

    def kernel(x, w, out):
        out[...] = dot_nn(x[...], w[...].reshape(depth, wide)).astype(kind)

    return pl.pallas_call(
        ignore(kernel, 2, len(later)),
        grid=(columns // wide,),
        in_specs=[
            pl.BlockSpec((rows, depth), lambda j: (0, 0)),
            block,
            *unread(later),
        ],
        out_specs=pl.BlockSpec((rows, wide), lambda j: (0, j)),
        out_shape=shape((rows, columns), kind),
        compiler_params=pltpu.CompilerParams(vmem_limit_bytes=VMEM_LIMIT),
        cost_estimate=lasting(6),
    )(a, b, *later)


def project_few(a, b, later):
    rows, depth = a.shape
    columns = b.shape[1]

    def kernel(x, w, out):
        out[...] = dot_nn(x[...], w[...])

    return pl.pallas_call(
        ignore(kernel, 2, len(later)),
        grid=(rows // 256,),
        in_specs=[
            pl.BlockSpec((256, depth), lambda i: (i, 0)),
            pl.BlockSpec((depth, columns), lambda i: (0, 0)),
            *unread(later),
        ],
        out_specs=pl.BlockSpec((256, columns), lambda i: (i, 0)),
        out_shape=shape((rows, columns), F32),
        compiler_params=pltpu.CompilerParams(vmem_limit_bytes=VMEM_LIMIT),
        cost_estimate=lasting(3),
    )(a, b, *later)


def project_back(up, w, yg, later):
    rows, depth = up.shape
    columns = w.shape[0]
    wide = min(columns, 512)

    def kernel(x, b, y, out, sums):
        value = dot_nt(x[...], b[...])
        out[...] = value.astype(BF16)
        value = value * y[...].astype(F32)
        total = value[:, :128]
        for k in range(1, wide // 128):
            total = total + value[:, k * 128 : (k + 1) * 128]

        @pl.when(pl.program_id(0) == 0)
        def _():
            sums[...] = total

        @pl.when(pl.program_id(0) > 0)
        def _():
            sums[...] += total

    return pl.pallas_call(
        ignore(kernel, 3, len(later)),
        grid=(columns // wide,),
        in_specs=[
            pl.BlockSpec((rows, depth), lambda j: (0, 0)),
            pl.BlockSpec((wide, depth), lambda j: (j, 0)),
            pl.BlockSpec((rows, wide), lambda j: (0, j)),
            *unread(later),
        ],
        out_specs=[pl.BlockSpec((rows, wide), lambda j: (0, j)), pl.BlockSpec((rows, 128), lambda j: (0, 0))],
        out_shape=[shape((rows, columns), BF16), shape((rows, 128), F32)],
        compiler_params=pltpu.CompilerParams(vmem_limit_bytes=VMEM_LIMIT),
        cost_estimate=lasting(8),
    )(up, w, yg, *later)


def rows_forward(lefts, rights, first, rows, later=()):
    columns = rights[0].shape[1]
    wide = 512
    count = len(lefts)
    start = first // rows

    def kernel(*refs):
        total = dot_nn(refs[0][...], refs[count][...])
        for n in range(1, count):
            total = total + dot_nn(refs[n][...], refs[count + n][...])
        refs[-1][...] = total.astype(BF16)

    return pl.pallas_call(
        ignore(kernel, 2 * count, len(later)),
        grid=(columns // wide,),
        in_specs=[pl.BlockSpec((rows, v.shape[1]), lambda j: (start, 0)) for v in lefts]
        + [pl.BlockSpec((v.shape[0], wide), lambda j: (0, j)) for v in rights]
        + unread(later),
        out_specs=pl.BlockSpec((rows, wide), lambda j: (0, j)),
        out_shape=shape((rows, columns), BF16),
        compiler_params=pltpu.CompilerParams(vmem_limit_bytes=VMEM_LIMIT),
        cost_estimate=lasting(5),
    )(*lefts, *rights, *later)


def delayed(v, later):
    flat = v.reshape(-1, v.shape[-1])
    rows, width = flat.shape
    block = rows // 2 if rows % 32 == 0 else rows

    def kernel(a, out):
        out[...] = a[...]

    return pl.pallas_call(
        ignore(kernel, 1, len(later)),
        grid=(rows // block,),
        in_specs=[pl.BlockSpec((block, width), lambda i: (i, 0)), *unread(later)],
        out_specs=pl.BlockSpec((block, width), lambda i: (i, 0)),
        out_shape=shape((rows, width), v.dtype),
        compiler_params=pltpu.CompilerParams(vmem_limit_bytes=VMEM_LIMIT),
        cost_estimate=lasting(2),
    )(flat, *later).reshape(v.shape)


def added(a, b, later):
    def kernel(x, y, out):
        out[...] = (x[...].astype(F32) + y[...].astype(F32)).astype(BF16)

    return pl.pallas_call(
        ignore(kernel, 2, len(later)),
        in_specs=[pl.BlockSpec(memory_space=pltpu.VMEM)] * 2 + unread(later),
        out_specs=pl.BlockSpec(memory_space=pltpu.VMEM),
        out_shape=shape(a.shape, BF16),
        compiler_params=pltpu.CompilerParams(vmem_limit_bytes=VMEM_LIMIT),
        cost_estimate=lasting(1),
    )(a, b, *later)


def norm_rows(own, got, gain, later):
    rows, width = own.shape
    block = min(rows, 256)
    here = rows // block

    def kernel(a, b, gain_row, out):
        def write(v):
            v = v.astype(F32)
            inverse = lax.rsqrt(jnp.mean(v * v, axis=1, keepdims=True) + EPSILON)
            out[...] = (v * inverse * gain_row[...]).astype(BF16)

        @pl.when(pl.program_id(0) < here)
        def _():
            write(a[...])

        @pl.when(pl.program_id(0) >= here)
        def _():
            write(b[...])

    return pl.pallas_call(
        ignore(kernel, 3, len(later)),
        grid=(SEQ_LEN // block,),
        in_specs=[
            pl.BlockSpec((block, width), lambda i: (jnp.minimum(i, here - 1), 0)),
            pl.BlockSpec((block, width), lambda i: (jnp.maximum(i - here, 0), 0)),
            pl.BlockSpec((1, width), lambda i: (0, 0)),
            *unread(later),
        ],
        out_specs=pl.BlockSpec((block, width), lambda i: (i, 0)),
        out_shape=shape((SEQ_LEN, width), BF16),
        compiler_params=pltpu.CompilerParams(vmem_limit_bytes=VMEM_LIMIT),
        cost_estimate=lasting(4),
    )(own, got, gain[None], *later)


def prep(per_block, info, pairs, par):
    t = SEQ_LEN
    return call(
        functools.partial(prep_kernel, per_block),
        1,
        [whole((t, WIDE)), whole((8, WIDE))],
        [whole((t, WIDE)), whole((WIDE, t))],
        [shape((t, WIDE), BF16), shape((WIDE, t), BF16)],
        [],
        2,
        info,
        pairs,
        par,
    )


def scan_forward(per_block, info, inner, gate, bc, bct, hs, par, later):
    t, channels = inner.shape
    blocks = channels // WIDE
    return call(
        functools.partial(fwd_kernel, per_block),
        blocks,
        [
            cols(t),
            cols(t),
            whole((t, WIDE)),
            whole((WIDE, t)),
            pl.BlockSpec((16, t), lambda i, info: (i, 0)),
            cols(8),
        ],
        [cols(t), cols(t), cols(t), cols(CHUNKS * STATE), whole((t, 128))],
        [
            shape((t, channels), BF16),
            shape((t, channels), BF16),
            shape((t, channels), BF16),
            shape((CHUNKS * STATE, channels), BF16),
            shape((t, 128), F32),
        ],
        [pltpu.VMEM((CHUNKS, SPAN, SPAN), F32), pltpu.VMEM((STATE, WIDE), F32)],
        20,
        info,
        inner,
        gate,
        bc,
        bct,
        hs,
        par,
        later=later,
    )


def scan_backward(per_block, info, inner, y, dy, bc, bct, hs, st, par, later):
    t, channels = inner.shape
    blocks = channels // WIDE
    return call(
        functools.partial(bwd_kernel, per_block, blocks),
        blocks,
        [
            cols(t),
            cols(t),
            cols(t),
            whole((t, WIDE)),
            whole((WIDE, t)),
            pl.BlockSpec((16, t), lambda i, info: (i, 0)),
            cols(CHUNKS * STATE),
            cols(8),
        ],
        [
            cols(t),
            whole((t, WIDE)),
            cols(8),
            pl.BlockSpec((16, t), lambda i, info: (i, 0)),
        ],
        [
            shape((t, channels), BF16),
            shape((t, WIDE), F32),
            shape((8, channels), F32),
            shape((blocks * 16, t), F32),
        ],
        [
            pltpu.VMEM((CHUNKS, SPAN, SPAN), F32),
            pltpu.VMEM((CHUNKS, SPAN, SPAN), F32),
            pltpu.VMEM((CHUNKS, SPAN, SPAN), BF16),
            pltpu.VMEM((STATE, WIDE), F32),
        ],
        36,
        info,
        inner,
        y,
        dy,
        bc,
        bct,
        hs,
        st,
        par,
        later=later,
    )


def gate_backward(mk, gate, dn, sk, par, later):
    t, channels = gate.shape
    block = pl.BlockSpec((t, WIDE), lambda i: (0, i))
    small = pl.BlockSpec((8, WIDE), lambda i: (0, i))
    return pl.pallas_call(
        ignore(gate_kernel, 5, len(later)),
        grid=(channels // WIDE,),
        in_specs=[block, block, block, pl.BlockSpec((8, t), lambda i: (0, 0)), small, *unread(later)],
        out_specs=[block, block, small],
        out_shape=[shape((t, channels), BF16)] * 2 + [shape((8, channels), F32)],
        compiler_params=pltpu.CompilerParams(vmem_limit_bytes=VMEM_LIMIT),
        cost_estimate=lasting(8),
    )(mk, gate, dn, sk, par, *later)


def turned(number, bits):
    return sum(((number >> k) & 1) << (bits - 1 - k) for k in range(bits))


def grad_half(lefts, rights, half, more=None, scale=None, later=(), pieces=1, bits=0):
    t, width = lefts[0].shape
    columns = rights[0].shape[1]
    count = max(len(lefts), len(rights))
    tall = width // 2 // pieces
    high, wide = min(width // 2, 256 if bits else 512), min(columns, 1024)
    down, along = width // 2 // high, columns // wide
    group = max(high // tall, 1)
    split = max(tall // high, 1)
    if bits and group > 1:
        high, group = tall, 1
        high = max(high, 128)
        group = high // tall
        down = width // 2 // high
    resident = bits > 0 and group > 1
    if resident:
        block = pl.BlockSpec((pieces, count, tall, wide), lambda j, i, info: (0, 0, 0, j))
    else:
        block = pl.BlockSpec(
            (group, count, tall // split, wide),
            lambda j, i, info: (turned(i // split, bits) if bits else i // split, 0, i % split, j),
        )
    operands = [*lefts, *rights] + ([] if more is None else [more]) + ([] if scale is None else [scale])

    def kernel(info, *refs):
        out = refs[-1]
        for n in range(count):
            left = refs[n % len(lefts)][...]
            if scale is not None:
                left = (left.astype(F32) * refs[-2][...].T[:, 0:1]).astype(BF16)
            total = dot_tn(left, refs[len(lefts) + n % len(rights)][...])
            for g in range(group):
                rows = total if group == 1 else total[g * tall : (g + 1) * tall]
                at = turned(pl.program_id(1) * group + g, bits) if resident else g
                if more is not None:
                    rows = rows + refs[len(lefts) + len(rights)][at, n].astype(F32)
                out[at, n] = rows.astype(BF16)

    return pl.pallas_call(
        ignore(kernel, 1 + len(operands), len(later)),
        grid_spec=pltpu.PrefetchScalarGridSpec(
            num_scalar_prefetch=1,
            grid=(along, down),
            in_specs=[pl.BlockSpec((t, high), lambda j, i, info: (0, info[0] * down + i)) for _ in lefts]
            + [pl.BlockSpec((t, wide), lambda j, i, info: (0, j)) for _ in rights]
            + ([] if more is None else [block])
            + ([] if scale is None else [pl.BlockSpec((8, t), lambda j, i, info: (0, 0))])
            + unread(later),
            out_specs=block,
        ),
        out_shape=shape((pieces, count, tall, columns), BF16),
        compiler_params=pltpu.CompilerParams(vmem_limit_bytes=VMEM_LIMIT),
        cost_estimate=lasting(7),
    )(half[None], *operands, *later)


def grad_pieces(left, right, shared, batches, bits, later=()):
    t, width = left.shape
    columns = right.shape[1]
    chips = batches // 2
    tall = width // batches // 2
    high = 256
    group = high // tall

    extra = 0 if shared is None else shared.shape[1]

    def kernel(a, b, *refs):
        out = refs[-1]
        total = dot_tn(a[...], b[...]).astype(BF16)
        for g in range(group):
            block = pl.program_id(0) * group + g
            core, quarter, number = block // (2 * chips), (block // chips) % 2, block % chips
            chip = jnp.where(quarter == 0, number, turned(number, bits))
            rows = pl.ds(pl.multiple_of(quarter * tall, tall), tall)
            out[chip * 2 + core, rows, :] = total[g * tall : (g + 1) * tall]

        if extra:

            @pl.when(pl.program_id(0) == width // high - 1)
            def _():
                out[:, 2 * tall :, :] = refs[0][...]

    return pl.pallas_call(
        ignore(kernel, 3 if extra else 2, len(later)),
        grid=(width // high,),
        in_specs=[
            pl.BlockSpec((t, high), lambda i: (0, i)),
            pl.BlockSpec((t, columns), lambda i: (0, 0)),
        ]
        + ([pl.BlockSpec(shared.shape, lambda i: (0, 0, 0))] if extra else [])
        + unread(later),
        out_specs=pl.BlockSpec((batches, 2 * tall + extra, columns), lambda i: (0, 0, 0)),
        out_shape=shape((batches, 2 * tall + extra, columns), BF16),
        compiler_params=pltpu.CompilerParams(vmem_limit_bytes=VMEM_LIMIT),
        cost_estimate=lasting(10),
    )(left, right, *([shared] if extra else []), *later)


def place_pieces(v, tall, bits, later):
    batches, _, columns = v.shape
    chips = batches // 2

    half = chips * tall
    wide = columns // 4

    def kernel(a, out):
        for core in range(2):
            for chip in range(chips):
                v = a[chip * 2 + core]
                for quarter, number in ((0, chip), (1, turned(chip, bits))):
                    at = (core * 2 + quarter) * half + number * tall
                    out[at : at + tall, :] = v[quarter * tall : (quarter + 1) * tall].astype(F32)

    return pl.pallas_call(
        ignore(kernel, 1, len(later)),
        grid=(4,),
        in_specs=[pl.BlockSpec((batches, 2 * tall, wide), lambda i: (0, 0, i)), *unread(later)],
        out_specs=pl.BlockSpec((4 * half, wide), lambda i: (0, i)),
        out_shape=shape((4 * half, columns), F32),
        compiler_params=pltpu.CompilerParams(vmem_limit_bytes=VMEM_LIMIT),
        cost_estimate=lasting(7),
    )(v, *later)


def place_halves(mine, other, core):
    rows, columns = mine.shape
    high = min(rows, 256)
    per = rows // high

    def kernel(info, a, b, out):
        here = pl.program_id(0) // per == info[0]

        @pl.when(here)
        def _():
            out[...] = a[...].astype(F32)

        @pl.when(jnp.logical_not(here))
        def _():
            out[...] = b[...].astype(F32)

    return pl.pallas_call(
        kernel,
        grid_spec=pltpu.PrefetchScalarGridSpec(
            num_scalar_prefetch=1,
            grid=(2 * per,),
            in_specs=[
                pl.BlockSpec((high, columns), lambda i, info: (jnp.clip(i - info[0] * per, 0, per - 1), 0)),
                pl.BlockSpec((high, columns), lambda i, info: (jnp.clip(i - (1 - info[0]) * per, 0, per - 1), 0)),
            ],
            out_specs=pl.BlockSpec((high, columns), lambda i, info: (i, 0)),
        ),
        out_shape=shape((2 * rows, columns), F32),
        compiler_params=pltpu.CompilerParams(vmem_limit_bytes=VMEM_LIMIT),
        cost_estimate=lasting(6),
    )(core[None], mine, other)


def small_grads(left, right, later):
    t, columns = right.shape
    wide = 512

    def kernel(a, b, out):
        out[...] = dot_tn(a[...], b[...])

    return pl.pallas_call(
        ignore(kernel, 2, len(later)),
        grid=(columns // wide,),
        in_specs=[
            pl.BlockSpec(left.shape, lambda j: (0, 0)),
            pl.BlockSpec((t, wide), lambda j: (0, j)),
            *unread(later),
        ],
        out_specs=pl.BlockSpec((left.shape[1], wide), lambda j: (0, j)),
        out_shape=shape((left.shape[1], columns), F32),
        compiler_params=pltpu.CompilerParams(vmem_limit_bytes=VMEM_LIMIT),
        cost_estimate=lasting(4),
    )(left, right, *later)


def rows_back(lefts, rights, first, rows, gain_rows, later=()):
    columns = rights[0].shape[0]
    wide = 512

    def right_block(v):
        if not isinstance(v, tuple):
            return pl.BlockSpec((wide, v.shape[1]), lambda j: (j, 0))
        v, number = v
        return pl.BlockSpec((wide // v.shape[2], 1, v.shape[2], v.shape[3]), lambda j: (j, number, 0, 0))

    count = len(lefts)
    start = first // rows

    def kernel(*refs):
        total = dot_nt(refs[0][...], refs[count][...].reshape(wide, -1))
        for n in range(1, count):
            total = total + dot_nt(refs[n][...], refs[count + n][...].reshape(wide, -1))
        unit, out, sums = refs[-3:]
        out[...] = total.astype(BF16)
        sums[...] = jnp.sum(total * unit[...].astype(F32), axis=0, keepdims=True) + jnp.zeros((8, wide), F32)

    return pl.pallas_call(
        ignore(kernel, 2 * count + 1, len(later)),
        grid=(columns // wide,),
        in_specs=[pl.BlockSpec((rows, v.shape[1]), lambda j: (start, 0)) for v in lefts]
        + [right_block(v) for v in rights]
        + [pl.BlockSpec((rows, wide), lambda j: (start, j))]
        + unread(later),
        out_specs=[pl.BlockSpec((rows, wide), lambda j: (0, j)), pl.BlockSpec((8, wide), lambda j: (0, j))],
        out_shape=[shape((rows, columns), BF16), shape((8, columns), F32)],
        compiler_params=pltpu.CompilerParams(vmem_limit_bytes=VMEM_LIMIT),
        cost_estimate=lasting(15),
    )(*lefts, *[v[0] if isinstance(v, tuple) else v for v in rights], gain_rows, *later)


def pair_backward(per_block, info, pairs, dbc_a, dbc_b, par):
    t = SEQ_LEN
    return call(
        functools.partial(pair_kernel, per_block),
        1,
        [whole((t, WIDE)), whole((t, WIDE)), whole((t, WIDE)), whole((8, WIDE))],
        [whole((t, WIDE)), whole((8, WIDE))],
        [shape((t, WIDE), BF16), shape((8, WIDE), F32)],
        [],
        4,
        info,
        pairs,
        dbc_a,
        dbc_b,
        par,
    )


def body(
    axis_sizes,
    hidden_in,
    out_grad,
    norm_gain,
    w_z,
    w_x,
    w_dt,
    w_bc,
    conv_x,
    conv_x_bias,
    conv_bc,
    conv_bc_bias,
    dt_bias,
    a_log,
    d_skip,
    gate_gain,
    w_out,
    doc_lengths,
    widths,
):
    batches, stacks = axis_sizes
    rows, width_in = hidden_in.shape
    heads_here = dt_bias.shape[0]
    channels = w_x.shape[1]
    members = stacks // widths.shape[0]
    far_bit = members
    per_block = rows // SPAN
    place = lax.axis_index("head")
    lot = lax.axis_index("batch")
    own_seq = place // members
    ends = jnp.cumsum(lax.dynamic_index_in_dim(doc_lengths, own_seq, 0, keepdims=False))
    width = lax.dynamic_index_in_dim(widths, own_seq, 0, keepdims=False)
    info = jnp.concatenate([ends.astype(jnp.int32), (place % members).astype(jnp.int32)[None]])

    def across(v, bit):
        return lax.ppermute(v, "head", [(i, i ^ bit) for i in range(stacks)])

    def sum_rows(v):
        bit = 1
        while bit < members:
            got = across(v, bit)
            flipped = got.reshape(v.shape[0], -1, 2, bit * rows)[:, :, ::-1, :].reshape(v.shape)
            v = v + flipped
            bit *= 2
        return v

    chip_bits = []
    bit = 2
    while bit < batches:
        chip_bits.append(bit)
        bit *= 2
    chips = batches // 2
    core = lot % 2
    chip_groups = [[2 * i + c for i in range(chips)] for c in range(2)]
    orders = (chip_bits, chip_bits[::-1])

    def planar(v, bit):
        return lax.ppermute(v, "batch", [(i, i ^ bit) for i in range(batches)])

    def side(bit):
        return (lot // bit) % 2

    def join(v, got, bit, axis=0):
        low, high = jnp.concatenate([v, got], axis=axis), jnp.concatenate([got, v], axis=axis)
        return jnp.where(side(bit) == 0, low, high)

    def add(a, b):
        return (a.astype(F32) + b.astype(F32)).astype(BF16)

    def nothing(v):
        return (v[(0,) * v.ndim].astype(F32) * 0.0).astype(jnp.int32)

    def others(v):
        got, bit = across(v, 1), 2
        while bit < members:
            got = jnp.concatenate([got, across(jnp.concatenate([v, got], axis=0), bit)], axis=0)
            bit *= 2
        return got

    hidden_got = others(hidden_in)
    piece = width_in // batches
    far_parts = across(
        jnp.concatenate([lax.dynamic_slice_in_dim(w, lot * piece, piece, 0) for w in (w_x, w_z)], axis=0), far_bit
    )
    w_dt_own = w_dt.T
    w_dt_far = across(w_dt_own, far_bit)
    head_row = jnp.concatenate([dt_bias, a_log])
    par_own = jnp.concatenate(
        [
            conv_x,
            conv_x_bias[None],
            jnp.repeat(d_skip, HEAD_DIM)[None],
            gate_gain[None],
            jnp.pad(head_row, (0, channels - head_row.shape[0]))[None],
        ],
        axis=0,
    )
    par_far = across(par_own, far_bit)
    up_sent = delayed(out_grad, (hidden_got,))
    normed = norm_rows(hidden_in, hidden_got, norm_gain, (far_parts, w_dt_far, par_far, up_sent))
    far_parts = delayed(far_parts, (hidden_got, w_dt_far, par_far))
    far_parts = delayed(far_parts, (hidden_got, w_dt_far, par_far))
    far_both = lax.all_gather(far_parts, "batch", axis=0, tiled=True).reshape(batches, 2, piece, channels)
    up_got = others(up_sent)
    upstream = jnp.concatenate([out_grad, up_got], axis=0)
    active = (jnp.arange(channels) // HEAD_DIM < width * heads_here // (heads_here * stacks)).astype(F32)
    rate_par = [(v[7, :heads_here], v[7, heads_here : 2 * heads_here]) for v in (par_own, par_far)]
    par2 = [jnp.concatenate([v[:7], active[None]], axis=0) for v in (par_own, par_far)]
    step_bias = jnp.concatenate([rate_par[0][0], rate_par[1][0]])[:, None]
    speed = jnp.exp(jnp.concatenate([rate_par[0][1], rate_par[1][1]]))[:, None]
    par_bc = jnp.concatenate([conv_bc, conv_bc_bias[None], jnp.zeros((3, 2 * STATE), F32)], axis=0)

    w_small = jnp.concatenate([w_bc, w_dt_own.T, w_dt_far.T], axis=1)
    small_cols = project_few(normed, w_small, ())
    pairs = small_cols[:, : 2 * STATE]
    rates = small_cols[:, 2 * STATE :].T
    step = jax.nn.softplus(rates + step_bias)
    decay = -step * speed
    upper = (jnp.arange(SPAN)[:, None] <= jnp.arange(SPAN)[None, :]).astype(F32)
    cum = lax.dot_general(
        decay.reshape(-1, SPAN), upper, (((1,), (0,)), ((), ())), precision=lax.Precision.HIGHEST
    ).reshape(decay.shape)

    def grouped(v):
        v = v.reshape(-1, GROUP, SEQ_LEN)
        return jnp.pad(v, ((0, 0), (0, 8 - GROUP), (0, 0)))

    hs = jnp.concatenate([grouped(cum), grouped(step)], axis=1).reshape(-1, SEQ_LEN)
    half = hs.shape[0] // 2
    hs2 = (hs[:half], hs[half:])
    bc, bct = prep(per_block, info, pairs, par_bc)

    inner_own = project(normed, w_x, BF16, (bc,))
    gate_own = project(normed, w_z, BF16, (inner_own,))
    out_piece = channels // batches
    w_out_part = across(
        lax.dynamic_slice_in_dim(w_out, lot * out_piece + nothing(gate_own), out_piece, 0), far_bit
    )
    forward_own = scan_forward(per_block, info, inner_own, gate_own, bc, bct, hs2[0], par2[0], (up_got,))
    dn_own = project_back(upstream, w_out, forward_own[2], ())
    w_x_far, w_z_far = (far_both, 0), (far_both, 1)
    w_out_far = lax.all_gather(delayed(w_out_part, (forward_own[0],)), "batch", axis=0, tiled=True)
    w_x2 = (w_x, w_x_far)
    w_z2 = (w_z, w_z_far)
    w_out2 = (w_out, w_out_far)
    inner2 = (inner_own, project(normed, w_x_far, BF16, (dn_own[0],)))
    gate2 = (gate_own, project(normed, w_z_far, BF16, (inner2[1],)))
    forward = (forward_own, scan_forward(per_block, info, inner2[1], gate2[1], bc, bct, hs2[1], par2[1], ()))
    y2, mk2, yg2, st2 = [[f[k] for f in forward] for k in range(4)]
    dn_far = project_back(upstream, w_out_far, yg2[1], ())
    dn2 = (dn_own[0], dn_far[0])

    def branch_rows(first, count):
        return rows_forward(yg2, w_out2, first, count, (dn_far[0],) if first else (give_out,))

    def scatter_rows(make):
        if members == 2:
            give = make(rows, rows)
            got = across(give, 1)
            return give, got, lambda: make(0, rows).astype(F32) + got.astype(F32)
        v = make(0, SEQ_LEN)
        bit = members // 2
        while bit >= 1:
            half = v.shape[0] // 2
            v = add(v[:half], across(v[half:], bit))
            bit //= 2
        return v, v, lambda: v.astype(F32)

    give_out = dn_far[0]
    branch_given, branch_got, branch = scatter_rows(branch_rows)
    square = jnp.sum(forward[0][4] + forward[1][4], axis=1)
    sums = sum_rows(jnp.stack([square, jnp.sum(dn_own[1] + dn_far[1], axis=1)]))
    count = (width * HEAD_DIM).astype(F32)
    scale = lax.rsqrt(sums[0] / count + EPSILON)
    fix = scale * scale * scale * sums[1] / count
    sk = jnp.concatenate([scale[None], fix[None], jnp.zeros((6, SEQ_LEN), F32)], axis=0)

    bits = len(chip_bits)

    def swap_halves(lefts, rights, scale=None, later=(), pieces=1, bits=0):
        give = grad_half(lefts, rights, 1 - core, None, scale, later, pieces, bits)
        got = planar(give, 1)
        return give, lambda later=(): grad_half(lefts, rights, core, got, scale, later, pieces, bits)

    def scatter_offloaded(mine):
        flat = mine.reshape(-1, mine.shape[-1])
        part = lax.psum_scatter(flat, "batch", scatter_dimension=0, tiled=True, axis_index_groups=chip_groups)
        return part.reshape(mine.shape[1:])

    def send_far(part, earlier):
        far = lax.dynamic_slice_in_dim(part, 1 + jnp.minimum(nothing(earlier), 0), 1, 0)[0]
        return across(far, far_bit)

    def gather_both(parts, seen):
        for step in range(bits):
            got = [planar(v, order[step]) for v, order in zip(parts, orders)]
            parts = [join(v, g, order[step]) for v, g, order in zip(parts, got, orders)]
            seen.append(parts)
        return parts, [planar(v, 1) for v in parts]

    give_out, keep_out = swap_halves(yg2, [upstream], sk, (branch_given,), pieces=chips)
    gates = [gate_backward(mk2[i], gate2[i], dn2[i], sk, par2[i], (give_out,)) for i in range(2)]
    d_gate2 = [v[0] for v in gates]
    mine_out = keep_out(later=(d_gate2[0],))
    part_out = scatter_offloaded(mine_out)
    give_z, keep_z = swap_halves([normed], d_gate2, later=(mine_out,), pieces=chips, bits=bits)
    give_out = give_z
    branch_sum = branch()
    mixed = (hidden_in.astype(F32) + branch_sum * scale[:rows, None]).astype(BF16)
    mine_z = keep_z(later=(give_z,))
    part_z = scatter_offloaded(mine_z)

    def scan_back(i, later):
        return scan_backward(per_block, info, inner2[i], y2[i], gates[i][1], bc, bct, hs2[i], st2[i], par2[i], later)

    back = [None, None]
    back[1] = scan_back(1, (mine_z,))
    far_cut = grad_pieces(normed, back[1][0], None, batches, bits)
    far_piece = lax.psum_scatter(far_cut.reshape(-1, channels), "batch", scatter_dimension=0, tiled=True)
    far_out = send_far(part_out, back[1][0])
    back[0] = scan_back(0, (far_cut,))
    d_pairs, g_bc = pair_backward(per_block, info, pairs, back[0][1], back[1][1], par_bc)
    heads_out = [b[3].reshape(-1, 16, SEQ_LEN) for b in back]
    d_step = jnp.concatenate([h[:, :GROUP].reshape(-1, SEQ_LEN) for h in heads_out], axis=0)
    skip_rows = jnp.concatenate([h[:, GROUP : 2 * GROUP].reshape(-1, SEQ_LEN) for h in heads_out], axis=0)
    d_decay = jnp.concatenate([h[:, 8 : 8 + GROUP].reshape(-1, SEQ_LEN) for h in heads_out], axis=0)
    d_rates_pre = (d_step - d_decay * speed) * jax.nn.sigmoid(rates + step_bias)
    head_grads = jnp.stack(
        [jnp.sum(d_rates_pre, axis=1), jnp.sum(d_decay * decay, axis=1), jnp.sum(skip_rows, axis=1)]
    )
    d_rates = d_rates_pre.astype(BF16)
    d_small = jnp.concatenate([d_pairs, d_rates.T], axis=1)

    g_small = small_grads(d_small, normed, (part_z, branch_got))

    def pack(i):
        gp = back[i][2]
        heads = head_grads[:, i * heads_here : (i + 1) * heads_here].reshape(-1)
        heads = jnp.pad(heads, (0, channels - heads.shape[0]))[None]
        start = 2 * STATE + i * heads_here
        return jnp.concatenate(
            [gp[:5], heads, gates[i][2][:1], gp[7:], g_small[start : start + heads_here].reshape(-1, channels)], axis=0
        )

    def spread(v):
        v = jnp.pad(v.astype(BF16), ((0, -v.shape[0] % (16 * batches)), (0, 0)))
        return v.reshape(batches, -1, channels)

    far_z = send_far(part_z, g_small)
    norm_sums = []

    def normed_rows(first, count):
        part, total = rows_back(
            [*d_gate2, back[0][0], back[1][0], d_small],
            [*w_z2, *w_x2, w_small],
            first,
            count,
            normed,
            (norm_sums[0],) if norm_sums else (g_small,),
        )
        norm_sums.append(total)
        return part

    _, d_normed_got, d_normed_in = scatter_rows(normed_rows)
    d_normed_in = d_normed_in()
    bc_rows, few_rows = 2 * STATE * width_in // channels, 8 * 2 * STATE // channels
    shared = spread(jnp.concatenate([g_small[: 2 * STATE].reshape(-1, channels), g_bc.reshape(-1, channels), sum(norm_sums)[:1].reshape(-1, channels)], axis=0))
    private = spread(pack(0) + delayed(across(pack(1), far_bit), (norm_sums[-1],)))
    own_cut = grad_pieces(normed, back[0][0], jnp.concatenate([shared, private], axis=1), batches, bits, (d_normed_got, far_z, far_out))
    own_part = lax.psum_scatter(own_cut.reshape(-1, channels), "batch", scatter_dimension=0, tiled=True)
    seen = []
    total_z = added(part_z[0], far_z, (norm_sums[-1],))
    total_out = added(part_out[0], far_out, (norm_sums[-1],))
    total_out = delayed(total_out, (total_z,))
    halves_here, halves_there = gather_both([total_out, total_z], seen)
    own_part = delayed(own_part, halves_here)

    cut = 2 * (width_in // batches // 2)
    far_sent = across(delayed(far_piece, seen[0]), far_bit)
    bc_piece = own_part[cut : cut + shared.shape[1]]
    bit = 1
    while bit < stacks:
        bc_piece = add(bc_piece, across(bc_piece, bit))
        bit *= 2
    own_total = jnp.concatenate(
        [add(own_part[:cut], far_sent), bc_piece, own_part[cut + shared.shape[1] :]], axis=0
    )
    everything = lax.all_gather(own_total, "batch", axis=0, tiled=True).reshape(batches, -1, channels)
    g_w_out, g_w_z = [place_halves(v, got, core) for v, got in zip(halves_here, halves_there)]
    common = everything[:, cut : cut + shared.shape[1]].reshape(-1, channels).astype(F32)
    packed = everything[:, cut + shared.shape[1] :].reshape(-1, channels).astype(F32)
    g_w_bc = common[:bc_rows].reshape(2 * STATE, width_in).T
    g_bc_total = common[bc_rows : bc_rows + few_rows].reshape(8, -1)
    heads_total = packed[5]
    g_w_dt = packed[8 : 8 + heads_here * width_in // channels].reshape(heads_here, width_in).T
    g_norm = common[bc_rows + few_rows : bc_rows + few_rows + width_in // channels].reshape(-1) / norm_gain

    residual = hidden_in.astype(F32)
    inverse = lax.rsqrt(jnp.mean(residual * residual, axis=-1, keepdims=True) + EPSILON)
    unit_rows = residual * inverse
    d_unit = d_normed_in * norm_gain
    d_residual = inverse * (d_unit - unit_rows * jnp.mean(d_unit * unit_rows, axis=-1, keepdims=True))
    in_grad = (out_grad.astype(F32) + d_residual).astype(BF16)
    g_w_x = place_pieces(everything, cut // 2, bits, (g_w_out, g_w_z, in_grad))
    return (
        mixed,
        in_grad,
        g_norm,
        g_w_z,
        g_w_x,
        g_w_dt,
        g_w_bc,
        packed[:4],
        packed[4],
        g_bc_total[:4],
        g_bc_total[4],
        heads_total[:heads_here],
        heads_total[heads_here : 2 * heads_here],
        heads_total[2 * heads_here : 3 * heads_here],
        packed[6],
        g_w_out,
    )


def solution(mesh):
    split = P(("batch", "head"), None)
    by_col, by_head, by_row = P(None, "head"), P("head"), P("head", None)
    return jax.shard_map(
        functools.partial(body, (mesh.shape["batch"], mesh.shape["head"])),
        mesh=mesh,
        in_specs=(
            split,
            split,
            P(),
            by_col,
            by_col,
            by_col,
            P(),
            by_col,
            by_head,
            P(),
            P(),
            by_head,
            by_head,
            by_head,
            by_head,
            by_row,
            P("batch", None),
            P("batch"),
        ),
        out_specs=(
            split,
            split,
            P(),
            by_col,
            by_col,
            by_col,
            P(),
            by_col,
            by_head,
            P(),
            P(),
            by_head,
            by_head,
            by_head,
            by_head,
            by_row,
        ),
        check_vma=False,
    )
```
